32 devices in a mesh: expert: 16 (over z, x, core), replica: 2 (over y).
Axes of the slice: x: 2, y: 2, z: 4, core: 2. Of those that a mesh axis runs over, the one named last changes fastest.
Arguments:
- tokens: bfloat16 [2048, 2048], P(('expert', 'replica')), may hold values from -6 to 6
- route_ids: int32 [2048, 6], P(('expert', 'replica')), may hold values from 0 to 15, all different within a row; in each aligned block of 64 rows (0 to 63, 64 to 127, ...) at most 32 rows name the same one
- gate_probs: float32 [2048, 6], P(('expert', 'replica')), may hold values from 0.05 to 0.35
- out_cot: bfloat16 [2048, 2048], P(('expert', 'replica')), may hold values from -6 to 6
- w_gate: bfloat16 [16, 2048, 768], P('expert'), may hold values from -0.125 to 0.125
- w_up: bfloat16 [16, 2048, 768], P('expert'), may hold values from -0.125 to 0.125
- w_down: bfloat16 [16, 768, 2048], P('expert'), may hold values from -0.21875 to 0.21875
Outputs:
- combined: bfloat16 [2048, 2048], P(('expert', 'replica'))
- grad_tokens: bfloat16 [2048, 2048], P(('expert', 'replica'))
- grad_gate: bfloat16 [16, 2048, 768], P('expert', 'replica')
- grad_up: bfloat16 [16, 2048, 768], P('expert', 'replica')
- grad_down: bfloat16 [16, 768, 2048], P('expert', 'replica')
The draws below stay inside these ranges and needn't reach their ends.
Inputs may be any that keep to these rules, and one draw needn't show every extreme that they name: `route_ids`: A token's 6 experts differ. Among the 64 tokens of one device, at most 32 choose any one expert, and in every draw some device's tokens choose some expert exactly 32 times.
All inputs are finite; a program needn't handle non-finite values.
Results may differ from the reference program's by a relative error of at most 0.0095.
Values may be sent and summed in bfloat16 or wider, within the bound.
No kernel may reach another device: no remote copies, remote signals or barrier semaphores. Data moves between devices by JAX's collectives and lax.ppermute only.
A program may use at most 128 MiB of HBM per device.

```python
import math
import jax
import jax.numpy as jnp
import numpy as np
from jax import lax

D = 2048
H = 768
TOPK = 6
TOK_DEV = 64
EXPERTS = 16
CAP = 32
TOKENS = 2048
N_EXPERT = 16
N_REPLICA = 2


def block_levels(rng, dims, shards, low, largest):
    gain, own = 1.0, jax.random.fold_in(rng, 6)
    for position, shards_of in shards:
        draws = jnp.exp(jax.random.uniform(jax.random.fold_in(own, position), (shards_of,), jnp.float32, low / len(shards), largest / len(shards)))
        gain = gain * jnp.repeat(draws, dims[position] // shards_of).reshape([-1 if axis == position else 1 for axis in range(len(dims))])
    return gain


def routed_block(rng, own, number, rows, number_of, top, most, slope):
    ranking = jax.random.permutation(rng, number_of)
    heavy_load, usual = load_shares(number_of, rows * top, most, slope, True), load_shares(number_of, rows * top, most, slope, False)
    places = jnp.arange(number_of)

    def named(sizes, rotation):
        used = int((sizes > 0).sum())
        fixed = max(1, used // 4)
        shifted = fixed + (places - fixed + rotation * (used - fixed)) % max(1, number_of - fixed)
        return jnp.zeros((number_of,), jnp.int32).at[ranking[jnp.where(places < fixed, places, shifted)]].set(jnp.asarray(sizes, jnp.int32))

    sizes = jnp.where(number % 4 == 0, named(heavy_load, number // 4), named(usual, number - number // 4 - 1))
    mixed = jax.random.permutation(jax.random.fold_in(own, 3), number_of)
    giver, receiver = mixed[0:number_of // 2 * 2:2], mixed[1:number_of // 2 * 2:2]
    room = jnp.minimum(sizes[giver] - 1, most - sizes[receiver]) // 2
    room = jnp.where((giver == ranking[0]) | (receiver == ranking[0]) | (sizes[receiver] == 0), 0, jnp.maximum(room, 0))
    shifted = jax.random.randint(jax.random.fold_in(own, 4), (number_of // 2,), 0, 1 << 20) % (room + 1)
    sizes = sizes.at[giver].add(-shifted).at[receiver].add(shifted)
    members = jnp.searchsorted(jnp.cumsum(sizes), jnp.arange(rows * top), side="right").astype(jnp.int32)
    listing = members.reshape(top, rows).T
    listing = listing[jax.random.permutation(jax.random.fold_in(own, 1), rows)]
    rotation = jax.random.randint(jax.random.fold_in(own, 2), (rows, 1), 0, top)
    return jnp.take_along_axis(listing, (jnp.arange(top)[None, :] + rotation) % top, axis=1)


def load_shares(amount, total, most, skew, full):
    portions = [(1 << 20) // math.isqrt(rank ** skew) + 1 for rank in range(1, amount + 1)]
    largest = most if full else min(most, max(-(-total // amount), total * portions[0] // sum(portions)))
    least = 1 if total - largest >= amount - 1 else 0
    holding, spare = [largest] + [least] * (amount - 1), total - largest - least * (amount - 1)
    while spare > 0:
        free = [i for i in range(1, amount) if holding[i] < largest] or [i for i in range(1, amount) if holding[i] < most]
        mass, left = sum([portions[i] for i in free]), spare
        for i in free:
            more = min(most - holding[i], max(1, left * portions[i] // mass), spare)
            holding[i] = holding[i] + more
            spare = spare - more
    return np.array(holding)


def bell_draw(key, shape, spread, reach, split=(), kind=jnp.bfloat16):
    values = jax.random.normal(key, shape, jnp.float32) * spread
    if len(split) > 0:
        values = block_levels(key, shape, split, -0.22, 0.18) * values
    return jnp.clip(values, min=-reach, max=reach).astype(kind)


def setup_inputs(seed: int = 0) -> dict:
    seeds = jax.random.split(jax.random.key(seed), 8)
    tokens = bell_draw(seeds[0], (TOKENS, D), 1.0, 6.0, ((0, 32),))
    route_ids_keys = jax.random.split(jax.random.fold_in(seeds[1], 1), TOKENS // TOK_DEV)
    route_ids_turns = jax.random.permutation(jax.random.fold_in(seeds[1], 3), TOKENS // TOK_DEV)
    route_ids = jax.vmap(lambda own, number: routed_block(jax.random.fold_in(seeds[1], 2), own, number, TOK_DEV, EXPERTS, TOPK, CAP, 2))(route_ids_keys, route_ids_turns).reshape((TOKENS, TOPK))
    gate_probs = jnp.clip(0.05 + 0.29999999 * jax.random.uniform(seeds[2], (TOKENS, TOPK), jnp.float32) ** block_levels(seeds[2], (TOKENS, TOPK), ((0, 32),), -0.2, 0.2), 0.05, 0.35)
    out_cot = bell_draw(seeds[3], (TOKENS, D), 1.0, 6.0, ((0, 32),))
    w_gate = bell_draw(seeds[4], (EXPERTS, D, H), D ** -0.5, 0.125, ((0, 16),))
    w_up = bell_draw(seeds[5], (EXPERTS, D, H), D ** -0.5, 0.125, ((0, 16),))
    w_down = bell_draw(seeds[6], (EXPERTS, H, D), H ** -0.5, 0.21875, ((0, 16),))
    return dict(tokens=tokens, route_ids=route_ids, gate_probs=gate_probs, out_cot=out_cot, w_gate=w_gate, w_up=w_up, w_down=w_down)


def slots(routes, experts, capacity):
    flat_ids = routes.reshape(-1).astype(jnp.int32)
    one_hot = (flat_ids[:, None] == jnp.arange(experts, dtype=jnp.int32)[None, :]).astype(jnp.int32)
    before = jnp.cumsum(one_hot, axis=0) - one_hot
    slot_rank = jnp.sum(before * one_hot, axis=1)
    return (flat_ids * capacity + slot_rank).astype(jnp.int32)


def place(token_rows, positions, total_rows):
    return jnp.zeros((total_rows, token_rows.shape[1]), token_rows.dtype).at[positions].set(token_rows)


def hidden_rows(token_rows, gate_weight, up_weight):
    pre_gate = jnp.dot(token_rows, gate_weight, preferred_element_type=jnp.float32)
    pre_up = jnp.dot(token_rows, up_weight, preferred_element_type=jnp.float32)
    activation = (jax.nn.silu(pre_gate) * pre_up).astype(jnp.bfloat16)
    return pre_gate, pre_up, activation


def backward_rows(grad_rows, pre_gate, pre_up, gate_weight, up_weight, down_weight):
    contract = (((1,), (1,)), ((), ()))
    d_hidden = lax.dot_general(grad_rows, down_weight, contract, preferred_element_type=jnp.float32)
    sigmoid_gate = jax.nn.sigmoid(pre_gate)
    d_gate = (d_hidden * pre_up * sigmoid_gate * (1.0 + pre_gate * (1.0 - sigmoid_gate))).astype(jnp.bfloat16)
    d_up = (d_hidden * pre_gate * sigmoid_gate).astype(jnp.bfloat16)
    back_rows = lax.dot_general(d_gate, gate_weight, contract, preferred_element_type=jnp.float32)
    back_rows = back_rows + lax.dot_general(d_up, up_weight, contract, preferred_element_type=jnp.float32)
    return back_rows.astype(jnp.bfloat16), d_gate, d_up


def outer_sum(left, right):
    return lax.dot_general(left, right, (((0,), (0,)), ((), ())), preferred_element_type=jnp.float32)


def reference(tokens, route_ids, gate_probs, out_cot, w_gate, w_up, w_down):
    owners = N_EXPERT
    groups = N_REPLICA
    total_rows = EXPERTS * CAP

    def slots_one(routes):
        return slots(routes, EXPERTS, CAP)

    def place_one(token_rows, positions):
        return place(token_rows, positions, total_rows)

    def pick_one(table, positions):
        return table[positions]

    positions = jax.vmap(jax.vmap(slots_one))(route_ids.reshape(owners, groups, TOK_DEV, TOPK))
    token_rows = jnp.repeat(tokens.reshape(owners, groups, TOK_DEV, D), TOPK, axis=2)
    shares = gate_probs.reshape(owners, groups, TOK_DEV, TOPK)
    cotangent = out_cot.reshape(owners, groups, TOK_DEV, D).astype(jnp.float32)
    scaled = (shares[..., None] * cotangent[:, :, :, None, :]).astype(jnp.bfloat16)
    scaled = scaled.reshape(owners, groups, TOK_DEV * TOPK, D)
    outgoing = jax.vmap(jax.vmap(place_one))(token_rows, positions).reshape(owners, groups, EXPERTS, CAP, D)
    grad_out = jax.vmap(jax.vmap(place_one))(scaled, positions).reshape(owners, groups, EXPERTS, CAP, D)
    received = jnp.transpose(outgoing, (2, 1, 0, 3, 4)).reshape(EXPERTS, groups, owners * CAP, D)
    grads_in = jnp.transpose(grad_out, (2, 1, 0, 3, 4)).reshape(EXPERTS, groups, owners * CAP, D)

    def one_expert(operands):
        rows_e, grads_e, gate_weight, up_weight, down_weight = operands

        def one_group(rows_g, grads_g):
            pre_gate, pre_up, activation = hidden_rows(rows_g, gate_weight, up_weight)
            result = jnp.dot(activation, down_weight, preferred_element_type=jnp.float32).astype(jnp.bfloat16)
            back_rows, d_gate, d_up = backward_rows(grads_g, pre_gate, pre_up, gate_weight, up_weight, down_weight)
            part_gate = outer_sum(rows_g, d_gate).astype(jnp.bfloat16)
            part_up = outer_sum(rows_g, d_up).astype(jnp.bfloat16)
            part_down = outer_sum(activation, grads_g).astype(jnp.bfloat16)
            return result, back_rows, part_gate, part_up, part_down

        result, back_rows, part_gate, part_up, part_down = jax.vmap(one_group)(rows_e, grads_e)
        part_gate, part_up, part_down = lax.optimization_barrier((part_gate, part_up, part_down))
        sum_gate = jnp.sum(part_gate.astype(jnp.float32), axis=0).astype(jnp.bfloat16)
        sum_up = jnp.sum(part_up.astype(jnp.float32), axis=0).astype(jnp.bfloat16)
        sum_down = jnp.sum(part_down.astype(jnp.float32), axis=0).astype(jnp.bfloat16)
        return result, back_rows, sum_gate, sum_up, sum_down

    results, backs, grad_gate, grad_up, grad_down = lax.map(one_expert, (received, grads_in, w_gate, w_up, w_down))
    results = jnp.transpose(results.reshape(EXPERTS, groups, owners, CAP, D), (2, 1, 0, 3, 4)).reshape(owners, groups, total_rows, D)
    backs = jnp.transpose(backs.reshape(EXPERTS, groups, owners, CAP, D), (2, 1, 0, 3, 4)).reshape(owners, groups, total_rows, D)
    picked = jax.vmap(jax.vmap(pick_one))(results, positions).reshape(owners, groups, TOK_DEV, TOPK, D)
    combined = jnp.sum(shares[..., None] * picked.astype(jnp.float32), axis=3).astype(jnp.bfloat16)
    picked_grad = jax.vmap(jax.vmap(pick_one))(backs, positions).reshape(owners, groups, TOK_DEV, TOPK, D)
    grad_tokens = jnp.sum(picked_grad.astype(jnp.float32), axis=3).astype(jnp.bfloat16)
    return (combined.reshape(TOKENS, D), grad_tokens.reshape(TOKENS, D), grad_gate, grad_up, grad_down)
```

```python
import jax
import jax.numpy as jnp
from jax import lax
from jax.sharding import PartitionSpec as P

BF = jnp.bfloat16
F32 = jnp.float32


def slots(routes, experts, capacity):
    flat_ids = routes.reshape(-1)
    one_hot = (flat_ids[:, None] == jnp.arange(experts, dtype=jnp.int32)[None, :]).astype(jnp.int32)
    before = jnp.cumsum(one_hot, axis=0) - one_hot
    slot_rank = jnp.sum(before * one_hot, axis=1)
    return flat_ids * capacity + slot_rank


def place(token_rows, positions, total_rows):
    return (
        jnp.zeros((total_rows, token_rows.shape[1]), token_rows.dtype).at[positions].set(token_rows)
    )


def hidden_rows(token_rows, gate_weight, up_weight):
    pre_gate = jnp.dot(token_rows, gate_weight, preferred_element_type=F32)
    pre_up = jnp.dot(token_rows, up_weight, preferred_element_type=F32)
    activation = (jax.nn.silu(pre_gate) * pre_up).astype(BF)
    return (pre_gate, pre_up, activation)


CONTRACT = (((1,), (1,)), ((), ()))


def hidden_grads(grad_rows, pre_gate, pre_up, down_weight):
    d_hidden = lax.dot_general(grad_rows, down_weight, CONTRACT, preferred_element_type=F32)
    sigmoid_gate = jax.nn.sigmoid(pre_gate)
    d_gate = (d_hidden * pre_up * sigmoid_gate * (1.0 + pre_gate * (1.0 - sigmoid_gate))).astype(BF)
    d_up = (d_hidden * pre_gate * sigmoid_gate).astype(BF)
    return d_gate, d_up


def input_rows(d_gate, d_up, gate_weight, up_weight):
    back_rows = lax.dot_general(d_gate, gate_weight, CONTRACT, preferred_element_type=F32)
    back_rows = back_rows + lax.dot_general(d_up, up_weight, CONTRACT, preferred_element_type=F32)
    return back_rows.astype(BF)


def outer_sum(left, right):
    return lax.dot_general(left, right, (((0,), (0,)), ((), ())), preferred_element_type=F32)


def routed_plan(tokens, route_ids, gate_probs, out_cot, w_gate, w_up, w_down):
    experts = lax.axis_size("expert")
    tok_rows, features = tokens.shape
    top_count = route_ids.shape[1]
    hidden = w_gate.shape[2]
    capacity = max(2, tok_rows * top_count * 4 // (3 * experts))
    total_rows = experts * capacity
    positions = slots(route_ids, experts, capacity)
    gate_weight, up_weight, down_weight = w_gate[0], w_up[0], w_down[0]

    def exchange(rows):
        blocks = rows.reshape(experts, capacity, features)
        return lax.all_to_all(blocks, "expert", 0, 0, tiled=True).reshape(-1, features)

    received = exchange(place(jnp.repeat(tokens, top_count, axis=0), positions, total_rows))
    pre_gate, pre_up, activation = hidden_rows(received, gate_weight, up_weight)
    result = jnp.dot(activation, down_weight, preferred_element_type=F32).astype(BF)
    picked = exchange(result)[positions].reshape(tok_rows, top_count, features)
    combined = jnp.einsum("tk,tkd->td", gate_probs, picked.astype(F32)).astype(BF)
    scaled = (gate_probs[:, :, None] * out_cot[:, None, :].astype(F32)).astype(BF)
    grads_in = exchange(place(scaled.reshape(-1, features), positions, total_rows))
    d_gate, d_up = hidden_grads(grads_in, pre_gate, pre_up, down_weight)
    back = exchange(input_rows(d_gate, d_up, gate_weight, up_weight))
    grad_tokens = jnp.sum(
        back[positions].reshape(tok_rows, top_count, features).astype(F32), axis=1
    ).astype(BF)
    gate_up_sum = lax.psum_scatter(
        outer_sum(received, jnp.concatenate([d_gate, d_up], axis=1)).astype(BF),
        "replica",
        scatter_dimension=0,
        tiled=True,
    )
    down_sum = lax.psum_scatter(
        outer_sum(activation, grads_in).astype(BF), "replica", scatter_dimension=0, tiled=True
    )
    return (
        combined,
        grad_tokens,
        gate_up_sum[:, :hidden][None],
        gate_up_sum[:, hidden:][None],
        down_sum[None],
    )


def split3(value):
    high = value.astype(BF)
    rest = value - high.astype(F32)
    mid = rest.astype(BF)
    low = (rest - mid.astype(F32)).astype(BF)
    return high, mid, low


def dense_plan(tokens, route_ids, gate_probs, out_cot, w_gate, w_up, w_down):
    experts = lax.axis_size("expert")
    tok_rows, features = tokens.shape
    top_count = route_ids.shape[1]
    hidden = w_gate.shape[2]
    capacity = max(2, tok_rows * top_count * 4 // (3 * experts))
    expert = lax.axis_index("expert")
    replica = lax.axis_index("replica")
    core = expert % 2
    gate_weight, up_weight, down_weight = w_gate[0], w_up[0], w_down[0]

    chosen = route_ids[:, :, None] == jnp.arange(experts, dtype=jnp.int32)
    share = jnp.sum(jnp.where(chosen, gate_probs[:, :, None], 0.0), axis=1)
    pad = -(3 * experts) % 128
    payload = jnp.concatenate(
        [tokens, out_cot, *split3(share), jnp.zeros((tok_rows, pad), BF)], axis=1
    )
    width = payload.shape[1]
    own = lax.all_gather(payload, "expert", axis=0, tiled=False)
    mine = lax.dynamic_index_in_dim(own.reshape(experts // 2, 2, tok_rows, width), core, 1, False)
    relay = lax.ppermute(mine, "replica", [(0, 1), (1, 0)])
    sibling = lax.ppermute(relay, "expert", [(i, i ^ 1) for i in range(experts)])
    other = jnp.stack([relay, sibling], axis=1).reshape(experts, tok_rows, width)

    together = 4
    groups = experts // together
    length = together * tok_rows
    room = together * capacity

    def pack(rows):
        rows = rows.reshape(groups, length, width)
        at = 2 * features + expert
        weight = sum(
            lax.dynamic_slice_in_dim(rows, at + i * experts, 1, 2)[:, :, 0].astype(F32)
            for i in range(3)
        )
        routed = weight > 0
        rank = jnp.cumsum(routed.astype(jnp.int32), axis=1) - 1
        pick = (rank[:, None, :] == jnp.arange(room)[None, :, None]) & routed[:, None, :]
        row_weight = jnp.sum(jnp.where(pick, weight[:, None, :], 0.0), axis=2).reshape(-1, 1)
        pick = pick.astype(BF)
        packed = jnp.einsum(
            "gst,gtd->gsd", pick, rows[:, :, : 2 * features], preferred_element_type=F32
        ).reshape(groups * room, 2 * features)
        x = packed[:, :features].astype(BF)
        cot = (row_weight * packed[:, features:]).astype(BF)
        return pick, row_weight, x, cot

    def spread(pick, rows):
        rows = rows.reshape(groups, room, features)
        return jnp.einsum("gst,gsd->gtd", pick, rows, preferred_element_type=F32).astype(BF)

    def middle(x, cot):
        pre_gate, pre_up, activation = hidden_rows(x, gate_weight, up_weight)
        d_gate, d_up = hidden_grads(cot, pre_gate, pre_up, down_weight)
        return activation, d_gate, d_up

    pick, row_weight, x, cot = pack(own)
    activation, d_gate, d_up = middle(x, cot)
    result = jnp.dot(activation, down_weight, preferred_element_type=F32).astype(BF)
    result = (row_weight * result.astype(F32)).astype(BF)
    back = input_rows(d_gate, d_up, gate_weight, up_weight)
    dense = jnp.concatenate([spread(pick, result), spread(pick, back)], axis=2)
    summed = lax.psum_scatter(
        dense.reshape(experts * tok_rows, 2 * features),
        "expert",
        scatter_dimension=0,
        tiled=True,
    )
    combined, grad_tokens = summed[:, :features], summed[:, features:]

    _, _, x2, cot2 = pack(other)
    activation2, d_gate2, d_up2 = middle(x2, cot2)
    both = lambda a, b: jnp.concatenate([a, b], axis=0)
    half = features // 2
    xs = lax.dynamic_slice_in_dim(both(x, x2), replica * half, half, 1)
    acts = lax.dynamic_slice_in_dim(
        both(activation, activation2), replica * (hidden // 2), hidden // 2, 1
    )
    grad_gate = outer_sum(xs, both(d_gate, d_gate2)).astype(BF)[None]
    grad_up = outer_sum(xs, both(d_up, d_up2)).astype(BF)[None]
    grad_down = outer_sum(acts, both(cot, cot2)).astype(BF)[None]
    return (combined, grad_tokens, grad_gate, grad_up, grad_down)


def solution(mesh):
    experts, replicas = mesh.shape["expert"], mesh.shape["replica"]
    placed = (
        P(("expert", "replica"), None),
        P(("expert", "replica"), None),
        P(("expert", "replica"), None),
        P(("expert", "replica"), None),
        P("expert", None, None),
        P("expert", None, None),
        P("expert", None, None),
    )
    small = replicas == 2 and experts <= 32 and experts % 4 == 0
    return jax.shard_map(
        dense_plan if small else routed_plan,
        mesh=mesh,
        in_specs=placed,
        out_specs=(
            P(("expert", "replica"), None),
            P(("expert", "replica"), None),
            P("expert", "replica", None),
            P("expert", "replica", None),
            P("expert", "replica", None),
        ),
        check_vma=False,
    )
```

```python
import math

import jax
import jax.numpy as jnp
from jax import lax
from jax.experimental import pallas as pl
from jax.experimental.pallas import tpu as pltpu
from jax.sharding import PartitionSpec as P

BF = jnp.bfloat16
F32 = jnp.float32
VMEM = 40 * 1024 * 1024


def slots(routes, experts, capacity):
    flat_ids = routes.reshape(-1)
    one_hot = (flat_ids[:, None] == jnp.arange(experts, dtype=jnp.int32)[None, :]).astype(jnp.int32)
    before = jnp.cumsum(one_hot, axis=0) - one_hot
    slot_rank = jnp.sum(before * one_hot, axis=1)
    return flat_ids * capacity + slot_rank


def place(token_rows, positions, total_rows):
    return (
        jnp.zeros((total_rows, token_rows.shape[1]), token_rows.dtype).at[positions].set(token_rows)
    )


def hidden_rows(token_rows, gate_weight, up_weight):
    pre_gate = jnp.dot(token_rows, gate_weight, preferred_element_type=F32)
    pre_up = jnp.dot(token_rows, up_weight, preferred_element_type=F32)
    activation = (jax.nn.silu(pre_gate) * pre_up).astype(BF)
    return (pre_gate, pre_up, activation)


CONTRACT = (((1,), (1,)), ((), ()))


def hidden_grads(grad_rows, pre_gate, pre_up, down_weight):
    d_hidden = lax.dot_general(grad_rows, down_weight, CONTRACT, preferred_element_type=F32)
    sigmoid_gate = jax.nn.sigmoid(pre_gate)
    d_gate = (d_hidden * pre_up * sigmoid_gate * (1.0 + pre_gate * (1.0 - sigmoid_gate))).astype(BF)
    d_up = (d_hidden * pre_gate * sigmoid_gate).astype(BF)
    return d_gate, d_up


def input_rows(d_gate, d_up, gate_weight, up_weight):
    back_rows = lax.dot_general(d_gate, gate_weight, CONTRACT, preferred_element_type=F32)
    back_rows = back_rows + lax.dot_general(d_up, up_weight, CONTRACT, preferred_element_type=F32)
    return back_rows.astype(BF)


def outer_sum(left, right):
    return lax.dot_general(left, right, (((0,), (0,)), ((), ())), preferred_element_type=F32)


def routed_plan(tokens, route_ids, gate_probs, out_cot, w_gate, w_up, w_down):
    experts = lax.axis_size("expert")
    tok_rows, features = tokens.shape
    top_count = route_ids.shape[1]
    hidden = w_gate.shape[2]
    capacity = max(2, tok_rows * top_count * 4 // (3 * experts))
    total_rows = experts * capacity
    positions = slots(route_ids, experts, capacity)
    gate_weight, up_weight, down_weight = w_gate[0], w_up[0], w_down[0]

    def exchange(rows):
        blocks = rows.reshape(experts, capacity, features)
        return lax.all_to_all(blocks, "expert", 0, 0, tiled=True).reshape(-1, features)

    received = exchange(place(jnp.repeat(tokens, top_count, axis=0), positions, total_rows))
    pre_gate, pre_up, activation = hidden_rows(received, gate_weight, up_weight)
    result = jnp.dot(activation, down_weight, preferred_element_type=F32).astype(BF)
    picked = exchange(result)[positions].reshape(tok_rows, top_count, features)
    combined = jnp.einsum("tk,tkd->td", gate_probs, picked.astype(F32)).astype(BF)
    scaled = (gate_probs[:, :, None] * out_cot[:, None, :].astype(F32)).astype(BF)
    grads_in = exchange(place(scaled.reshape(-1, features), positions, total_rows))
    d_gate, d_up = hidden_grads(grads_in, pre_gate, pre_up, down_weight)
    back = exchange(input_rows(d_gate, d_up, gate_weight, up_weight))
    grad_tokens = jnp.sum(
        back[positions].reshape(tok_rows, top_count, features).astype(F32), axis=1
    ).astype(BF)
    gate_up_sum = lax.psum_scatter(
        outer_sum(received, jnp.concatenate([d_gate, d_up], axis=1)).astype(BF),
        "replica",
        scatter_dimension=0,
        tiled=True,
    )
    down_sum = lax.psum_scatter(
        outer_sum(activation, grads_in).astype(BF), "replica", scatter_dimension=0, tiled=True
    )
    return (
        combined,
        grad_tokens,
        gate_up_sum[:, :hidden][None],
        gate_up_sum[:, hidden:][None],
        down_sum[None],
    )

def dot(left, right):
    return jnp.dot(left, right, preferred_element_type=F32)


def dot_t(left, right):
    return lax.dot_general(left, right, CONTRACT, preferred_element_type=F32)


def whole(array):
    return pl.BlockSpec(array.shape, lambda *_: (0,) * array.ndim)


def cost(flops, *arrays):
    moved = sum(math.prod(a.shape) * a.dtype.itemsize for a in arrays)
    return pl.CostEstimate(flops=flops, bytes_accessed=moved, transcendentals=0)


def params(steps=0):
    order = ("arbitrary",) * steps if steps else None
    return pltpu.CompilerParams(dimension_semantics=order, vmem_limit_bytes=VMEM)


def pack(pick, chunks):
    room, features = pick.shape[0] // 2, chunks[0].shape[1]

    def body(pick_ref, *refs):
        mine_ref, theirs_ref = refs[-2:]
        for at in range(0, features, 512):
            cols = pl.ds(at, min(512, features - at))
            rows = jnp.concatenate([ref[:, cols] for ref in refs[:-2]], axis=0)
            packed = dot(pick_ref[...], rows).astype(BF)
            mine_ref[:, cols] = packed[:room]
            theirs_ref[:, cols] = packed[room:]

    out = jax.ShapeDtypeStruct((room, features), BF)
    return pl.pallas_call(
        body,
        out_shape=(out, out),
        compiler_params=params(),
        cost_estimate=cost(2 * math.prod(pick.shape) * features, *chunks, out, out),
        name="pack",
    )(pick, *chunks)


def spread(pick, mine, theirs, parts):
    room, features = mine.shape
    length = pick.shape[1] // parts

    def body(pick_ref, mine_ref, theirs_ref, *outs):
        for at in range(0, features, 512):
            cols = pl.ds(at, min(512, features - at))
            rows = jnp.concatenate([mine_ref[:, cols], theirs_ref[:, cols]], axis=0)
            dense = lax.dot_general(
                pick_ref[...], rows, (((0,), (0,)), ((), ())), preferred_element_type=F32
            ).astype(BF)
            for i, out in enumerate(outs):
                out[:, cols] = dense[i * length : (i + 1) * length]

    out = jax.ShapeDtypeStruct((length, features), BF)
    return pl.pallas_call(
        body,
        out_shape=(out,) * parts,
        compiler_params=params(),
        cost_estimate=cost(2 * math.prod(pick.shape) * features, mine, theirs, *(out,) * parts),
        name="spread",
    )(pick, mine, theirs)


def forward(mine, theirs, weight, w_gate, w_up, w_down, with_result):
    room, features = mine.shape
    rows, hidden = 2 * room, w_gate.shape[2]
    block = 256 if hidden % 256 == 0 else hidden
    steps = hidden // block

    def body(mine_ref, theirs_ref, weight_ref, gate_ref, up_ref, down_ref, *refs):
        act_ref, to_gate_ref, to_up_ref = refs[:3]
        x = jnp.concatenate([mine_ref[...], theirs_ref[...]], axis=0)
        pre_gate = dot(x, gate_ref[0])
        pre_up = dot(x, up_ref[0])
        s = jax.nn.sigmoid(pre_gate)
        silu = pre_gate * s
        act = (silu * pre_up).astype(BF)
        act_ref[...] = act
        to_gate_ref[...] = pre_up * s * (1.0 + pre_gate * (1.0 - s))
        to_up_ref[...] = silu
        if with_result:
            mine_out, theirs_out, total = refs[3:]
            step = pl.program_id(0)
            part = dot(act, down_ref[0])

            @pl.when(step == 0)
            def _():
                total[...] = part

            @pl.when(step > 0)
            def _():
                total[...] += part

            @pl.when(step == steps - 1)
            def _():
                out = (total[...] * weight_ref[...]).astype(BF)
                mine_out[...] = out[:room]
                theirs_out[...] = out[room:]

    row_out = jax.ShapeDtypeStruct((room, features), BF)
    outs = [jax.ShapeDtypeStruct((rows, hidden), t) for t in (BF, F32, F32)]
    out_specs = [pl.BlockSpec((rows, block), lambda i: (0, i))] * 3
    scratch = []
    if with_result:
        outs += [row_out, row_out]
        out_specs += [whole(row_out)] * 2
        scratch = [pltpu.VMEM((rows, features), F32)]
    columns = pl.BlockSpec((1, features, block), lambda i: (0, 0, i))
    return pl.pallas_call(
        body,
        grid=(steps,),
        in_specs=[
            whole(mine),
            whole(theirs),
            whole(weight),
            columns,
            columns,
            pl.BlockSpec((1, block, features), lambda i: (0, i if with_result else 0, 0)),
        ],
        out_specs=out_specs,
        out_shape=outs,
        scratch_shapes=scratch,
        compiler_params=params(1),
        cost_estimate=cost(
            2 * rows * features * hidden * (3 if with_result else 2),
            mine, theirs, w_gate, w_up, *outs,
        ),
        name="forward",
    )(mine, theirs, weight, w_gate, w_up, w_down)


def backward(mine, theirs, weight, to_gate, to_up, w_gate, w_up, w_down, with_result):
    room, features = mine.shape
    rows, hidden = to_gate.shape
    block = 256 if hidden % 256 == 0 else hidden
    steps = hidden // block

    def body(
        mine_ref, theirs_ref, weight_ref, to_gate_ref, to_up_ref, gate_ref, up_ref, down_ref, *refs
    ):
        scaled_ref, d_gate_ref, d_up_ref = refs[:3]
        step = pl.program_id(0)

        @pl.when(step == 0)
        def _():
            cot = jnp.concatenate([mine_ref[...], theirs_ref[...]], axis=0)
            scaled_ref[...] = (cot.astype(F32) * weight_ref[...]).astype(BF)

        d_hidden = dot_t(scaled_ref[...], down_ref[0])
        d_gate = (d_hidden * to_gate_ref[...]).astype(BF)
        d_up = (d_hidden * to_up_ref[...]).astype(BF)
        d_gate_ref[...] = d_gate
        d_up_ref[...] = d_up
        if with_result:
            mine_out, theirs_out, total = refs[3:]
            part = dot_t(d_gate, gate_ref[0]) + dot_t(d_up, up_ref[0])

            @pl.when(step == 0)
            def _():
                total[...] = part

            @pl.when(step > 0)
            def _():
                total[...] += part

            @pl.when(step == steps - 1)
            def _():
                out = total[...].astype(BF)
                mine_out[...] = out[:room]
                theirs_out[...] = out[room:]

    row_out = jax.ShapeDtypeStruct((room, features), BF)
    scaled = jax.ShapeDtypeStruct((rows, features), BF)
    part_out = jax.ShapeDtypeStruct((rows, hidden), BF)
    outs = [scaled, part_out, part_out]
    part_spec = pl.BlockSpec((rows, block), lambda i: (0, i))
    out_specs = [whole(scaled), part_spec, part_spec]
    scratch = []
    if with_result:
        outs += [row_out, row_out]
        out_specs += [whole(row_out)] * 2
        scratch = [pltpu.VMEM((rows, features), F32)]
    columns = pl.BlockSpec((1, features, block), lambda i: (0, 0, i if with_result else 0))
    return pl.pallas_call(
        body,
        grid=(steps,),
        in_specs=[
            whole(mine),
            whole(theirs),
            whole(weight),
            part_spec,
            part_spec,
            columns,
            columns,
            pl.BlockSpec((1, block, features), lambda i: (0, i, 0)),
        ],
        out_specs=out_specs,
        out_shape=outs,
        scratch_shapes=scratch,
        compiler_params=params(1),
        cost_estimate=cost(
            2 * rows * features * hidden * (3 if with_result else 1), mine, theirs, w_down, *outs
        ),
        name="backward",
    )(mine, theirs, weight, to_gate, to_up, w_gate, w_up, w_down)


def rows_grad(left, right):
    return lax.dot_general(left, right, (((0,), (0,)), ((), ())), preferred_element_type=F32)


def gate_up_grad(replica, xs, d_gates, d_ups):
    features, hidden = xs[0].shape[1], d_gates[0].shape[1]
    half = features // 2
    block = 256 if half % 256 == 0 else half
    steps = half // block

    def body(_, *refs):
        n = len(xs)
        m = len(d_gates)
        x = jnp.concatenate([ref[...] for ref in refs[:n]], axis=0)
        for at, out in ((n, refs[-2]), (n + m, refs[-1])):
            d = jnp.concatenate([ref[...] for ref in refs[at : at + m]], axis=0)
            out[0] = rows_grad(x, d).astype(BF)

    out = jax.ShapeDtypeStruct((1, half, hidden), BF)
    rows = sum(x.shape[0] for x in xs)
    return pl.pallas_call(
        body,
        grid_spec=pltpu.PrefetchScalarGridSpec(
            num_scalar_prefetch=1,
            grid=(steps,),
            in_specs=[
                pl.BlockSpec((x.shape[0], block), lambda i, r: (0, r[0] * steps + i)) for x in xs
            ]
            + [whole(d) for d in (*d_gates, *d_ups)],
            out_specs=[pl.BlockSpec((1, block, hidden), lambda i, r: (0, i, 0))] * 2,
        ),
        out_shape=(out, out),
        compiler_params=params(1),
        cost_estimate=cost(4 * rows * half * hidden, *xs, *d_gates, *d_ups, out, out),
        name="gate_up_grad",
    )(replica, *xs, *d_gates, *d_ups)


def down_grad(replica, acts, scaleds):
    features, hidden = scaleds[0].shape[1], acts[0].shape[1]
    half = hidden // 2
    block = 512 if features % 512 == 0 else features

    def body(_, *refs):
        n = len(acts)
        act = jnp.concatenate([ref[...] for ref in refs[:n]], axis=0)
        cot = jnp.concatenate([ref[...] for ref in refs[n : 2 * n]], axis=0)
        refs[-1][0] = rows_grad(act, cot).astype(BF)

    out = jax.ShapeDtypeStruct((1, half, features), BF)
    rows = sum(a.shape[0] for a in acts)
    return pl.pallas_call(
        body,
        grid_spec=pltpu.PrefetchScalarGridSpec(
            num_scalar_prefetch=1,
            grid=(features // block,),
            in_specs=[pl.BlockSpec((a.shape[0], half), lambda i, r: (0, r[0])) for a in acts]
            + [pl.BlockSpec((c.shape[0], block), lambda i, r: (0, i)) for c in scaleds],
            out_specs=pl.BlockSpec((1, half, block), lambda i, r: (0, 0, i)),
        ),
        out_shape=out,
        compiler_params=params(1),
        cost_estimate=cost(2 * rows * half * features, *acts, *scaleds, out),
        name="down_grad",
    )(replica, *acts, *scaleds)


def route_plan(share, capacity, expert, replica, lines):
    tok_rows, experts = share.shape
    z, x, core = expert // 4, (expert // 2) % 2, expert % 2
    table = lax.all_gather(share.T, ("expert", "replica"), axis=0, tiled=False)
    table = table.reshape(lines, 2, 2, 2, experts, tok_rows)
    table = lax.dynamic_slice_in_dim(table, expert - core, 2, axis=4)
    for axis, index in ((1, x), (2, core), (3, replica), (4, core)):
        table = jnp.where(index == 0, table, jnp.flip(table, axis))
    table = jnp.flip(table, 0)
    table = jnp.concatenate([table, table], axis=0)
    table = lax.dynamic_slice_in_dim(table, lines - 1 - z, lines, axis=0)
    table = jnp.transpose(table, (3, 1, 2, 4, 0, 5)).reshape(2, 2, 2, 2, lines * tok_rows)
    routed = table > 0
    before = jnp.triu(jnp.ones((lines * tok_rows,) * 2, BF))
    rank = jnp.einsum("abcdt,tu->abcdu", routed.astype(BF), before, preferred_element_type=F32)
    slot = jnp.where(routed, rank - 1.0, -1.0)
    room = lines * capacity
    places = jnp.arange(room, dtype=F32)[:, None]
    pick = (slot[:, :, 0, :, None, :] == places).astype(BF)
    weight = jnp.sum(
        jnp.where(slot[:, :, :, 0, None, :] == places, table[:, :, :, 0, None, :], 0.0), axis=-1
    )
    length = lines * tok_rows
    return pick.reshape(2, 2, 2 * room, length), weight.reshape(2, 2, 2 * room, 1)


def dense_plan(tokens, route_ids, gate_probs, out_cot, w_gate, w_up, w_down):
    experts = lax.axis_size("expert")
    tok_rows, features = tokens.shape
    top_count = route_ids.shape[1]
    capacity = max(2, tok_rows * top_count * 4 // (3 * experts))
    lines = experts // 4
    expert = lax.axis_index("expert")
    replica = lax.axis_index("replica")

    def to_core(rows):
        return lax.ppermute(rows, "expert", [(i, i ^ 1) for i in range(experts)])

    def to_x(rows):
        return lax.ppermute(rows, "expert", [(i, i ^ 2) for i in range(experts)])

    def to_z(rows):
        return lax.ppermute(rows, "expert", [(i, (i + 4) % experts) for i in range(experts)])

    def to_y(rows):
        return lax.ppermute(rows, "replica", [(0, 1), (1, 0)])

    def gather(rows):
        near = [rows]
        for _ in range(lines - 1):
            near.append(to_z(near[-1]))
        far = [to_x(a) for a in near]
        return near, far

    chosen = route_ids[:, :, None] == jnp.arange(experts, dtype=jnp.int32)
    share = jnp.sum(jnp.where(chosen, gate_probs[:, :, None], 0.0), axis=1)
    pick, weight = route_plan(share, capacity, expert, replica, lines)

    token_sets = gather(tokens)
    cot_sets = gather(out_cot)
    other_tokens = [[to_y(a) for a in group] for group in token_sets]
    other_cots = [[to_y(a) for a in group] for group in cot_sets]

    def packed(plane, group, chunks):
        mine, theirs = pack(pick[plane, group], chunks)
        return mine, to_core(theirs)

    def home(results):
        near = spread(pick[0, 0], results[0][0], to_core(results[0][1]), lines)
        far = spread(pick[0, 1], results[1][0], to_core(results[1][1]), lines)
        total = None
        for s in (*range(1, lines), 0):
            part = near[s].astype(F32) + to_x(far[s]).astype(F32)
            if total is not None:
                part = part + to_z(total).astype(F32)
            total = part.astype(BF)
        return total

    xs, acts, firsts, results = [], [], [], []
    for plane, sets in enumerate((token_sets, other_tokens)):
        for group in range(2):
            x = packed(plane, group, sets[group])
            act, to_gate, to_up, *result = forward(
                *x, weight[plane, group], w_gate, w_up, w_down, plane == 0
            )
            xs += x
            acts.append(act)
            firsts.append((to_gate, to_up))
            results.append(result)
    combined = home(results[:2])

    scaleds, d_gates, d_ups, results = [], [], [], []
    for plane, sets in enumerate((cot_sets, other_cots)):
        for group in range(2):
            cot = packed(plane, group, sets[group])
            scaled, d_gate, d_up, *result = backward(
                *cot, weight[plane, group], *firsts[2 * plane + group],
                w_gate, w_up, w_down, plane == 0,
            )
            scaleds.append(scaled)
            d_gates.append(d_gate)
            d_ups.append(d_up)
            results.append(result)
    grad_tokens = home(results[:2])

    half = replica.astype(jnp.int32).reshape(1)
    grad_gate, grad_up = gate_up_grad(half, xs, d_gates, d_ups)
    grad_down = down_grad(half, acts, scaleds)
    return (combined, grad_tokens, grad_gate, grad_up, grad_down)


def solution(mesh):
    experts, replicas = mesh.shape["expert"], mesh.shape["replica"]
    placed = (
        P(("expert", "replica"), None),
        P(("expert", "replica"), None),
        P(("expert", "replica"), None),
        P(("expert", "replica"), None),
        P("expert", None, None),
        P("expert", None, None),
        P("expert", None, None),
    )
    small = replicas == 2 and experts <= 32 and experts % 4 == 0
    return jax.shard_map(
        dense_plan if small else routed_plan,
        mesh=mesh,
        in_specs=placed,
        out_specs=(
            P(("expert", "replica"), None),
            P(("expert", "replica"), None),
            P("expert", "replica", None),
            P("expert", "replica", None),
            P("expert", "replica", None),
        ),
        check_vma=False,
    )
```

```python
import math

import jax
import jax.numpy as jnp
from jax import lax
from jax.experimental import pallas as pl
from jax.experimental.pallas import tpu as pltpu
from jax.sharding import PartitionSpec as P

BF = jnp.bfloat16
F32 = jnp.float32
VMEM = 56 * 1024 * 1024
TOGETHER = 4


def slots(routes, experts, capacity):
    flat_ids = routes.reshape(-1)
    one_hot = (flat_ids[:, None] == jnp.arange(experts, dtype=jnp.int32)[None, :]).astype(jnp.int32)
    before = jnp.cumsum(one_hot, axis=0) - one_hot
    slot_rank = jnp.sum(before * one_hot, axis=1)
    return flat_ids * capacity + slot_rank


def place(token_rows, positions, total_rows):
    return (
        jnp.zeros((total_rows, token_rows.shape[1]), token_rows.dtype).at[positions].set(token_rows)
    )


def hidden_rows(token_rows, gate_weight, up_weight):
    pre_gate = jnp.dot(token_rows, gate_weight, preferred_element_type=F32)
    pre_up = jnp.dot(token_rows, up_weight, preferred_element_type=F32)
    activation = (jax.nn.silu(pre_gate) * pre_up).astype(BF)
    return (pre_gate, pre_up, activation)


CONTRACT = (((1,), (1,)), ((), ()))


def hidden_grads(grad_rows, pre_gate, pre_up, down_weight):
    d_hidden = lax.dot_general(grad_rows, down_weight, CONTRACT, preferred_element_type=F32)
    sigmoid_gate = jax.nn.sigmoid(pre_gate)
    d_gate = (d_hidden * pre_up * sigmoid_gate * (1.0 + pre_gate * (1.0 - sigmoid_gate))).astype(BF)
    d_up = (d_hidden * pre_gate * sigmoid_gate).astype(BF)
    return d_gate, d_up


def input_rows(d_gate, d_up, gate_weight, up_weight):
    back_rows = lax.dot_general(d_gate, gate_weight, CONTRACT, preferred_element_type=F32)
    back_rows = back_rows + lax.dot_general(d_up, up_weight, CONTRACT, preferred_element_type=F32)
    return back_rows.astype(BF)


def outer_sum(left, right):
    return lax.dot_general(left, right, (((0,), (0,)), ((), ())), preferred_element_type=F32)


def routed_plan(tokens, route_ids, gate_probs, out_cot, w_gate, w_up, w_down):
    experts = lax.axis_size("expert")
    tok_rows, features = tokens.shape
    top_count = route_ids.shape[1]
    hidden = w_gate.shape[2]
    capacity = max(2, tok_rows * top_count * 4 // (3 * experts))
    total_rows = experts * capacity
    positions = slots(route_ids, experts, capacity)
    gate_weight, up_weight, down_weight = w_gate[0], w_up[0], w_down[0]

    def exchange(rows):
        blocks = rows.reshape(experts, capacity, features)
        return lax.all_to_all(blocks, "expert", 0, 0, tiled=True).reshape(-1, features)

    received = exchange(place(jnp.repeat(tokens, top_count, axis=0), positions, total_rows))
    pre_gate, pre_up, activation = hidden_rows(received, gate_weight, up_weight)
    result = jnp.dot(activation, down_weight, preferred_element_type=F32).astype(BF)
    picked = exchange(result)[positions].reshape(tok_rows, top_count, features)
    combined = jnp.einsum("tk,tkd->td", gate_probs, picked.astype(F32)).astype(BF)
    scaled = (gate_probs[:, :, None] * out_cot[:, None, :].astype(F32)).astype(BF)
    grads_in = exchange(place(scaled.reshape(-1, features), positions, total_rows))
    d_gate, d_up = hidden_grads(grads_in, pre_gate, pre_up, down_weight)
    back = exchange(input_rows(d_gate, d_up, gate_weight, up_weight))
    grad_tokens = jnp.sum(
        back[positions].reshape(tok_rows, top_count, features).astype(F32), axis=1
    ).astype(BF)
    gate_up_sum = lax.psum_scatter(
        outer_sum(received, jnp.concatenate([d_gate, d_up], axis=1)).astype(BF),
        "replica",
        scatter_dimension=0,
        tiled=True,
    )
    down_sum = lax.psum_scatter(
        outer_sum(activation, grads_in).astype(BF), "replica", scatter_dimension=0, tiled=True
    )
    return (
        combined,
        grad_tokens,
        gate_up_sum[:, :hidden][None],
        gate_up_sum[:, hidden:][None],
        down_sum[None],
    )

def dot(left, right):
    return jnp.dot(left, right, preferred_element_type=F32)


def dot_t(left, right):
    return lax.dot_general(left, right, CONTRACT, preferred_element_type=F32)


def whole(array):
    return pl.BlockSpec(array.shape, lambda *_: (0,) * array.ndim)


def cost(flops, *arrays):
    moved = sum(math.prod(a.shape) * a.dtype.itemsize for a in arrays)
    return pl.CostEstimate(flops=flops, bytes_accessed=moved, transcendentals=0)


def params(steps=0):
    order = ("arbitrary",) * steps if steps else None
    return pltpu.CompilerParams(dimension_semantics=order, vmem_limit_bytes=VMEM)


def plan_and_pack(expert, experts, capacity, left, right):
    count, tok_rows, half = right.shape
    lanes = left.shape[2] - half
    length, room = TOGETHER * tok_rows, TOGETHER * capacity
    groups = count // TOGETHER
    width = 2 * half + lanes

    def body(expert_ref, left_ref, right_ref, mine_ref, theirs_ref, pick_ref, place_ref):
        shares = left_ref[:, :, half:].reshape(length, lanes).astype(F32)
        lane = lax.broadcasted_iota(jnp.int32, (length, lanes), 1)
        routed = []
        for index in (expert_ref[0], expert_ref[0] ^ 1):
            held = (lane == index) | (lane == index + experts) | (lane == index + 2 * experts)
            weight = jnp.sum(jnp.where(held, shares, 0.0), axis=1, keepdims=True)
            routed.append(jnp.broadcast_to((weight > 0).astype(F32), (length, room)))
        routed = jnp.concatenate(routed, axis=1)
        row = lax.broadcasted_iota(jnp.int32, (length, length), 0)
        col = lax.broadcasted_iota(jnp.int32, (length, length), 1)
        rank = dot((row >= col).astype(BF), routed.astype(BF))
        slot = lax.broadcasted_iota(jnp.int32, (length, 2 * room), 1) % room
        chosen = (rank == (slot + 1).astype(F32)) & (routed > 0)
        place = jnp.where(chosen, 1.0, 0.0)
        place_ref[0] = place.astype(BF)
        pick = place.T.astype(BF)
        pick_ref[0] = pick
        for ref, start, stop, to in (
            (left_ref, 0, half, 0),
            (right_ref, 0, half, half),
            (left_ref, half, half + lanes, 2 * half),
        ):
            for at in range(start, stop, 512):
                size = min(512, stop - at)
                rows = ref[:, :, at : at + size].reshape(length, size)
                packed = dot(pick, rows).astype(BF)
                out = pl.ds(to + at - start, size)
                mine_ref[:, out] = packed[:room]
                theirs_ref[:, out] = packed[room:]

    rows = jax.ShapeDtypeStruct((groups * room, width), BF)
    pick = jax.ShapeDtypeStruct((groups, 2 * room, length), BF)
    place = jax.ShapeDtypeStruct((groups, length, 2 * room), BF)
    outs = (rows, rows, pick, place)
    return pl.pallas_call(
        body,
        grid_spec=pltpu.PrefetchScalarGridSpec(
            num_scalar_prefetch=1,
            grid=(groups,),
            in_specs=[
                pl.BlockSpec((TOGETHER, tok_rows, half + lanes), lambda i, e: (i, 0, 0)),
                pl.BlockSpec((TOGETHER, tok_rows, half), lambda i, e: (i, 0, 0)),
            ],
            out_specs=[
                pl.BlockSpec((room, width), lambda i, e: (i, 0)),
                pl.BlockSpec((room, width), lambda i, e: (i, 0)),
                pl.BlockSpec((1, 2 * room, length), lambda i, e: (i, 0, 0)),
                pl.BlockSpec((1, length, 2 * room), lambda i, e: (i, 0, 0)),
            ],
        ),
        out_shape=outs,
        compiler_params=params(1),
        cost_estimate=cost(2 * groups * length * 2 * room * width, left, right, *outs),
        name="plan_and_pack",
    )(expert, left, right)


def pack(pick, chunks, first):
    count, tok_rows, features = chunks.shape
    room, length = pick.shape[1] // 2, pick.shape[2]
    groups = count // TOGETHER

    def body(pick_ref, rows_ref, mine_ref, theirs_ref):
        for at in range(0, features, 512):
            cols = pl.ds(at, 512)
            packed = dot(pick_ref[0], rows_ref[:, :, cols].reshape(length, 512)).astype(BF)
            mine_ref[:, cols] = packed[:room]
            theirs_ref[:, cols] = packed[room:]

    out = jax.ShapeDtypeStruct((groups * room, features), BF)
    return pl.pallas_call(
        body,
        grid=(groups,),
        in_specs=[
            pl.BlockSpec((1, 2 * room, length), lambda i: (first + i, 0, 0)),
            pl.BlockSpec((TOGETHER, tok_rows, features), lambda i: (i, 0, 0)),
        ],
        out_specs=[pl.BlockSpec((room, features), lambda i: (i, 0))] * 2,
        out_shape=(out, out),
        compiler_params=params(1),
        cost_estimate=cost(2 * groups * length * 2 * room * features, chunks, out, out),
        name="pack",
    )(pick, chunks)


def spread(place, mine, theirs):
    groups, length, slots_of = place.shape
    room, features = slots_of // 2, mine.shape[1]

    def body(place_ref, mine_ref, theirs_ref, out_ref):
        for at in range(0, features, 512):
            cols = pl.ds(at, 512)
            rows = jnp.concatenate([mine_ref[:, cols], theirs_ref[:, cols]], axis=0)
            out_ref[:, cols] = dot(place_ref[0], rows).astype(BF)

    out = jax.ShapeDtypeStruct((groups * length, features), BF)
    return pl.pallas_call(
        body,
        grid=(groups,),
        in_specs=[
            pl.BlockSpec((1, length, slots_of), lambda i: (i, 0, 0)),
            pl.BlockSpec((room, features), lambda i: (i, 0)),
            pl.BlockSpec((room, features), lambda i: (i, 0)),
        ],
        out_specs=pl.BlockSpec((length, features), lambda i: (i, 0)),
        out_shape=out,
        compiler_params=params(1),
        cost_estimate=cost(2 * math.prod(place.shape) * features, mine, theirs, out),
        name="spread",
    )(place, mine, theirs)


def row_weight(expert, experts, *lane_refs):
    lanes = jnp.concatenate([ref[...] for ref in lane_refs], axis=0).astype(F32)
    lane = lax.broadcasted_iota(jnp.int32, lanes.shape, 1)
    held = (lane == expert) | (lane == expert + experts) | (lane == expert + 2 * experts)
    return jnp.sum(jnp.where(held, lanes, 0.0), axis=1, keepdims=True)


def forward(expert, experts, mine, theirs, w_gate, w_up, w_down, with_result):
    part_rows, width = mine.shape
    _, features, hidden = w_gate.shape
    rows = 2 * part_rows
    block = 256 if hidden % 256 == 0 else hidden
    steps = hidden // block

    def body(expert_ref, mine_ref, theirs_ref, gate_ref, up_ref, down_ref, *refs):
        act_ref, to_gate_ref, to_up_ref = refs[:3]
        x = jnp.concatenate([mine_ref[:, :features], theirs_ref[:, :features]], axis=0)
        pre_gate = dot(x, gate_ref[0])
        pre_up = dot(x, up_ref[0])
        s = jax.nn.sigmoid(pre_gate)
        silu = pre_gate * s
        act = (silu * pre_up).astype(BF)
        act_ref[...] = act
        to_gate_ref[...] = pre_up * s * (1.0 + pre_gate * (1.0 - s))
        to_up_ref[...] = silu
        if with_result:
            mine_out, theirs_out, total = refs[3:]
            step = pl.program_id(0)
            part = dot(act, down_ref[0])

            @pl.when(step == 0)
            def _():
                total[...] = part

            @pl.when(step > 0)
            def _():
                total[...] += part

            @pl.when(step == steps - 1)
            def _():
                weight = row_weight(
                    expert_ref[0],
                    experts,
                    mine_ref.at[:, features:],
                    theirs_ref.at[:, features:],
                )
                out = (total[...] * weight).astype(BF)
                mine_out[...] = out[:part_rows]
                theirs_out[...] = out[part_rows:]

    row_out = jax.ShapeDtypeStruct((part_rows, features), BF)
    outs = [jax.ShapeDtypeStruct((rows, hidden), t) for t in (BF, F32, F32)]
    out_specs = [pl.BlockSpec((rows, block), lambda i, e: (0, i))] * 3
    scratch = []
    if with_result:
        outs += [row_out, row_out]
        out_specs += [whole(row_out)] * 2
        scratch = [pltpu.VMEM((rows, features), F32)]
    columns = pl.BlockSpec((1, features, block), lambda i, e: (0, 0, i))
    return pl.pallas_call(
        body,
        grid_spec=pltpu.PrefetchScalarGridSpec(
            num_scalar_prefetch=1,
            grid=(steps,),
            in_specs=[
                whole(mine),
                whole(theirs),
                columns,
                columns,
                pl.BlockSpec((1, block, features), lambda i, e: (0, i if with_result else 0, 0)),
            ],
            out_specs=out_specs,
            scratch_shapes=scratch,
        ),
        out_shape=outs,
        compiler_params=params(1),
        cost_estimate=cost(
            2 * rows * features * hidden * (3 if with_result else 2),
            mine, theirs, w_gate, w_up, *outs,
        ),
        name="forward",
    )(expert, mine, theirs, w_gate, w_up, w_down)


def backward(
    expert, experts, mine, theirs, x_mine, x_theirs, to_gate, to_up, weights, group, with_result
):
    part_rows, features = mine.shape
    hidden = to_gate.shape[1]
    rows = 2 * part_rows
    skip = to_gate.shape[0] // rows
    lanes = x_mine.shape[1] - features
    block = 256 if hidden % 256 == 0 else hidden
    steps = hidden // block

    def body(expert_ref, mine_ref, theirs_ref, lanes_a, lanes_b, *refs):
        gate_a, gate_b, up_a, up_b, w_gate_ref, w_up_ref, w_down_ref = refs[:7]
        scaled_ref, d_gate_ref, d_up_ref = refs[7:10]
        step = pl.program_id(0)

        @pl.when(step == 0)
        def _():
            weight = row_weight(expert_ref[0], experts, lanes_a, lanes_b)
            cot = jnp.concatenate([mine_ref[...], theirs_ref[...]], axis=0)
            scaled_ref[...] = (cot.astype(F32) * weight).astype(BF)

        d_hidden = dot_t(scaled_ref[...], w_down_ref[0])
        to_gates = jnp.concatenate([gate_a[...], gate_b[...]], axis=0)
        to_ups = jnp.concatenate([up_a[...], up_b[...]], axis=0)
        d_gate = (d_hidden * to_gates).astype(BF)
        d_up = (d_hidden * to_ups).astype(BF)
        d_gate_ref[...] = d_gate
        d_up_ref[...] = d_up
        if with_result:
            mine_out, theirs_out, total = refs[10:]
            part = dot_t(d_gate, w_gate_ref[0]) + dot_t(d_up, w_up_ref[0])

            @pl.when(step == 0)
            def _():
                total[...] = part

            @pl.when(step > 0)
            def _():
                total[...] += part

            @pl.when(step == steps - 1)
            def _():
                out = total[...].astype(BF)
                mine_out[...] = out[:part_rows]
                theirs_out[...] = out[part_rows:]

    row_out = jax.ShapeDtypeStruct((part_rows, features), BF)
    scaled = jax.ShapeDtypeStruct((rows, features), BF)
    part_out = jax.ShapeDtypeStruct((rows, hidden), BF)
    outs = [scaled, part_out, part_out]
    part_spec = pl.BlockSpec((rows, block), lambda i, e: (0, i))
    out_specs = [whole(scaled), part_spec, part_spec]
    scratch = []
    if with_result:
        outs += [row_out, row_out]
        out_specs += [whole(row_out)] * 2
        scratch = [pltpu.VMEM((rows, features), F32)]
    lane_spec = pl.BlockSpec((part_rows, lanes), lambda i, e: (group, features // lanes))
    first = pl.BlockSpec((part_rows, block), lambda i, e: (group, i))
    second = pl.BlockSpec((part_rows, block), lambda i, e: (group + skip, i))
    columns = pl.BlockSpec((1, features, block), lambda i, e: (0, 0, i if with_result else 0))
    return pl.pallas_call(
        body,
        grid_spec=pltpu.PrefetchScalarGridSpec(
            num_scalar_prefetch=1,
            grid=(steps,),
            in_specs=[
                whole(mine),
                whole(theirs),
                lane_spec,
                lane_spec,
                first,
                second,
                first,
                second,
                columns,
                columns,
                pl.BlockSpec((1, block, features), lambda i, e: (0, i, 0)),
            ],
            out_specs=out_specs,
            scratch_shapes=scratch,
        ),
        out_shape=outs,
        compiler_params=params(1),
        cost_estimate=cost(
            2 * rows * features * hidden * (3 if with_result else 1), mine, theirs, *outs
        ),
        name="backward",
    )(expert, mine, theirs, x_mine, x_theirs, to_gate, to_gate, to_up, to_up, *weights)


def rows_grad(left, right):
    return lax.dot_general(left, right, (((0,), (0,)), ((), ())), preferred_element_type=F32)


def in_order(mine, theirs, groups):
    size = mine.shape[0] // groups
    parts = []
    for at in range(0, mine.shape[0], size):
        parts += [mine[at : at + size], theirs[at : at + size]]
    return parts


def gate_up_grad(replica, xs, xs_other, d_gates, d_ups):
    features, hidden = xs[0].shape[1] // 256 * 256, d_gates[0].shape[1]
    half = features // 2
    block = 256
    steps = half // block
    n = len(d_gates)
    groups = n - 1

    def body(_, *refs):
        a, b, c, d = refs[:4]
        x = jnp.concatenate([a[...], b[...], *in_order(c[...], d[...], groups)], axis=0)
        for at, out in ((4, refs[-2]), (4 + n, refs[-1])):
            grads = jnp.concatenate([ref[...] for ref in refs[at : at + n]], axis=0)
            out[0] = rows_grad(x, grads).astype(BF)

    out = jax.ShapeDtypeStruct((1, half, hidden), BF)
    ins = (*xs, *xs_other)
    rows = sum(x.shape[0] for x in ins)
    return pl.pallas_call(
        body,
        grid_spec=pltpu.PrefetchScalarGridSpec(
            num_scalar_prefetch=1,
            grid=(steps,),
            in_specs=[
                pl.BlockSpec((x.shape[0], block), lambda i, r: (0, r[0] * steps + i)) for x in ins
            ]
            + [whole(d) for d in (*d_gates, *d_ups)],
            out_specs=[pl.BlockSpec((1, block, hidden), lambda i, r: (0, i, 0))] * 2,
        ),
        out_shape=(out, out),
        compiler_params=params(1),
        cost_estimate=cost(4 * rows * half * hidden, *ins, *d_gates, *d_ups, out, out),
        name="gate_up_grad",
    )(replica, *ins, *d_gates, *d_ups)


def down_grad(replica, act, act_other, scaleds):
    features, hidden = scaleds[0].shape[1], act.shape[1]
    half, rows = hidden // 2, act.shape[0]
    block = 512
    groups = len(scaleds) - 1

    def body(_, act_ref, other_ref, *refs):
        other = other_ref[...]
        acts = [act_ref[...], *in_order(other[: rows // 2], other[rows // 2 :], groups)]
        cot = jnp.concatenate([ref[...] for ref in refs[:-1]], axis=0)
        refs[-1][0] = rows_grad(jnp.concatenate(acts, axis=0), cot).astype(BF)

    out = jax.ShapeDtypeStruct((1, half, features), BF)
    return pl.pallas_call(
        body,
        grid_spec=pltpu.PrefetchScalarGridSpec(
            num_scalar_prefetch=1,
            grid=(features // block,),
            in_specs=[pl.BlockSpec((rows, half), lambda i, r: (0, r[0]))] * 2
            + [pl.BlockSpec((c.shape[0], block), lambda i, r: (0, i)) for c in scaleds],
            out_specs=pl.BlockSpec((1, half, block), lambda i, r: (0, 0, i)),
        ),
        out_shape=out,
        compiler_params=params(1),
        cost_estimate=cost(4 * rows * half * features, act, act_other, *scaleds, out),
        name="down_grad",
    )(replica, act, act_other, *scaleds)


def split3(value):
    high = value.astype(BF)
    rest = value - high.astype(F32)
    mid = rest.astype(BF)
    low = (rest - mid.astype(F32)).astype(BF)
    return high, mid, low


def dense_plan(tokens, route_ids, gate_probs, out_cot, w_gate, w_up, w_down):
    experts = lax.axis_size("expert")
    tok_rows, features = tokens.shape
    top_count = route_ids.shape[1]
    half = features // 2
    capacity = max(2, tok_rows * top_count * 4 // (3 * experts))
    expert = lax.axis_index("expert").astype(jnp.int32).reshape(1)
    replica = lax.axis_index("replica").astype(jnp.int32).reshape(1)
    same_core = [list(range(core, experts, 2)) for core in range(2)]

    def gather(rows):
        return lax.all_gather(rows, "expert", axis_index_groups=same_core)

    def home(rows):
        return lax.psum_scatter(
            rows, "expert", scatter_dimension=0, axis_index_groups=same_core, tiled=True
        )

    def to_core(rows):
        return lax.ppermute(rows, "expert", [(i, i ^ 1) for i in range(experts)])

    def to_y(rows):
        return lax.ppermute(rows, "replica", [(0, 1), (1, 0)])

    chosen = route_ids[:, :, None] == jnp.arange(experts, dtype=jnp.int32)
    share = jnp.sum(jnp.where(chosen, gate_probs[:, :, None], 0.0), axis=1)
    pad = jnp.zeros((tok_rows, -(3 * experts) % 128), BF)
    left = gather(jnp.concatenate([tokens[:, :half], *split3(share), pad], axis=1))
    right = gather(tokens[:, half:])
    cot = gather(out_cot)
    left_other, right_other = to_y(left), to_y(right)
    cot_other = [to_y(cot[at : at + TOGETHER]) for at in range(0, cot.shape[0], TOGETHER)]

    mine, theirs, pick, place = plan_and_pack(expert, experts, capacity, left, right)
    theirs = to_core(theirs)
    weights = (w_gate, w_up, w_down)
    act, to_gate, to_up, out_mine, out_theirs = forward(
        expert, experts, mine, theirs, *weights, True
    )
    combined = home(spread(place, out_mine, to_core(out_theirs)))

    cot_mine, cot_theirs = pack(pick, cot, 0)
    scaled, d_gate, d_up, out_mine, out_theirs = backward(
        expert, experts, cot_mine, to_core(cot_theirs), mine, theirs, to_gate, to_up,
        weights, 0, True,
    )
    grad_tokens = home(spread(place, out_mine, to_core(out_theirs)))
    scaleds, d_gates, d_ups = [scaled], [d_gate], [d_up]

    mine_other, theirs_other, pick, _ = plan_and_pack(
        expert, experts, capacity, left_other, right_other
    )
    theirs_other = to_core(theirs_other)
    act_other, to_gate, to_up = forward(
        expert, experts, mine_other, theirs_other, *weights, False
    )
    for group, rows in enumerate(cot_other):
        cot_mine, cot_theirs = pack(pick, rows, group)
        scaled, d_gate, d_up = backward(
            expert, experts, cot_mine, to_core(cot_theirs), mine_other, theirs_other,
            to_gate, to_up, weights, group, False,
        )
        scaleds.append(scaled)
        d_gates.append(d_gate)
        d_ups.append(d_up)

    grad_gate, grad_up = gate_up_grad(
        replica, (mine, theirs), (mine_other, theirs_other), d_gates, d_ups
    )
    grad_down = down_grad(replica, act, act_other, scaleds)
    return (combined, grad_tokens, grad_gate, grad_up, grad_down)


def dense_fits(mesh):
    experts, replicas = mesh.shape["expert"], mesh.shape["replica"]
    return replicas == 2 and experts % (2 * TOGETHER) == 0 and experts <= 16


def solution(mesh):
    placed = (
        P(("expert", "replica"), None),
        P(("expert", "replica"), None),
        P(("expert", "replica"), None),
        P(("expert", "replica"), None),
        P("expert", None, None),
        P("expert", None, None),
        P("expert", None, None),
    )
    return jax.shard_map(
        dense_plan if dense_fits(mesh) else routed_plan,
        mesh=mesh,
        in_specs=placed,
        out_specs=(
            P(("expert", "replica"), None),
            P(("expert", "replica"), None),
            P("expert", "replica", None),
            P("expert", "replica", None),
            P("expert", "replica", None),
        ),
        check_vma=False,
    )
```

```python
import jax
import jax.numpy as jnp
from jax import lax
from jax.experimental import pallas as pl
from jax.experimental.pallas import tpu as pltpu
from jax.sharding import PartitionSpec as P

BF = jnp.bfloat16
F32 = jnp.float32
VMEM = 56 * 1024 * 1024
TOGETHER = 4
LANES = 128
SMALL = pl.CostEstimate(flops=1, bytes_accessed=1, transcendentals=0)


def slots(routes, experts, capacity):
    flat_ids = routes.reshape(-1)
    one_hot = (flat_ids[:, None] == jnp.arange(experts, dtype=jnp.int32)[None, :]).astype(jnp.int32)
    before = jnp.cumsum(one_hot, axis=0) - one_hot
    slot_rank = jnp.sum(before * one_hot, axis=1)
    return flat_ids * capacity + slot_rank


def place(token_rows, positions, total_rows):
    return (
        jnp.zeros((total_rows, token_rows.shape[1]), token_rows.dtype).at[positions].set(token_rows)
    )


def hidden_rows(token_rows, gate_weight, up_weight):
    pre_gate = jnp.dot(token_rows, gate_weight, preferred_element_type=F32)
    pre_up = jnp.dot(token_rows, up_weight, preferred_element_type=F32)
    activation = (jax.nn.silu(pre_gate) * pre_up).astype(BF)
    return (pre_gate, pre_up, activation)


CONTRACT = (((1,), (1,)), ((), ()))


def hidden_grads(grad_rows, pre_gate, pre_up, down_weight):
    d_hidden = lax.dot_general(grad_rows, down_weight, CONTRACT, preferred_element_type=F32)
    sigmoid_gate = jax.nn.sigmoid(pre_gate)
    d_gate = (d_hidden * pre_up * sigmoid_gate * (1.0 + pre_gate * (1.0 - sigmoid_gate))).astype(BF)
    d_up = (d_hidden * pre_gate * sigmoid_gate).astype(BF)
    return d_gate, d_up


def input_rows(d_gate, d_up, gate_weight, up_weight):
    back_rows = lax.dot_general(d_gate, gate_weight, CONTRACT, preferred_element_type=F32)
    back_rows = back_rows + lax.dot_general(d_up, up_weight, CONTRACT, preferred_element_type=F32)
    return back_rows.astype(BF)


def outer_sum(left, right):
    return lax.dot_general(left, right, (((0,), (0,)), ((), ())), preferred_element_type=F32)


def routed_plan(tokens, route_ids, gate_probs, out_cot, w_gate, w_up, w_down):
    experts = lax.axis_size("expert")
    tok_rows, features = tokens.shape
    top_count = route_ids.shape[1]
    hidden = w_gate.shape[2]
    capacity = max(2, tok_rows * top_count * 4 // (3 * experts))
    total_rows = experts * capacity
    positions = slots(route_ids, experts, capacity)
    gate_weight, up_weight, down_weight = w_gate[0], w_up[0], w_down[0]

    def exchange(rows):
        blocks = rows.reshape(experts, capacity, features)
        return lax.all_to_all(blocks, "expert", 0, 0, tiled=True).reshape(-1, features)

    received = exchange(place(jnp.repeat(tokens, top_count, axis=0), positions, total_rows))
    pre_gate, pre_up, activation = hidden_rows(received, gate_weight, up_weight)
    result = jnp.dot(activation, down_weight, preferred_element_type=F32).astype(BF)
    picked = exchange(result)[positions].reshape(tok_rows, top_count, features)
    combined = jnp.einsum("tk,tkd->td", gate_probs, picked.astype(F32)).astype(BF)
    scaled = (gate_probs[:, :, None] * out_cot[:, None, :].astype(F32)).astype(BF)
    grads_in = exchange(place(scaled.reshape(-1, features), positions, total_rows))
    d_gate, d_up = hidden_grads(grads_in, pre_gate, pre_up, down_weight)
    back = exchange(input_rows(d_gate, d_up, gate_weight, up_weight))
    grad_tokens = jnp.sum(
        back[positions].reshape(tok_rows, top_count, features).astype(F32), axis=1
    ).astype(BF)
    gate_up_sum = lax.psum_scatter(
        outer_sum(received, jnp.concatenate([d_gate, d_up], axis=1)).astype(BF),
        "replica",
        scatter_dimension=0,
        tiled=True,
    )
    down_sum = lax.psum_scatter(
        outer_sum(activation, grads_in).astype(BF), "replica", scatter_dimension=0, tiled=True
    )
    return (
        combined,
        grad_tokens,
        gate_up_sum[:, :hidden][None],
        gate_up_sum[:, hidden:][None],
        down_sum[None],
    )

def dot(left, right):
    return jnp.dot(left, right, preferred_element_type=F32)


def whole(array):
    return pl.BlockSpec(array.shape, lambda *_: (0,) * array.ndim)


def params(steps=0):
    order = ("arbitrary",) * steps if steps else None
    return pltpu.CompilerParams(dimension_semantics=order, vmem_limit_bytes=VMEM)


ANYWHERE = pl.BlockSpec(memory_space=pl.ANY)


def landing(chunks):
    tok_rows, width = chunks[0].shape
    return [
        pltpu.VMEM((len(chunks) * tok_rows, width), BF),
        pltpu.SemaphoreType.DMA((len(chunks),)),
    ]


def load(chunk_refs, rows_ref, sems):
    copies = []
    for i, ref in enumerate(chunk_refs):
        size = ref.shape[0]
        copies.append(
            pltpu.make_async_copy(ref, rows_ref.at[i * size : (i + 1) * size], sems.at[i])
        )
        copies[-1].start()
    return copies


def plan_and_pack(expert, experts, capacity, chunks):
    tok_rows, width = chunks[0].shape
    lanes = LANES
    features = width - lanes
    length, room = TOGETHER * tok_rows, TOGETHER * capacity
    groups = len(chunks) // TOGETHER

    def body(expert_ref, *refs):
        mine_ref, theirs_ref, pick_ref, place_ref, rows_ref, sems = refs[len(chunks) :]
        copies = load(refs[: len(chunks)], rows_ref, sems)
        lane = lax.broadcasted_iota(jnp.int32, (length, lanes), 1)
        row = lax.broadcasted_iota(jnp.int32, (length, length), 0)
        col = lax.broadcasted_iota(jnp.int32, (length, length), 1)
        before = (row >= col).astype(BF)
        slot = lax.broadcasted_iota(jnp.int32, (length, 2 * room), 1) % room
        wanted = (slot + 1).astype(F32)
        for group in range(groups):
            for copy in copies[group * TOGETHER : (group + 1) * TOGETHER]:
                copy.wait()
            held_rows = slice(group * length, (group + 1) * length)
            shares = rows_ref[held_rows, features:].astype(F32)
            routed = []
            for index in (expert_ref[0], expert_ref[0] ^ 1):
                held = (lane == index) | (lane == index + experts) | (lane == index + 2 * experts)
                weight = jnp.sum(jnp.where(held, shares, 0.0), axis=1, keepdims=True)
                routed.append(jnp.broadcast_to((weight > 0).astype(F32), (length, room)))
            routed = jnp.concatenate(routed, axis=1)
            rank = dot(before, routed.astype(BF))
            place = jnp.where((rank == wanted) & (routed > 0), 1.0, 0.0)
            place_ref[group] = place.astype(BF)
            pick = place.T.astype(BF)
            pick_ref[group] = pick
            here = slice(group * room, (group + 1) * room)
            for at in range(0, width, 512):
                cols = slice(at, min(at + 512, width))
                packed = dot(pick, rows_ref[held_rows, cols]).astype(BF)
                mine_ref[here, cols] = packed[:room]
                theirs_ref[here, cols] = packed[room:]

    rows = jax.ShapeDtypeStruct((groups * room, width), BF)
    pick = jax.ShapeDtypeStruct((groups, 2 * room, length), BF)
    place = jax.ShapeDtypeStruct((groups, length, 2 * room), BF)
    return pl.pallas_call(
        body,
        grid_spec=pltpu.PrefetchScalarGridSpec(
            num_scalar_prefetch=1,
            grid=(1,),
            in_specs=[ANYWHERE] * len(chunks),
            out_specs=[whole(a) for a in (rows, rows, pick, place)],
            scratch_shapes=landing(chunks),
        ),
        out_shape=(rows, rows, pick, place),
        compiler_params=params(1),
        cost_estimate=SMALL,
        name="plan_and_pack",
    )(expert, *chunks)


def pack(pick, chunks):
    features = chunks[0].shape[1]
    groups, room, length = pick.shape[0], pick.shape[1] // 2, pick.shape[2]

    def body(pick_ref, *refs):
        mine_ref, theirs_ref, rows_ref, sems = refs[-4:]
        copies = load(refs[:-4], rows_ref, sems)
        for group in range(groups):
            for copy in copies[group * TOGETHER : (group + 1) * TOGETHER]:
                copy.wait()
            held_rows = slice(group * length, (group + 1) * length)
            here = slice(group * room, (group + 1) * room)
            for at in range(0, features, 512):
                cols = slice(at, at + 512)
                packed = dot(pick_ref[group], rows_ref[held_rows, cols]).astype(BF)
                mine_ref[here, cols] = packed[:room]
                theirs_ref[here, cols] = packed[room:]

    out = jax.ShapeDtypeStruct((groups * room, features), BF)
    return pl.pallas_call(
        body,
        in_specs=[pl.BlockSpec(memory_space=pltpu.VMEM)] + [ANYWHERE] * len(chunks),
        out_shape=(out, out),
        scratch_shapes=landing(chunks),
        compiler_params=params(),
        cost_estimate=SMALL,
        name="pack",
    )(pick, *chunks)


def spread(place, mine, theirs, parts):
    groups, length, slots_of = place.shape
    room, features = slots_of // 2, mine.shape[1]
    size = groups * length // parts

    def body(place_ref, mine_ref, theirs_ref, *outs):
        for group in reversed(range(groups)):
            here = slice(group * room, (group + 1) * room)
            for at in range(0, features, 512):
                cols = slice(at, at + 512)
                rows = jnp.concatenate([mine_ref[here, cols], theirs_ref[here, cols]], axis=0)
                dense = dot(place_ref[group], rows).astype(BF)
                for i in range(parts // groups):
                    out = outs[group * (parts // groups) + i]
                    out[:, cols] = dense[i * size : (i + 1) * size]

    out = jax.ShapeDtypeStruct((size, features), BF)
    return pl.pallas_call(
        body,
        out_shape=(out,) * parts,
        compiler_params=params(),
        cost_estimate=SMALL,
        name="spread",
    )(place, mine, theirs)


def split3(value):
    high = value.astype(BF)
    rest = value - high.astype(F32)
    mid = rest.astype(BF)
    low = (rest - mid.astype(F32)).astype(BF)
    return high, mid, low


def after(value, *earlier):
    return lax.optimization_barrier((value, *earlier))[0]


def dense_plan(tokens, route_ids, gate_probs, out_cot, w_gate, w_up, w_down):
    experts = lax.axis_size("expert")
    tok_rows, features = tokens.shape
    hidden = w_gate.shape[2]
    top_count = route_ids.shape[1]
    capacity = max(2, tok_rows * top_count * 4 // (3 * experts))
    expert = lax.axis_index("expert").astype(jnp.int32)
    replica = lax.axis_index("replica").astype(jnp.int32)
    w_gate, w_up, w_down = w_gate[0], w_up[0], w_down[0]

    def to_core(rows):
        return lax.ppermute(rows, "expert", [(i, i ^ 1) for i in range(experts)])

    def to_x(rows):
        return lax.ppermute(rows, "expert", [(i, i ^ 2) for i in range(experts)])

    def to_z(rows):
        return lax.ppermute(rows, "expert", [(i, (i + 4) % experts) for i in range(experts)])

    def to_y(rows):
        return lax.ppermute(rows, "replica", [(0, 1), (1, 0)])

    chosen = route_ids[:, :, None] == jnp.arange(experts, dtype=jnp.int32)
    share = jnp.sum(jnp.where(chosen, gate_probs[:, :, None], 0.0), axis=1)
    pad = jnp.zeros((tok_rows, LANES - 3 * experts), BF)

    token_near = [jnp.concatenate([tokens, *split3(share), pad], axis=1)]
    for _ in range(TOGETHER - 1):
        token_near.append(to_z(token_near[-1]))
    token_far = [to_x(a) for a in token_near]
    cot_near = [out_cot, to_z(after(out_cot, token_near[2]))]
    for _ in range(TOGETHER - 2):
        cot_near.append(to_z(cot_near[-1]))
    cot_far = [to_x(a) for a in cot_near]
    relay = [to_y(a) for pair in zip(token_near, token_far) for a in pair]
    relay += [to_y(a) for pair in zip(cot_near, cot_far) for a in pair]
    token_other = relay[0 : 2 * TOGETHER : 2] + relay[1 : 2 * TOGETHER : 2]
    cot_other = relay[2 * TOGETHER :: 2] + relay[2 * TOGETHER + 1 :: 2]

    def join(mine, theirs):
        return jnp.concatenate([mine, to_core(theirs)], axis=0)

    def enter(chunks, *earlier):
        mine, theirs, pick, place = plan_and_pack(
            expert.reshape(1), experts, capacity, chunks
        )
        theirs = after(to_core(theirs), *earlier)
        x = jnp.concatenate([mine[:, :features], theirs[:, :features]], axis=0)
        shares = jnp.concatenate([mine[:, features:], theirs[:, features:]], axis=0)
        held = (jnp.arange(LANES) % experts == expert) & (jnp.arange(LANES) < 3 * experts)
        weight = jnp.sum(jnp.where(held, shares.astype(F32), 0.0), axis=1, keepdims=True)
        pre_gate, pre_up = dot(x, w_gate), dot(x, w_up)
        activation = (jax.nn.silu(pre_gate) * pre_up).astype(BF)
        return x, weight, pick, place, pre_gate, pre_up, activation

    def leave(place, rows_of, *earlier):
        half = place.shape[0] * place.shape[2] // 2
        theirs = after(to_core(rows_of(slice(half, None))), *earlier)
        parts = spread(place, rows_of(slice(0, half)), theirs, 2 * TOGETHER)
        near, far = parts[:TOGETHER], parts[TOGETHER:]
        totals = []
        for s in (*range(1, TOGETHER), 0):
            part = near[s].astype(F32) + to_x(far[s]).astype(F32)
            if totals:
                part = part + to_z(totals[-1]).astype(F32)
            totals.append(part.astype(BF))
        return totals, parts

    def grads(x, activation, cot, d_gate, d_up):
        x = lax.dynamic_slice_in_dim(x, replica * (features // 2), features // 2, 1)
        activation = lax.dynamic_slice_in_dim(activation, replica * (hidden // 2), hidden // 2, 1)
        return outer_sum(x, d_gate), outer_sum(x, d_up), outer_sum(activation, cot)

    chunks = after([*token_near, *token_far], relay[0], relay[1], relay[2], cot_near[1])
    x, weight, pick, place, pre_gate, pre_up, activation = enter(
        chunks, relay[3], cot_near[2], cot_far[0]
    )
    activation = after(activation, relay[4], cot_near[3], cot_far[1])
    totals, sent = leave(
        place,
        lambda rows: (dot(activation[rows], w_down) * weight[rows]).astype(BF),
        relay[5],
        cot_far[2],
    )
    cot_chunks = after([*cot_near, *cot_far], sent, relay[6])
    cot = (join(*pack(pick, cot_chunks)).astype(F32) * weight).astype(BF)
    cot = after(cot, relay[7])
    d_gate, d_up = hidden_grads(cot, pre_gate, pre_up, w_down)
    d_gate, d_up = after((d_gate, d_up), relay[8])
    grad_totals, sent = leave(
        place,
        lambda rows: input_rows(d_gate[rows], d_up[rows], w_gate, w_up),
        relay[9],
        totals[1],
    )
    own = x, activation, cot, d_gate, d_up

    x, weight, pick, _, pre_gate, pre_up, activation = enter(
        after(token_other, sent, relay[10], totals[2]), relay[11], totals[3]
    )
    own = grads(*after(own, activation, relay[12], grad_totals[1]))
    cot_chunks = after(cot_other, own, grad_totals[2])
    cot = (join(*pack(pick, cot_chunks)).astype(F32) * weight).astype(BF)
    d_gate, d_up = hidden_grads(cot, pre_gate, pre_up, w_down)
    other = grads(x, activation, cot, d_gate, d_up)
    grad_gate, grad_up, grad_down = ((a + b).astype(BF)[None] for a, b in zip(own, other))
    return (totals[-1], grad_totals[-1], grad_gate, grad_up, grad_down)


def dense_fits(mesh):
    experts, replicas = mesh.shape["expert"], mesh.shape["replica"]
    return replicas == 2 and experts == 4 * TOGETHER


def solution(mesh):
    placed = (
        P(("expert", "replica"), None),
        P(("expert", "replica"), None),
        P(("expert", "replica"), None),
        P(("expert", "replica"), None),
        P("expert", None, None),
        P("expert", None, None),
        P("expert", None, None),
    )
    return jax.shard_map(
        dense_plan if dense_fits(mesh) else routed_plan,
        mesh=mesh,
        in_specs=placed,
        out_specs=(
            P(("expert", "replica"), None),
            P(("expert", "replica"), None),
            P("expert", "replica", None),
            P("expert", "replica", None),
            P("expert", "replica", None),
        ),
        check_vma=False,
    )
```

```python
import jax
import jax.numpy as jnp
from jax import lax
from jax.experimental import pallas as pl
from jax.experimental.pallas import tpu as pltpu
from jax.sharding import PartitionSpec as P

BF = jnp.bfloat16
F32 = jnp.float32
VMEM = 56 * 1024 * 1024
TOGETHER = 4
LANES = 128
SMALL = pl.CostEstimate(flops=1, bytes_accessed=1, transcendentals=0)


def slots(routes, experts, capacity):
    flat_ids = routes.reshape(-1)
    one_hot = (flat_ids[:, None] == jnp.arange(experts, dtype=jnp.int32)[None, :]).astype(jnp.int32)
    before = jnp.cumsum(one_hot, axis=0) - one_hot
    slot_rank = jnp.sum(before * one_hot, axis=1)
    return flat_ids * capacity + slot_rank


def place(token_rows, positions, total_rows):
    return (
        jnp.zeros((total_rows, token_rows.shape[1]), token_rows.dtype).at[positions].set(token_rows)
    )


def hidden_rows(token_rows, gate_weight, up_weight):
    pre_gate = jnp.dot(token_rows, gate_weight, preferred_element_type=F32)
    pre_up = jnp.dot(token_rows, up_weight, preferred_element_type=F32)
    activation = (jax.nn.silu(pre_gate) * pre_up).astype(BF)
    return (pre_gate, pre_up, activation)


CONTRACT = (((1,), (1,)), ((), ()))


def hidden_grads(grad_rows, pre_gate, pre_up, down_weight):
    d_hidden = lax.dot_general(grad_rows, down_weight, CONTRACT, preferred_element_type=F32)
    sigmoid_gate = jax.nn.sigmoid(pre_gate)
    d_gate = (d_hidden * pre_up * sigmoid_gate * (1.0 + pre_gate * (1.0 - sigmoid_gate))).astype(BF)
    d_up = (d_hidden * pre_gate * sigmoid_gate).astype(BF)
    return d_gate, d_up


def input_rows(d_gate, d_up, gate_weight, up_weight):
    back_rows = lax.dot_general(d_gate, gate_weight, CONTRACT, preferred_element_type=F32)
    back_rows = back_rows + lax.dot_general(d_up, up_weight, CONTRACT, preferred_element_type=F32)
    return back_rows.astype(BF)


def outer_sum(left, right):
    return lax.dot_general(left, right, (((0,), (0,)), ((), ())), preferred_element_type=F32)


def routed_plan(tokens, route_ids, gate_probs, out_cot, w_gate, w_up, w_down):
    experts = lax.axis_size("expert")
    tok_rows, features = tokens.shape
    top_count = route_ids.shape[1]
    hidden = w_gate.shape[2]
    capacity = max(2, tok_rows * top_count * 4 // (3 * experts))
    total_rows = experts * capacity
    positions = slots(route_ids, experts, capacity)
    gate_weight, up_weight, down_weight = w_gate[0], w_up[0], w_down[0]

    def exchange(rows):
        blocks = rows.reshape(experts, capacity, features)
        return lax.all_to_all(blocks, "expert", 0, 0, tiled=True).reshape(-1, features)

    received = exchange(place(jnp.repeat(tokens, top_count, axis=0), positions, total_rows))
    pre_gate, pre_up, activation = hidden_rows(received, gate_weight, up_weight)
    result = jnp.dot(activation, down_weight, preferred_element_type=F32).astype(BF)
    picked = exchange(result)[positions].reshape(tok_rows, top_count, features)
    combined = jnp.einsum("tk,tkd->td", gate_probs, picked.astype(F32)).astype(BF)
    scaled = (gate_probs[:, :, None] * out_cot[:, None, :].astype(F32)).astype(BF)
    grads_in = exchange(place(scaled.reshape(-1, features), positions, total_rows))
    d_gate, d_up = hidden_grads(grads_in, pre_gate, pre_up, down_weight)
    back = exchange(input_rows(d_gate, d_up, gate_weight, up_weight))
    grad_tokens = jnp.sum(
        back[positions].reshape(tok_rows, top_count, features).astype(F32), axis=1
    ).astype(BF)
    gate_up_sum = lax.psum_scatter(
        outer_sum(received, jnp.concatenate([d_gate, d_up], axis=1)).astype(BF),
        "replica",
        scatter_dimension=0,
        tiled=True,
    )
    down_sum = lax.psum_scatter(
        outer_sum(activation, grads_in).astype(BF), "replica", scatter_dimension=0, tiled=True
    )
    return (
        combined,
        grad_tokens,
        gate_up_sum[:, :hidden][None],
        gate_up_sum[:, hidden:][None],
        down_sum[None],
    )

def dot(left, right):
    return jnp.dot(left, right, preferred_element_type=F32)


def whole(array):
    return pl.BlockSpec(array.shape, lambda *_: (0,) * array.ndim)


def params(steps=0):
    order = ("arbitrary",) * steps if steps else None
    return pltpu.CompilerParams(dimension_semantics=order, vmem_limit_bytes=VMEM)


def column_specs(pieces, block):
    return [pl.BlockSpec((a.shape[0], block), lambda i, *_: (0, i)) for a in pieces]


def group_rows(refs, groups):
    each = len(refs) // groups
    return [
        jnp.concatenate([ref[...] for ref in refs[g * each : (g + 1) * each]], axis=0)
        for g in range(groups)
    ]


def plan_and_pack(expert, experts, capacity, pieces):
    features = pieces[0].shape[1] - LANES
    groups, block = 2, 512
    length = sum(a.shape[0] for a in pieces) // groups
    room = TOGETHER * capacity
    n = len(pieces)

    def body(expert_ref, *refs):
        mine_ref, theirs_ref, mine_lanes, theirs_lanes, pick_ref, place_ref = refs[2 * n :]

        @pl.when(pl.program_id(0) == 0)
        def _():
            lane = lax.broadcasted_iota(jnp.int32, (length, LANES), 1)
            row = lax.broadcasted_iota(jnp.int32, (length, length), 0)
            col = lax.broadcasted_iota(jnp.int32, (length, length), 1)
            before = (row >= col).astype(BF)
            slot = lax.broadcasted_iota(jnp.int32, (length, 2 * room), 1) % room
            wanted = (slot + 1).astype(F32)
            for group, lanes in enumerate(group_rows(refs[n : 2 * n], groups)):
                shares = lanes.astype(F32)
                routed = []
                for index in (expert_ref[0], expert_ref[0] ^ 1):
                    held = (lane == index) | (lane == index + experts)
                    held = held | (lane == index + 2 * experts)
                    weight = jnp.sum(jnp.where(held, shares, 0.0), axis=1, keepdims=True)
                    routed.append(jnp.broadcast_to((weight > 0).astype(F32), (length, room)))
                routed = jnp.concatenate(routed, axis=1)
                rank = dot(before, routed.astype(BF))
                place = jnp.where((rank == wanted) & (routed > 0), 1.0, 0.0)
                place_ref[group] = place.astype(BF)
                pick = place.T.astype(BF)
                pick_ref[group] = pick
                packed = dot(pick, lanes).astype(BF)
                here = slice(group * room, (group + 1) * room)
                mine_lanes[here] = packed[:room]
                theirs_lanes[here] = packed[room:]

        for group, rows in enumerate(group_rows(refs[:n], groups)):
            packed = dot(pick_ref[group], rows).astype(BF)
            here = slice(group * room, (group + 1) * room)
            mine_ref[here] = packed[:room]
            theirs_ref[here] = packed[room:]

    rows = jax.ShapeDtypeStruct((groups * room, features), BF)
    lanes = jax.ShapeDtypeStruct((groups * room, LANES), BF)
    pick = jax.ShapeDtypeStruct((groups, 2 * room, length), BF)
    place = jax.ShapeDtypeStruct((groups, length, 2 * room), BF)
    return pl.pallas_call(
        body,
        grid_spec=pltpu.PrefetchScalarGridSpec(
            num_scalar_prefetch=1,
            grid=(features // block,),
            in_specs=column_specs(pieces, block)
            + [
                pl.BlockSpec((a.shape[0], LANES), lambda i, e: (0, features // LANES))
                for a in pieces
            ],
            out_specs=column_specs((rows, rows), block)
            + [whole(a) for a in (lanes, lanes, pick, place)],
        ),
        out_shape=(rows, rows, lanes, lanes, pick, place),
        compiler_params=params(1),
        cost_estimate=SMALL,
        name="plan_and_pack",
    )(expert, *pieces, *pieces)


def pack(pick, pieces):
    features = pieces[0].shape[1]
    groups, room, block = pick.shape[0], pick.shape[1] // 2, 512

    def body(pick_ref, *refs):
        mine_ref, theirs_ref = refs[-2:]
        for group, rows in enumerate(group_rows(refs[:-2], groups)):
            packed = dot(pick_ref[group], rows).astype(BF)
            here = slice(group * room, (group + 1) * room)
            mine_ref[here] = packed[:room]
            theirs_ref[here] = packed[room:]

    out = jax.ShapeDtypeStruct((groups * room, features), BF)
    return pl.pallas_call(
        body,
        grid=(features // block,),
        in_specs=[whole(pick)] + column_specs(pieces, block),
        out_specs=column_specs((out, out), block),
        out_shape=(out, out),
        compiler_params=params(1),
        cost_estimate=SMALL,
        name="pack",
    )(pick, *pieces)


def spread(place, mine, theirs):
    groups, length, slots_of = place.shape
    room, features, block = slots_of // 2, mine.shape[1], 512
    half = length // 2

    def body(place_ref, mine_ref, theirs_ref, near_ref, first_ref, second_ref):
        dense = []
        for group in range(groups):
            here = slice(group * room, (group + 1) * room)
            rows = jnp.concatenate([mine_ref[here], theirs_ref[here]], axis=0)
            dense.append(dot(place_ref[group], rows).astype(BF))
        near_ref[...] = dense[0]
        tok_rows = length // TOGETHER
        first_ref[...] = dense[1][tok_rows : 3 * tok_rows]
        second_ref[...] = jnp.concatenate([dense[1][3 * tok_rows :], dense[1][:tok_rows]], axis=0)

    outs = [jax.ShapeDtypeStruct((size, features), BF) for size in (length, half, half)]
    return pl.pallas_call(
        body,
        grid=(features // block,),
        in_specs=[whole(place)] + column_specs((mine, theirs), block),
        out_specs=column_specs(outs, block),
        out_shape=outs,
        compiler_params=params(1),
        cost_estimate=SMALL,
        name="spread",
    )(place, mine, theirs)


def split3(value):
    high = value.astype(BF)
    rest = value - high.astype(F32)
    mid = rest.astype(BF)
    low = (rest - mid.astype(F32)).astype(BF)
    return high, mid, low


def after(value, *earlier):
    return lax.optimization_barrier((value, *earlier))[0]


def dense_plan(tokens, route_ids, gate_probs, out_cot, w_gate, w_up, w_down):
    experts = lax.axis_size("expert")
    tok_rows, features = tokens.shape
    hidden = w_gate.shape[2]
    top_count = route_ids.shape[1]
    capacity = max(2, tok_rows * top_count * 4 // (3 * experts))
    expert = lax.axis_index("expert").astype(jnp.int32)
    replica = lax.axis_index("replica").astype(jnp.int32)
    w_gate, w_up, w_down = w_gate[0], w_up[0], w_down[0]

    def to_core(rows):
        return lax.ppermute(rows, "expert", [(i, i ^ 1) for i in range(experts)])

    def to_x(rows):
        return lax.ppermute(rows, "expert", [(i, i ^ 2) for i in range(experts)])

    def to_z(rows):
        return lax.ppermute(rows, "expert", [(i, (i + 4) % experts) for i in range(experts)])

    def to_y(rows):
        return lax.ppermute(rows, "replica", [(0, 1), (1, 0)])

    chosen = route_ids[:, :, None] == jnp.arange(experts, dtype=jnp.int32)
    share = jnp.sum(jnp.where(chosen, gate_probs[:, :, None], 0.0), axis=1)
    pad = jnp.zeros((tok_rows, LANES - 3 * experts), BF)

    cot_far_own, cot_relay_own = to_x(out_cot), to_y(out_cot)
    token_own = jnp.concatenate([tokens, *split3(share), pad], axis=1)
    token_far_own, token_relay_own = to_x(token_own), to_y(token_own)
    ring = [after(to_z(token_own), cot_far_own)]
    ring.append(after(to_z(ring[0]), token_far_own, cot_relay_own))
    ring.append(after(to_z(ring[1]), token_relay_own))
    token_ring = jnp.concatenate(ring, axis=0)
    token_far_ring, token_relay_ring = to_x(token_ring), to_y(token_ring)
    token_relay_far_own = to_y(token_far_own)
    cot_relay_far_own = to_y(cot_far_own)
    ring = [after(to_z(after(out_cot, ring[1])), token_relay_far_own)]
    ring.append(to_z(ring[0]))
    ring.append(to_z(ring[1]))
    cot_ring = jnp.concatenate(ring, axis=0)
    cot_far_ring, cot_relay_ring = to_x(cot_ring), to_y(cot_ring)
    token_relay_far_ring = to_y(token_far_ring)
    cot_relay_far_ring = to_y(cot_far_ring)

    def enter(pieces, before_plan, before_dots):
        mine, theirs, mine_lanes, theirs_lanes, pick, place = plan_and_pack(
            after(expert.reshape(1), *before_plan), experts, capacity, pieces
        )
        theirs = after(to_core(theirs), *before_dots)
        x = jnp.concatenate([mine, theirs], axis=0)
        shares = jnp.concatenate([mine_lanes, to_core(theirs_lanes)], axis=0)
        held = (jnp.arange(LANES) % experts == expert) & (jnp.arange(LANES) < 3 * experts)
        weight = jnp.sum(jnp.where(held, shares.astype(F32), 0.0), axis=1, keepdims=True)
        pre_gate, pre_up = dot(x, w_gate), dot(x, w_up)
        activation = (jax.nn.silu(pre_gate) * pre_up).astype(BF)
        return x, weight, pick, place, pre_gate, pre_up, activation

    def enter_cot(pick, pieces, weight, *earlier):
        mine, theirs = pack(pick, pieces)
        cot = jnp.concatenate([mine, after(to_core(theirs), *earlier)], axis=0)
        return (cot.astype(F32) * weight).astype(BF)

    def leave(place, rows_of, *earlier):
        half = place.shape[0] * place.shape[2] // 2
        theirs = after(to_core(rows_of(slice(half, None))), *earlier)
        near, *far = spread(place, rows_of(slice(0, half)), theirs)
        arrived = [to_x(a) for a in far]
        totals = []
        for i, s in enumerate((1, 2, 3, 0)):
            part = near[s * tok_rows : (s + 1) * tok_rows].astype(F32)
            at = i % 2 * tok_rows
            part = part + arrived[i // 2][at : at + tok_rows].astype(F32)
            if totals:
                part = part + to_z(totals[-1]).astype(F32)
            totals.append(part.astype(BF))
        return totals, arrived, near

    def grads(x, activation, cot, d_gate, d_up):
        x = lax.dynamic_slice_in_dim(x, replica * (features // 2), features // 2, 1)
        activation = lax.dynamic_slice_in_dim(activation, replica * (hidden // 2), hidden // 2, 1)
        return outer_sum(x, d_gate), outer_sum(x, d_up), outer_sum(activation, cot)

    x, weight, pick, place, pre_gate, pre_up, activation = enter(
        (token_own, token_ring, token_far_own, token_far_ring),
        (token_relay_far_own, ring[1]),
        (token_relay_ring, cot_ring, cot_relay_far_own),
    )
    totals, arrived, near = leave(
        place, lambda rows: (dot(activation[rows], w_down) * weight[rows]).astype(BF)
    )
    cot = enter_cot(
        after(pick, near),
        (out_cot, cot_ring, cot_far_own, cot_far_ring),
        weight,
        token_relay_far_ring,
    )
    d_gate, d_up = hidden_grads(cot, pre_gate, pre_up, w_down)
    grad_totals, grad_arrived, near = leave(
        place,
        lambda rows: input_rows(d_gate[rows], d_up[rows], w_gate, w_up),
        arrived[0],
    )
    own = x, activation, cot, d_gate, d_up

    x, weight, pick, _, pre_gate, pre_up, activation = enter(
        (token_relay_own, token_relay_ring, token_relay_far_own, token_relay_far_ring),
        (near, totals[1], cot_relay_ring),
        (arrived[1],),
    )
    own = grads(*after(own, activation, totals[3], grad_arrived[0]))
    cot = enter_cot(
        after(pick, own, grad_totals[1]),
        (cot_relay_own, cot_relay_ring, cot_relay_far_own, cot_relay_far_ring),
        weight,
    )
    d_gate, d_up = hidden_grads(cot, pre_gate, pre_up, w_down)
    other = grads(x, activation, cot, d_gate, d_up)
    grad_gate, grad_up, grad_down = ((a + b).astype(BF)[None] for a, b in zip(own, other))
    return (totals[3], grad_totals[3], grad_gate, grad_up, grad_down)


def dense_fits(mesh):
    experts, replicas = mesh.shape["expert"], mesh.shape["replica"]
    return replicas == 2 and experts == 4 * TOGETHER


def solution(mesh):
    placed = (
        P(("expert", "replica"), None),
        P(("expert", "replica"), None),
        P(("expert", "replica"), None),
        P(("expert", "replica"), None),
        P("expert", None, None),
        P("expert", None, None),
        P("expert", None, None),
    )
    return jax.shard_map(
        dense_plan if dense_fits(mesh) else routed_plan,
        mesh=mesh,
        in_specs=placed,
        out_specs=(
            P(("expert", "replica"), None),
            P(("expert", "replica"), None),
            P("expert", "replica", None),
            P("expert", "replica", None),
            P("expert", "replica", None),
        ),
        check_vma=False,
    )
```

```python
import jax
import jax.numpy as jnp
from jax import lax
from jax.experimental import pallas as pl
from jax.experimental.pallas import tpu as pltpu
from jax.sharding import PartitionSpec as P

BF = jnp.bfloat16
F32 = jnp.float32
VMEM = 56 * 1024 * 1024
TOGETHER = 4
LANES = 128
SMALL = pl.CostEstimate(flops=1, bytes_accessed=1, transcendentals=0)


def slots(routes, experts, capacity):
    flat_ids = routes.reshape(-1)
    one_hot = (flat_ids[:, None] == jnp.arange(experts, dtype=jnp.int32)[None, :]).astype(jnp.int32)
    before = jnp.cumsum(one_hot, axis=0) - one_hot
    slot_rank = jnp.sum(before * one_hot, axis=1)
    return flat_ids * capacity + slot_rank


def place(token_rows, positions, total_rows):
    return (
        jnp.zeros((total_rows, token_rows.shape[1]), token_rows.dtype).at[positions].set(token_rows)
    )


def hidden_rows(token_rows, gate_weight, up_weight):
    pre_gate = jnp.dot(token_rows, gate_weight, preferred_element_type=F32)
    pre_up = jnp.dot(token_rows, up_weight, preferred_element_type=F32)
    activation = (jax.nn.silu(pre_gate) * pre_up).astype(BF)
    return (pre_gate, pre_up, activation)


CONTRACT = (((1,), (1,)), ((), ()))


def hidden_grads(grad_rows, pre_gate, pre_up, down_weight):
    d_hidden = lax.dot_general(grad_rows, down_weight, CONTRACT, preferred_element_type=F32)
    sigmoid_gate = jax.nn.sigmoid(pre_gate)
    d_gate = (d_hidden * pre_up * sigmoid_gate * (1.0 + pre_gate * (1.0 - sigmoid_gate))).astype(BF)
    d_up = (d_hidden * pre_gate * sigmoid_gate).astype(BF)
    return d_gate, d_up


def input_rows(d_gate, d_up, gate_weight, up_weight):
    back_rows = lax.dot_general(d_gate, gate_weight, CONTRACT, preferred_element_type=F32)
    back_rows = back_rows + lax.dot_general(d_up, up_weight, CONTRACT, preferred_element_type=F32)
    return back_rows.astype(BF)


def outer_sum(left, right):
    return lax.dot_general(left, right, (((0,), (0,)), ((), ())), preferred_element_type=F32)


def routed_plan(tokens, route_ids, gate_probs, out_cot, w_gate, w_up, w_down):
    experts = lax.axis_size("expert")
    tok_rows, features = tokens.shape
    top_count = route_ids.shape[1]
    hidden = w_gate.shape[2]
    capacity = max(2, tok_rows * top_count * 4 // (3 * experts))
    total_rows = experts * capacity
    positions = slots(route_ids, experts, capacity)
    gate_weight, up_weight, down_weight = w_gate[0], w_up[0], w_down[0]

    def exchange(rows):
        blocks = rows.reshape(experts, capacity, features)
        return lax.all_to_all(blocks, "expert", 0, 0, tiled=True).reshape(-1, features)

    received = exchange(place(jnp.repeat(tokens, top_count, axis=0), positions, total_rows))
    pre_gate, pre_up, activation = hidden_rows(received, gate_weight, up_weight)
    result = jnp.dot(activation, down_weight, preferred_element_type=F32).astype(BF)
    picked = exchange(result)[positions].reshape(tok_rows, top_count, features)
    combined = jnp.einsum("tk,tkd->td", gate_probs, picked.astype(F32)).astype(BF)
    scaled = (gate_probs[:, :, None] * out_cot[:, None, :].astype(F32)).astype(BF)
    grads_in = exchange(place(scaled.reshape(-1, features), positions, total_rows))
    d_gate, d_up = hidden_grads(grads_in, pre_gate, pre_up, down_weight)
    back = exchange(input_rows(d_gate, d_up, gate_weight, up_weight))
    grad_tokens = jnp.sum(
        back[positions].reshape(tok_rows, top_count, features).astype(F32), axis=1
    ).astype(BF)
    gate_up_sum = lax.psum_scatter(
        outer_sum(received, jnp.concatenate([d_gate, d_up], axis=1)).astype(BF),
        "replica",
        scatter_dimension=0,
        tiled=True,
    )
    down_sum = lax.psum_scatter(
        outer_sum(activation, grads_in).astype(BF), "replica", scatter_dimension=0, tiled=True
    )
    return (
        combined,
        grad_tokens,
        gate_up_sum[:, :hidden][None],
        gate_up_sum[:, hidden:][None],
        down_sum[None],
    )

def dot(left, right):
    return jnp.dot(left, right, preferred_element_type=F32)


def dot_t(left, right):
    return lax.dot_general(left, right, CONTRACT, preferred_element_type=F32)


def whole(array):
    return pl.BlockSpec(array.shape, lambda *_: (0,) * array.ndim)


def params(steps=0):
    order = ("arbitrary",) * steps if steps else None
    return pltpu.CompilerParams(dimension_semantics=order, vmem_limit_bytes=VMEM)


ANYWHERE = pl.BlockSpec(memory_space=pl.ANY)


def landing(chunks):
    tok_rows, width = chunks[0].shape
    return [
        pltpu.VMEM((len(chunks) * tok_rows, width), BF),
        pltpu.SemaphoreType.DMA((len(chunks),)),
    ]


def load(chunk_refs, rows_ref, sems):
    copies = []
    for i, ref in enumerate(chunk_refs):
        size = ref.shape[0]
        copies.append(
            pltpu.make_async_copy(ref, rows_ref.at[i * size : (i + 1) * size], sems.at[i])
        )
        copies[-1].start()
    return copies


def plan_and_pack(expert, experts, capacity, chunks):
    tok_rows, width = chunks[0].shape
    features = width - LANES
    groups = 2
    length, room = TOGETHER * tok_rows, TOGETHER * capacity

    def body(expert_ref, *refs):
        outs = refs[len(chunks) :]
        mine_ref, theirs_ref, mine_lanes, theirs_lanes, pick_ref, place_ref = outs[:6]
        rows_ref, sems = outs[6:]
        copies = load(refs[: len(chunks)], rows_ref, sems)
        lane = lax.broadcasted_iota(jnp.int32, (length, LANES), 1)
        row = lax.broadcasted_iota(jnp.int32, (length, length), 0)
        col = lax.broadcasted_iota(jnp.int32, (length, length), 1)
        before = (row >= col).astype(BF)
        slot = lax.broadcasted_iota(jnp.int32, (length, 2 * room), 1) % room
        wanted = (slot + 1).astype(F32)

        def places(shares, first):
            routed = []
            for index in (first, first ^ 1):
                held = (lane == index) | (lane == index + experts) | (lane == index + 2 * experts)
                weight = jnp.sum(jnp.where(held, shares, 0.0), axis=1, keepdims=True)
                routed.append(jnp.broadcast_to((weight > 0).astype(F32), (length, room)))
            routed = jnp.concatenate(routed, axis=1)
            rank = dot(before, routed.astype(BF))
            return jnp.where((rank == wanted) & (routed > 0), 1.0, 0.0)

        for group in range(groups):
            for copy in copies[group * TOGETHER : (group + 1) * TOGETHER]:
                copy.wait()
            held_rows = slice(group * length, (group + 1) * length)
            lanes = rows_ref[held_rows, features:]
            place = places(lanes.astype(F32), expert_ref[0])
            if group == 0:
                place_ref[:, : 2 * room] = place.astype(BF)
                place_ref[:, 2 * room :] = places(lanes.astype(F32), expert_ref[0] ^ 2).astype(BF)
            pick = place.T.astype(BF)
            pick_ref[group] = pick
            here = slice(group * room, (group + 1) * room)
            packed = dot(pick, lanes).astype(BF)
            mine_lanes[here] = packed[:room]
            theirs_lanes[here] = packed[room:]
            for at in range(0, features, 512):
                cols = slice(at, at + 512)
                packed = dot(pick, rows_ref[held_rows, cols]).astype(BF)
                mine_ref[here, cols] = packed[:room]
                theirs_ref[here, cols] = packed[room:]

    rows = jax.ShapeDtypeStruct((groups * room, features), BF)
    lanes = jax.ShapeDtypeStruct((groups * room, LANES), BF)
    pick = jax.ShapeDtypeStruct((groups, 2 * room, length), BF)
    place = jax.ShapeDtypeStruct((length, 4 * room), BF)
    outs = (rows, rows, lanes, lanes, pick, place)
    return pl.pallas_call(
        body,
        grid_spec=pltpu.PrefetchScalarGridSpec(
            num_scalar_prefetch=1,
            grid=(1,),
            in_specs=[ANYWHERE] * len(chunks),
            out_specs=[whole(a) for a in outs],
            scratch_shapes=landing(chunks),
        ),
        out_shape=outs,
        compiler_params=params(1),
        cost_estimate=SMALL,
        name="plan_and_pack",
    )(expert, *chunks)


def pack(pick, chunks):
    features = chunks[0].shape[1]
    groups, room, length = pick.shape[0], pick.shape[1] // 2, pick.shape[2]

    def body(pick_ref, *refs):
        mine_ref, theirs_ref, rows_ref, sems = refs[len(chunks) :]
        copies = load(refs[: len(chunks)], rows_ref, sems)
        for group in range(groups):
            for copy in copies[group * TOGETHER : (group + 1) * TOGETHER]:
                copy.wait()
            held_rows = slice(group * length, (group + 1) * length)
            here = slice(group * room, (group + 1) * room)
            for at in range(0, features, 512):
                cols = slice(at, at + 512)
                packed = dot(pick_ref[group], rows_ref[held_rows, cols]).astype(BF)
                mine_ref[here, cols] = packed[:room]
                theirs_ref[here, cols] = packed[room:]

    out = jax.ShapeDtypeStruct((groups * room, features), BF)
    return pl.pallas_call(
        body,
        in_specs=[pl.BlockSpec(memory_space=pltpu.VMEM)] + [ANYWHERE] * len(chunks),
        out_shape=(out, out),
        scratch_shapes=landing(chunks),
        compiler_params=params(),
        cost_estimate=SMALL,
        name="pack",
    )(pick, *chunks)


def spread(place, parts):
    length, slots_of = place.shape
    room, features = parts[0].shape
    size = length // TOGETHER

    def body(place_ref, *refs):
        outs = refs[len(parts) :]
        for at in range(0, features, 512):
            cols = slice(at, at + 512)
            rows = jnp.concatenate([ref[:, cols] for ref in refs[: len(parts)]], axis=0)
            dense = dot(place_ref[...], rows).astype(BF)
            for i, out in enumerate(outs):
                out[:, cols] = dense[i * size : (i + 1) * size]

    out = jax.ShapeDtypeStruct((size, features), BF)
    return pl.pallas_call(
        body,
        out_shape=(out,) * TOGETHER,
        compiler_params=params(),
        cost_estimate=SMALL,
        name="spread",
    )(place, *parts)


def row_weight(expert, experts, *lane_refs):
    lanes = jnp.concatenate([ref[...] for ref in lane_refs], axis=0).astype(F32)
    lane = lax.broadcasted_iota(jnp.int32, lanes.shape, 1)
    held = (lane == expert) | (lane == expert + experts) | (lane == expert + 2 * experts)
    return jnp.sum(jnp.where(held, lanes, 0.0), axis=1, keepdims=True)


def forward(expert, experts, mine, theirs, mine_lanes, theirs_lanes, weights, with_result):
    w_gate, w_up, w_down = weights
    part, features = mine.shape
    hidden = w_gate.shape[2]
    rows, block, wide = 2 * part, 256, 1024
    first = hidden // block
    steps = first + (features // wide if with_result else 0)

    def body(expert_ref, mine_ref, theirs_ref, lanes_a, lanes_b, gate_ref, up_ref, *refs):
        down_ref = refs[0] if with_result else None
        act_ref, to_gate_ref, to_up_ref, weight_ref, *outs = refs[int(with_result) :]
        step = pl.program_id(0)

        @pl.when(step == 0)
        def _():
            weight = row_weight(expert_ref[0], experts, lanes_a, lanes_b)
            weight_ref[...] = jnp.broadcast_to(weight, weight_ref.shape)

        @pl.when(step < first)
        def _():
            x = jnp.concatenate([mine_ref[...], theirs_ref[...]], axis=0)
            pre_gate = dot(x, gate_ref[0])
            pre_up = dot(x, up_ref[0])
            s = jax.nn.sigmoid(pre_gate)
            silu = pre_gate * s
            act_ref[:, pl.ds(pl.multiple_of(step * block, block), block)] = (
                silu * pre_up
            ).astype(BF)
            to_gate_ref[...] = pre_up * s * (1.0 + pre_gate * (1.0 - s))
            to_up_ref[...] = silu

        if with_result:

            @pl.when(step >= first)
            def _():
                out = dot(act_ref[...], down_ref[0])
                out = (out * weight_ref[:, :1]).astype(BF)
                near, far, theirs_out = outs
                near[...] = out[: part // 2]
                far[...] = out[part // 2 : part]
                theirs_out[...] = out[part:]

    def early(i):
        return jnp.minimum(i, first - 1)

    def late(i):
        return jnp.maximum(i - first, 0)

    act = jax.ShapeDtypeStruct((rows, hidden), BF)
    factor = jax.ShapeDtypeStruct((rows, hidden), F32)
    weight = jax.ShapeDtypeStruct((rows, LANES), F32)
    outs = [act, factor, factor, weight]
    factor_spec = pl.BlockSpec((rows, block), lambda i, e: (0, early(i)))
    out_specs = [whole(act), factor_spec, factor_spec, whole(weight)]
    columns = pl.BlockSpec((1, features, block), lambda i, e: (0, 0, early(i)))
    in_specs = [whole(a) for a in (mine, theirs, mine_lanes, theirs_lanes)] + [columns, columns]
    ins = [mine, theirs, mine_lanes, theirs_lanes, w_gate, w_up]
    if with_result:
        ins.append(w_down)
        in_specs.append(pl.BlockSpec((1, hidden, wide), lambda i, e: (0, 0, late(i))))
        for size in (part // 2, part // 2, part):
            outs.append(jax.ShapeDtypeStruct((size, features), BF))
            out_specs.append(pl.BlockSpec((size, wide), lambda i, e: (0, late(i))))
    return pl.pallas_call(
        body,
        grid_spec=pltpu.PrefetchScalarGridSpec(
            num_scalar_prefetch=1, grid=(steps,), in_specs=in_specs, out_specs=out_specs
        ),
        out_shape=outs,
        compiler_params=params(1),
        cost_estimate=SMALL,
        name="forward",
    )(expert, *ins)


def backward(mine, theirs, weight, to_gate, to_up, weights, with_result):
    w_gate, w_up, w_down = weights
    part, features = mine.shape
    rows, hidden = to_gate.shape
    block, wide = 256, 1024
    first = hidden // block
    steps = first + (features // wide if with_result else 0)

    def body(mine_ref, theirs_ref, weight_ref, to_gate_ref, to_up_ref, down_ref, *refs):
        gate_ref, up_ref = refs[:2] if with_result else (None, None)
        scaled_ref, d_gate_ref, d_up_ref, *outs = refs[2 * int(with_result) :]
        step = pl.program_id(0)

        @pl.when(step == 0)
        def _():
            cot = jnp.concatenate([mine_ref[...], theirs_ref[...]], axis=0)
            scaled_ref[...] = (cot.astype(F32) * weight_ref[:, :1]).astype(BF)

        @pl.when(step < first)
        def _():
            d_hidden = dot_t(scaled_ref[...], down_ref[0])
            cols = pl.ds(pl.multiple_of(step * block, block), block)
            d_gate_ref[:, cols] = (d_hidden * to_gate_ref[...]).astype(BF)
            d_up_ref[:, cols] = (d_hidden * to_up_ref[...]).astype(BF)

        if with_result:

            @pl.when(step >= first)
            def _():
                out = dot_t(d_gate_ref[...], gate_ref[0]) + dot_t(d_up_ref[...], up_ref[0])
                out = out.astype(BF)
                near, far, theirs_out = outs
                near[...] = out[: part // 2]
                far[...] = out[part // 2 : part]
                theirs_out[...] = out[part:]

    def early(i):
        return jnp.minimum(i, first - 1)

    def late(i):
        return jnp.maximum(i - first, 0)

    scaled = jax.ShapeDtypeStruct((rows, features), BF)
    grad = jax.ShapeDtypeStruct((rows, hidden), BF)
    outs = [scaled, grad, grad]
    out_specs = [whole(a) for a in outs]
    factor_spec = pl.BlockSpec((rows, block), lambda i: (0, early(i)))
    in_specs = [whole(a) for a in (mine, theirs, weight)] + [factor_spec] * 2
    in_specs.append(pl.BlockSpec((1, block, features), lambda i: (0, early(i), 0)))
    ins = [mine, theirs, weight, to_gate, to_up, w_down]
    if with_result:
        ins += [w_gate, w_up]
        in_specs += [pl.BlockSpec((1, wide, hidden), lambda i: (0, late(i), 0))] * 2
        for size in (part // 2, part // 2, part):
            outs.append(jax.ShapeDtypeStruct((size, features), BF))
            out_specs.append(pl.BlockSpec((size, wide), lambda i: (0, late(i))))
    return pl.pallas_call(
        body,
        grid=(steps,),
        in_specs=in_specs,
        out_specs=out_specs,
        out_shape=outs,
        compiler_params=params(1),
        cost_estimate=SMALL,
        name="backward",
    )(*ins)


def split3(value):
    high = value.astype(BF)
    rest = value - high.astype(F32)
    mid = rest.astype(BF)
    low = (rest - mid.astype(F32)).astype(BF)
    return high, mid, low


def after(value, *earlier):
    return lax.optimization_barrier((value, *earlier))[0]


def dense_plan(tokens, route_ids, gate_probs, out_cot, w_gate, w_up, w_down):
    experts = lax.axis_size("expert")
    tok_rows, features = tokens.shape
    hidden = w_gate.shape[2]
    top_count = route_ids.shape[1]
    capacity = max(2, tok_rows * top_count * 4 // (3 * experts))
    expert = lax.axis_index("expert").astype(jnp.int32)
    replica = lax.axis_index("replica").astype(jnp.int32)
    weights = (w_gate, w_up, w_down)

    def to_core(rows):
        return lax.ppermute(rows, "expert", [(i, i ^ 1) for i in range(experts)])

    def to_x(rows):
        return lax.ppermute(rows, "expert", [(i, i ^ 2) for i in range(experts)])

    def to_z(rows, step):
        return lax.ppermute(
            rows, "expert", [(i, (i + 4 * step) % experts) for i in range(experts)]
        )

    def to_y(rows):
        return lax.ppermute(rows, "replica", [(0, 1), (1, 0)])

    chosen = route_ids[:, :, None] == jnp.arange(experts, dtype=jnp.int32)
    share = jnp.sum(jnp.where(chosen, gate_probs[:, :, None], 0.0), axis=1)
    pad = jnp.zeros((tok_rows, LANES - 3 * experts), BF)

    token_own = jnp.concatenate([tokens, *split3(share), pad], axis=1)
    token_near = [token_own] + [to_z(token_own, step) for step in range(1, TOGETHER)]
    cot_source = after(out_cot, token_near[2])
    cot_near = [out_cot] + [to_z(cot_source, step) for step in range(1, TOGETHER)]
    token_sets = token_near + [to_x(a) for a in token_near]
    cot_sets = cot_near + [to_x(a) for a in cot_near]
    token_other = [to_y(a) for a in token_sets]
    cot_other = [to_y(a) for a in cot_sets]
    expert = expert.reshape(1)

    def enter(chunks, with_result, before_plan, before_dots):
        mine, theirs, mine_lanes, theirs_lanes, pick, place = plan_and_pack(
            after(expert, *before_plan), experts, capacity, chunks
        )
        theirs = after(to_core(theirs), *before_dots)
        act, to_gate, to_up, weight, *results = forward(
            expert, experts, mine, theirs, mine_lanes, to_core(theirs_lanes), weights, with_result
        )
        return (mine, theirs), pick, place, act, to_gate, to_up, weight, results

    def enter_cot(pick, chunks, weight, to_gate, to_up, with_result, *before_dots):
        mine, theirs = pack(pick, chunks)
        theirs = after(to_core(theirs), *before_dots)
        return backward(mine, theirs, weight, to_gate, to_up, weights, with_result)

    def leave(results):
        near, far, theirs = results
        theirs = to_core(theirs)
        half = near.shape[0]
        return near, theirs[:half], to_x(far), to_x(theirs[half:])

    def home(place, parts):
        own, *others = spread(place, parts)
        return [own] + [to_z(a, -step) for step, a in enumerate(others, 1)]

    def total(chunks):
        return sum(a.astype(F32) for a in chunks).astype(BF)

    def grads(rows, act, cot, d_gate, d_up):
        x = jnp.concatenate(
            [
                lax.dynamic_slice_in_dim(a, replica * (features // 2), features // 2, 1)
                for a in rows
            ],
            axis=0,
        )
        act = lax.dynamic_slice_in_dim(act, replica * (hidden // 2), hidden // 2, 1)
        return outer_sum(x, d_gate), outer_sum(x, d_up), outer_sum(act, cot)

    own_rows, pick, place, own_act, to_gate, to_up, weight, results = enter(
        token_sets, True, token_other + [cot_other[0]] + cot_sets[1:6], [*cot_sets[6:], cot_other[4]]
    )
    parts = leave(results)
    *own_grads, near, far, theirs = enter_cot(
        after(pick, results[0], cot_other[1]),
        cot_sets, weight, to_gate, to_up, True, cot_other[5],
    )
    chunks = home(after(place, near), parts)
    parts = leave((near, far, theirs))

    rows, pick, _, act, to_gate, to_up, weight, _ = enter(
        token_other, False, (chunks[0], cot_other[2]), (cot_other[6], chunks[1])
    )
    grad_chunks = home(after(place, act, cot_other[3], chunks[2]), parts)
    own_grads = after(tuple(own_grads), grad_chunks[0], cot_other[7], chunks[3])
    own = grads(own_rows, own_act, *own_grads)
    scaled, d_gate, d_up = enter_cot(
        after(pick, *own, grad_chunks[1]), cot_other, weight, to_gate, to_up, False, grad_chunks[2]
    )
    other = grads(rows, act, scaled, d_gate, d_up)
    grad_gate, grad_up, grad_down = ((a + b).astype(BF)[None] for a, b in zip(own, other))
    return (total(chunks), total(grad_chunks), grad_gate, grad_up, grad_down)


def dense_fits(mesh):
    experts, replicas = mesh.shape["expert"], mesh.shape["replica"]
    return replicas == 2 and experts == 4 * TOGETHER


def solution(mesh):
    placed = (
        P(("expert", "replica"), None),
        P(("expert", "replica"), None),
        P(("expert", "replica"), None),
        P(("expert", "replica"), None),
        P("expert", None, None),
        P("expert", None, None),
        P("expert", None, None),
    )
    return jax.shard_map(
        dense_plan if dense_fits(mesh) else routed_plan,
        mesh=mesh,
        in_specs=placed,
        out_specs=(
            P(("expert", "replica"), None),
            P(("expert", "replica"), None),
            P("expert", "replica", None),
            P("expert", "replica", None),
            P("expert", "replica", None),
        ),
        check_vma=False,
    )
```

```python
import jax
import jax.numpy as jnp
from jax import lax
from jax.experimental import pallas as pl
from jax.experimental.pallas import tpu as pltpu
from jax.sharding import PartitionSpec as P

BF = jnp.bfloat16
F32 = jnp.float32
VMEM = 56 * 1024 * 1024
TOGETHER = 4
LANES = 128
SMALL = pl.CostEstimate(flops=1, bytes_accessed=1, transcendentals=0)


def slots(routes, experts, capacity):
    flat_ids = routes.reshape(-1)
    one_hot = (flat_ids[:, None] == jnp.arange(experts, dtype=jnp.int32)[None, :]).astype(jnp.int32)
    before = jnp.cumsum(one_hot, axis=0) - one_hot
    slot_rank = jnp.sum(before * one_hot, axis=1)
    return flat_ids * capacity + slot_rank


def place(token_rows, positions, total_rows):
    return (
        jnp.zeros((total_rows, token_rows.shape[1]), token_rows.dtype).at[positions].set(token_rows)
    )


def hidden_rows(token_rows, gate_weight, up_weight):
    pre_gate = jnp.dot(token_rows, gate_weight, preferred_element_type=F32)
    pre_up = jnp.dot(token_rows, up_weight, preferred_element_type=F32)
    activation = (jax.nn.silu(pre_gate) * pre_up).astype(BF)
    return (pre_gate, pre_up, activation)


CONTRACT = (((1,), (1,)), ((), ()))


def hidden_grads(grad_rows, pre_gate, pre_up, down_weight):
    d_hidden = lax.dot_general(grad_rows, down_weight, CONTRACT, preferred_element_type=F32)
    sigmoid_gate = jax.nn.sigmoid(pre_gate)
    d_gate = (d_hidden * pre_up * sigmoid_gate * (1.0 + pre_gate * (1.0 - sigmoid_gate))).astype(BF)
    d_up = (d_hidden * pre_gate * sigmoid_gate).astype(BF)
    return d_gate, d_up


def input_rows(d_gate, d_up, gate_weight, up_weight):
    back_rows = lax.dot_general(d_gate, gate_weight, CONTRACT, preferred_element_type=F32)
    back_rows = back_rows + lax.dot_general(d_up, up_weight, CONTRACT, preferred_element_type=F32)
    return back_rows.astype(BF)


def outer_sum(left, right):
    return lax.dot_general(left, right, (((0,), (0,)), ((), ())), preferred_element_type=F32)


def routed_plan(tokens, route_ids, gate_probs, out_cot, w_gate, w_up, w_down):
    experts = lax.axis_size("expert")
    tok_rows, features = tokens.shape
    top_count = route_ids.shape[1]
    hidden = w_gate.shape[2]
    capacity = max(2, tok_rows * top_count * 4 // (3 * experts))
    total_rows = experts * capacity
    positions = slots(route_ids, experts, capacity)
    gate_weight, up_weight, down_weight = w_gate[0], w_up[0], w_down[0]

    def exchange(rows):
        blocks = rows.reshape(experts, capacity, features)
        return lax.all_to_all(blocks, "expert", 0, 0, tiled=True).reshape(-1, features)

    received = exchange(place(jnp.repeat(tokens, top_count, axis=0), positions, total_rows))
    pre_gate, pre_up, activation = hidden_rows(received, gate_weight, up_weight)
    result = jnp.dot(activation, down_weight, preferred_element_type=F32).astype(BF)
    picked = exchange(result)[positions].reshape(tok_rows, top_count, features)
    combined = jnp.einsum("tk,tkd->td", gate_probs, picked.astype(F32)).astype(BF)
    scaled = (gate_probs[:, :, None] * out_cot[:, None, :].astype(F32)).astype(BF)
    grads_in = exchange(place(scaled.reshape(-1, features), positions, total_rows))
    d_gate, d_up = hidden_grads(grads_in, pre_gate, pre_up, down_weight)
    back = exchange(input_rows(d_gate, d_up, gate_weight, up_weight))
    grad_tokens = jnp.sum(
        back[positions].reshape(tok_rows, top_count, features).astype(F32), axis=1
    ).astype(BF)
    gate_up_sum = lax.psum_scatter(
        outer_sum(received, jnp.concatenate([d_gate, d_up], axis=1)).astype(BF),
        "replica",
        scatter_dimension=0,
        tiled=True,
    )
    down_sum = lax.psum_scatter(
        outer_sum(activation, grads_in).astype(BF), "replica", scatter_dimension=0, tiled=True
    )
    return (
        combined,
        grad_tokens,
        gate_up_sum[:, :hidden][None],
        gate_up_sum[:, hidden:][None],
        down_sum[None],
    )

def dot(left, right):
    return jnp.dot(left, right, preferred_element_type=F32)


def whole(array):
    return pl.BlockSpec(array.shape, lambda *_: (0,) * array.ndim)


def params(steps=0):
    order = ("arbitrary",) * steps if steps else None
    return pltpu.CompilerParams(dimension_semantics=order, vmem_limit_bytes=VMEM)


ANYWHERE = pl.BlockSpec(memory_space=pl.ANY)


def landing(pieces):
    rows = sum(a.shape[0] for a in pieces)
    return [
        pltpu.VMEM((rows, pieces[0].shape[1]), BF),
        pltpu.SemaphoreType.DMA((len(pieces),)),
    ]


def load(piece_refs, rows_ref, sems):
    copies, at = [], 0
    for i, ref in enumerate(piece_refs):
        size = ref.shape[0]
        copies.append(pltpu.make_async_copy(ref, rows_ref.at[at : at + size], sems.at[i]))
        copies[-1].start()
        at += size
    return copies


def plan_and_pack(expert, experts, capacity, chunks):
    tok_rows, width = chunks[0].shape
    features = width - LANES
    groups, each = 2, len(chunks) // 2
    length, room = TOGETHER * tok_rows, TOGETHER * capacity

    def body(expert_ref, *refs):
        outs = refs[len(chunks) :]
        mine_ref, theirs_ref, mine_lanes, theirs_lanes, pick_ref, place_ref = outs[:6]
        rows_ref, sems = outs[6:]
        copies = load(refs[: len(chunks)], rows_ref, sems)
        lane = lax.broadcasted_iota(jnp.int32, (length, LANES), 1)
        row = lax.broadcasted_iota(jnp.int32, (length, length), 0)
        col = lax.broadcasted_iota(jnp.int32, (length, length), 1)
        before = (row >= col).astype(BF)
        slot = lax.broadcasted_iota(jnp.int32, (length, 2 * room), 1) % room
        wanted = (slot + 1).astype(F32)

        def places(shares, first):
            routed = []
            for index in (first, first ^ 1):
                held = (lane == index) | (lane == index + experts) | (lane == index + 2 * experts)
                weight = jnp.sum(jnp.where(held, shares, 0.0), axis=1, keepdims=True)
                routed.append(jnp.broadcast_to((weight > 0).astype(F32), (length, room)))
            routed = jnp.concatenate(routed, axis=1)
            rank = dot(before, routed.astype(BF))
            return jnp.where((rank == wanted) & (routed > 0), 1.0, 0.0)

        for group in range(groups):
            for copy in copies[group * each : (group + 1) * each]:
                copy.wait()
            held_rows = slice(group * length, (group + 1) * length)
            lanes = rows_ref[held_rows, features:]
            place = places(lanes.astype(F32), expert_ref[0])
            if group == 0:
                place_ref[:, : 2 * room] = place.astype(BF)
                place_ref[:, 2 * room :] = places(lanes.astype(F32), expert_ref[0] ^ 2).astype(BF)
            pick = place.T.astype(BF)
            pick_ref[group] = pick
            here = slice(group * room, (group + 1) * room)
            packed = dot(pick, lanes).astype(BF)
            mine_lanes[here] = packed[:room]
            theirs_lanes[here] = packed[room:]
            for at in range(0, features, 512):
                cols = slice(at, at + 512)
                packed = dot(pick, rows_ref[held_rows, cols]).astype(BF)
                mine_ref[here, cols] = packed[:room]
                theirs_ref[here, cols] = packed[room:]

    rows = jax.ShapeDtypeStruct((groups * room, features), BF)
    lanes = jax.ShapeDtypeStruct((groups * room, LANES), BF)
    pick = jax.ShapeDtypeStruct((groups, 2 * room, length), BF)
    place = jax.ShapeDtypeStruct((length, 4 * room), BF)
    outs = (rows, rows, lanes, lanes, pick, place)
    return pl.pallas_call(
        body,
        grid_spec=pltpu.PrefetchScalarGridSpec(
            num_scalar_prefetch=1,
            grid=(1,),
            in_specs=[ANYWHERE] * len(chunks),
            out_specs=[whole(a) for a in outs],
            scratch_shapes=landing(chunks),
        ),
        out_shape=outs,
        compiler_params=params(1),
        cost_estimate=SMALL,
        name="plan_and_pack",
    )(expert, *chunks)


def pack(pick, chunks):
    features = chunks[0].shape[1]
    groups, room, length = pick.shape[0], pick.shape[1] // 2, pick.shape[2]
    each = len(chunks) // groups

    def body(pick_ref, *refs):
        mine_ref, theirs_ref, rows_ref, sems = refs[len(chunks) :]
        copies = load(refs[: len(chunks)], rows_ref, sems)
        for group in range(groups):
            for copy in copies[group * each : (group + 1) * each]:
                copy.wait()
            held_rows = slice(group * length, (group + 1) * length)
            here = slice(group * room, (group + 1) * room)
            for at in range(0, features, 512):
                cols = slice(at, at + 512)
                packed = dot(pick_ref[group], rows_ref[held_rows, cols]).astype(BF)
                mine_ref[here, cols] = packed[:room]
                theirs_ref[here, cols] = packed[room:]

    out = jax.ShapeDtypeStruct((groups * room, features), BF)
    return pl.pallas_call(
        body,
        in_specs=[pl.BlockSpec(memory_space=pltpu.VMEM)] + [ANYWHERE] * len(chunks),
        out_shape=(out, out),
        scratch_shapes=landing(chunks),
        compiler_params=params(),
        cost_estimate=SMALL,
        name="pack",
    )(pick, *chunks)


def spread(place, mine, theirs, far_mine, far_theirs):
    length, slots_of = place.shape
    room, features = far_mine.shape
    size = length // TOGETHER
    parts = (mine, theirs, far_mine, far_theirs)

    def body(place_ref, *refs):
        outs = refs[len(parts) :]
        for at in range(0, features, 512):
            cols = slice(at, at + 512)
            rows = jnp.concatenate([ref[:, cols] for ref in refs[: len(parts)]], axis=0)
            dense = dot(place_ref[...], rows).astype(BF)
            for i, out in enumerate(outs):
                out[:, cols] = dense[i * size : (i + 1) * size]

    out = jax.ShapeDtypeStruct((size, features), BF)
    return pl.pallas_call(
        body,
        grid=(1,),
        in_specs=[whole(place)] + [pl.BlockSpec((room, features), lambda i: (0, 0))] * len(parts),
        out_specs=[whole(out)] * TOGETHER,
        out_shape=(out,) * TOGETHER,
        compiler_params=params(1),
        cost_estimate=SMALL,
        name="spread",
    )(place, *parts)


def split3(value):
    high = value.astype(BF)
    rest = value - high.astype(F32)
    mid = rest.astype(BF)
    low = (rest - mid.astype(F32)).astype(BF)
    return high, mid, low


def after(value, *earlier):
    return lax.optimization_barrier((value, *earlier))[0]


def dense_plan(tokens, route_ids, gate_probs, out_cot, w_gate, w_up, w_down):
    experts = lax.axis_size("expert")
    tok_rows, features = tokens.shape
    hidden = w_gate.shape[2]
    top_count = route_ids.shape[1]
    capacity = max(2, tok_rows * top_count * 4 // (3 * experts))
    expert = lax.axis_index("expert").astype(jnp.int32)
    replica = lax.axis_index("replica").astype(jnp.int32)
    w_gate, w_up, w_down = w_gate[0], w_up[0], w_down[0]

    def to_core(rows):
        return lax.ppermute(rows, "expert", [(i, i ^ 1) for i in range(experts)])

    def to_x(rows):
        return lax.ppermute(rows, "expert", [(i, i ^ 2) for i in range(experts)])

    def to_z(rows, step):
        return lax.ppermute(
            rows, "expert", [(i, (i + 4 * step) % experts) for i in range(experts)]
        )

    def to_y(rows):
        return lax.ppermute(rows, "replica", [(0, 1), (1, 0)])

    chosen = route_ids[:, :, None] == jnp.arange(experts, dtype=jnp.int32)
    share = jnp.sum(jnp.where(chosen, gate_probs[:, :, None], 0.0), axis=1)
    pad = jnp.zeros((tok_rows, LANES - 3 * experts), BF)

    cot_far, cot_relay = to_x(out_cot), to_y(out_cot)
    near = [jnp.concatenate([tokens, *split3(share), pad], axis=1)]
    far, relay = [to_x(near[0])], [to_y(near[0])]
    near.append(after(to_z(near[0], 1), cot_far))
    near.append(after(to_z(near[1], 1), far[0], cot_relay, relay[0]))
    far.append(to_x(near[1]))
    relay += [to_y(far[0]), to_y(near[1])]
    near.append(after(to_z(near[2], 1), relay[1], relay[2]))
    far += [to_x(near[2]), to_x(near[3])]
    cot_relay_far = to_y(cot_far)
    relay += [to_y(far[1]), to_y(near[2]), to_y(far[2]), to_y(near[3]), to_y(far[3])]
    token_sets = near + far
    token_other = [relay[0], relay[2], relay[4], relay[6], relay[1], relay[3], relay[5], relay[7]]
    ring = [to_z(after(out_cot, near[2]), 1)]
    ring.append(to_z(ring[0], 1))
    ring.append(to_z(ring[1], 1))
    cot_ring = jnp.concatenate(ring, axis=0)
    cot_far_ring, cot_relay_ring = to_x(cot_ring), to_y(cot_ring)
    cot_relay_far_ring = to_y(cot_far_ring)
    expert_index = expert
    expert = expert.reshape(1)

    def enter(chunks, before_plan, before_dots):
        mine, theirs, mine_lanes, theirs_lanes, pick, place = plan_and_pack(
            after(expert, *before_plan), experts, capacity, chunks
        )
        theirs = after(to_core(theirs), *before_dots)
        x = jnp.concatenate([mine, theirs], axis=0)
        shares = jnp.concatenate([mine_lanes, to_core(theirs_lanes)], axis=0)
        held = (jnp.arange(LANES) % experts == expert_index) & (jnp.arange(LANES) < 3 * experts)
        weight = jnp.sum(jnp.where(held, shares.astype(F32), 0.0), axis=1, keepdims=True)
        pre_gate, pre_up = dot(x, w_gate), dot(x, w_up)
        act = (jax.nn.silu(pre_gate) * pre_up).astype(BF)
        return x, weight, pick, place, pre_gate, pre_up, act

    def enter_cot(pick, pieces, weight, pre_gate, pre_up, *before_dots):
        mine, theirs = pack(pick, pieces)
        theirs = after(to_core(theirs), *before_dots)
        cot = jnp.concatenate([mine, theirs], axis=0)
        cot = (cot.astype(F32) * weight).astype(BF)
        return cot, *hidden_grads(cot, pre_gate, pre_up, w_down)

    def leave(rows_of):
        half = TOGETHER * capacity
        theirs = to_core(rows_of(slice(2 * half, None)))
        mine = rows_of(slice(0, 2 * half))
        return mine, theirs, to_x(mine[half:]), to_x(theirs[half:])

    def home(place, parts):
        own, *others = spread(place, *parts)
        return [own] + [to_z(a, -step) for step, a in enumerate(others, 1)]

    def total(chunks):
        return sum(a.astype(F32) for a in chunks).astype(BF)

    def grads(x, act, cot, d_gate, d_up):
        x = lax.dynamic_slice_in_dim(x, replica * (features // 2), features // 2, 1)
        act = lax.dynamic_slice_in_dim(act, replica * (hidden // 2), hidden // 2, 1)
        return outer_sum(x, d_gate), outer_sum(x, d_up), outer_sum(act, cot)

    own_x, weight, pick, place, pre_gate, pre_up, act = enter(
        token_sets, (cot_relay_far, relay[3], ring[1]), (relay[4],)
    )
    act = after(act, cot_ring)
    parts = leave(lambda rows: (dot(act[rows], w_down) * weight[rows]).astype(BF))
    chunks = home(after(place, relay[5]), parts)
    cot, d_gate, d_up = enter_cot(
        after(pick, chunks[0], relay[6], relay[7]),
        (out_cot, cot_ring, cot_far, cot_far_ring),
        weight, pre_gate, pre_up,
    )
    own_grads = cot, d_gate, d_up
    parts = leave(lambda rows: input_rows(d_gate[rows], d_up[rows], w_gate, w_up))

    x, weight, pick, _, pre_gate, pre_up, other_act = enter(
        token_other, (parts[0], cot_relay_ring, chunks[1]), (chunks[2],)
    )
    grad_chunks = home(after(place, other_act), parts)
    own_grads = after(own_grads, grad_chunks[0], chunks[3])
    own = grads(own_x, act, *own_grads)
    cot, d_gate, d_up = enter_cot(
        after(pick, *own, grad_chunks[1]),
        (cot_relay, cot_relay_ring, cot_relay_far, cot_relay_far_ring),
        weight, pre_gate, pre_up, grad_chunks[2],
    )
    other = grads(x, other_act, cot, d_gate, d_up)
    grad_gate, grad_up, grad_down = ((a + b).astype(BF)[None] for a, b in zip(own, other))
    return (total(chunks), total(grad_chunks), grad_gate, grad_up, grad_down)


def dense_fits(mesh):
    experts, replicas = mesh.shape["expert"], mesh.shape["replica"]
    return replicas == 2 and experts == 4 * TOGETHER


def solution(mesh):
    placed = (
        P(("expert", "replica"), None),
        P(("expert", "replica"), None),
        P(("expert", "replica"), None),
        P(("expert", "replica"), None),
        P("expert", None, None),
        P("expert", None, None),
        P("expert", None, None),
    )
    return jax.shard_map(
        dense_plan if dense_fits(mesh) else routed_plan,
        mesh=mesh,
        in_specs=placed,
        out_specs=(
            P(("expert", "replica"), None),
            P(("expert", "replica"), None),
            P("expert", "replica", None),
            P("expert", "replica", None),
            P("expert", "replica", None),
        ),
        check_vma=False,
    )
```

```python
import jax
import jax.numpy as jnp
from jax import lax
from jax.experimental import pallas as pl
from jax.experimental.pallas import tpu as pltpu
from jax.sharding import PartitionSpec as P

BF = jnp.bfloat16
F32 = jnp.float32
VMEM = 56 * 1024 * 1024
TOGETHER = 4
LANES = 128
SMALL = pl.CostEstimate(flops=1, bytes_accessed=1, transcendentals=0)


def slots(routes, experts, capacity):
    flat_ids = routes.reshape(-1)
    one_hot = (flat_ids[:, None] == jnp.arange(experts, dtype=jnp.int32)[None, :]).astype(jnp.int32)
    before = jnp.cumsum(one_hot, axis=0) - one_hot
    slot_rank = jnp.sum(before * one_hot, axis=1)
    return flat_ids * capacity + slot_rank


def place(token_rows, positions, total_rows):
    return (
        jnp.zeros((total_rows, token_rows.shape[1]), token_rows.dtype).at[positions].set(token_rows)
    )


def hidden_rows(token_rows, gate_weight, up_weight):
    pre_gate = jnp.dot(token_rows, gate_weight, preferred_element_type=F32)
    pre_up = jnp.dot(token_rows, up_weight, preferred_element_type=F32)
    activation = (jax.nn.silu(pre_gate) * pre_up).astype(BF)
    return (pre_gate, pre_up, activation)


CONTRACT = (((1,), (1,)), ((), ()))


def hidden_grads(grad_rows, pre_gate, pre_up, down_weight):
    d_hidden = lax.dot_general(grad_rows, down_weight, CONTRACT, preferred_element_type=F32)
    sigmoid_gate = jax.nn.sigmoid(pre_gate)
    d_gate = (d_hidden * pre_up * sigmoid_gate * (1.0 + pre_gate * (1.0 - sigmoid_gate))).astype(BF)
    d_up = (d_hidden * pre_gate * sigmoid_gate).astype(BF)
    return d_gate, d_up


def input_rows(d_gate, d_up, gate_weight, up_weight):
    back_rows = lax.dot_general(d_gate, gate_weight, CONTRACT, preferred_element_type=F32)
    back_rows = back_rows + lax.dot_general(d_up, up_weight, CONTRACT, preferred_element_type=F32)
    return back_rows.astype(BF)


def outer_sum(left, right):
    return lax.dot_general(left, right, (((0,), (0,)), ((), ())), preferred_element_type=F32)


def routed_plan(tokens, route_ids, gate_probs, out_cot, w_gate, w_up, w_down):
    experts = lax.axis_size("expert")
    tok_rows, features = tokens.shape
    top_count = route_ids.shape[1]
    hidden = w_gate.shape[2]
    capacity = max(2, tok_rows * top_count * 4 // (3 * experts))
    total_rows = experts * capacity
    positions = slots(route_ids, experts, capacity)
    gate_weight, up_weight, down_weight = w_gate[0], w_up[0], w_down[0]

    def exchange(rows):
        blocks = rows.reshape(experts, capacity, features)
        return lax.all_to_all(blocks, "expert", 0, 0, tiled=True).reshape(-1, features)

    received = exchange(place(jnp.repeat(tokens, top_count, axis=0), positions, total_rows))
    pre_gate, pre_up, activation = hidden_rows(received, gate_weight, up_weight)
    result = jnp.dot(activation, down_weight, preferred_element_type=F32).astype(BF)
    picked = exchange(result)[positions].reshape(tok_rows, top_count, features)
    combined = jnp.einsum("tk,tkd->td", gate_probs, picked.astype(F32)).astype(BF)
    scaled = (gate_probs[:, :, None] * out_cot[:, None, :].astype(F32)).astype(BF)
    grads_in = exchange(place(scaled.reshape(-1, features), positions, total_rows))
    d_gate, d_up = hidden_grads(grads_in, pre_gate, pre_up, down_weight)
    back = exchange(input_rows(d_gate, d_up, gate_weight, up_weight))
    grad_tokens = jnp.sum(
        back[positions].reshape(tok_rows, top_count, features).astype(F32), axis=1
    ).astype(BF)
    gate_up_sum = lax.psum_scatter(
        outer_sum(received, jnp.concatenate([d_gate, d_up], axis=1)).astype(BF),
        "replica",
        scatter_dimension=0,
        tiled=True,
    )
    down_sum = lax.psum_scatter(
        outer_sum(activation, grads_in).astype(BF), "replica", scatter_dimension=0, tiled=True
    )
    return (
        combined,
        grad_tokens,
        gate_up_sum[:, :hidden][None],
        gate_up_sum[:, hidden:][None],
        down_sum[None],
    )

def dot(left, right):
    return jnp.dot(left, right, preferred_element_type=F32)


def whole(array):
    return pl.BlockSpec(array.shape, lambda *_: (0,) * array.ndim)


def params(steps=0):
    order = ("arbitrary",) * steps if steps else None
    return pltpu.CompilerParams(dimension_semantics=order, vmem_limit_bytes=VMEM)


ANYWHERE = pl.BlockSpec(memory_space=pl.ANY)


def landing(pieces):
    rows = sum(a.shape[0] for a in pieces)
    return [
        pltpu.VMEM((rows, pieces[0].shape[1]), BF),
        pltpu.SemaphoreType.DMA((len(pieces),)),
    ]


def load(piece_refs, rows_ref, sems):
    copies, at = [], 0
    for i, ref in enumerate(piece_refs):
        size = ref.shape[0]
        copies.append(pltpu.make_async_copy(ref, rows_ref.at[at : at + size], sems.at[i]))
        copies[-1].start()
        at += size
    return copies


def plan_and_pack(expert, experts, capacity, chunks):
    tok_rows, width = chunks[0].shape
    features = width - LANES
    groups, each = 2, len(chunks) // 2
    length, room = TOGETHER * tok_rows, TOGETHER * capacity

    def body(expert_ref, *refs):
        outs = refs[len(chunks) :]
        mine_ref, theirs_ref, mine_lanes, theirs_lanes, pick_ref, place_ref = outs[:6]
        rows_ref, sems = outs[6:]
        copies = load(refs[: len(chunks)], rows_ref, sems)
        lane = lax.broadcasted_iota(jnp.int32, (length, LANES), 1)
        row = lax.broadcasted_iota(jnp.int32, (length, length), 0)
        col = lax.broadcasted_iota(jnp.int32, (length, length), 1)
        before = (row >= col).astype(BF)
        slot = lax.broadcasted_iota(jnp.int32, (length, 2 * room), 1) % room
        wanted = (slot + 1).astype(F32)

        def places(shares, first):
            routed = []
            for index in (first, first ^ 1):
                held = (lane == index) | (lane == index + experts) | (lane == index + 2 * experts)
                weight = jnp.sum(jnp.where(held, shares, 0.0), axis=1, keepdims=True)
                routed.append(jnp.broadcast_to((weight > 0).astype(F32), (length, room)))
            routed = jnp.concatenate(routed, axis=1)
            rank = dot(before, routed.astype(BF))
            return jnp.where((rank == wanted) & (routed > 0), 1.0, 0.0)

        for group in range(groups):
            for copy in copies[group * each : (group + 1) * each]:
                copy.wait()
            held_rows = slice(group * length, (group + 1) * length)
            lanes = rows_ref[held_rows, features:]
            place = places(lanes.astype(F32), expert_ref[0])
            if group == 0:
                place_ref[:, : 2 * room] = place.astype(BF)
                place_ref[:, 2 * room :] = places(lanes.astype(F32), expert_ref[0] ^ 2).astype(BF)
            pick = place.T.astype(BF)
            pick_ref[group] = pick
            here = slice(group * room, (group + 1) * room)
            packed = dot(pick, lanes).astype(BF)
            mine_lanes[here] = packed[:room]
            theirs_lanes[here] = packed[room:]
            for at in range(0, features, 512):
                cols = slice(at, at + 512)
                packed = dot(pick, rows_ref[held_rows, cols]).astype(BF)
                mine_ref[here, cols] = packed[:room]
                theirs_ref[here, cols] = packed[room:]

    rows = jax.ShapeDtypeStruct((groups * room, features), BF)
    lanes = jax.ShapeDtypeStruct((groups * room, LANES), BF)
    pick = jax.ShapeDtypeStruct((groups, 2 * room, length), BF)
    place = jax.ShapeDtypeStruct((length, 4 * room), BF)
    outs = (rows, rows, lanes, lanes, pick, place)
    return pl.pallas_call(
        body,
        grid_spec=pltpu.PrefetchScalarGridSpec(
            num_scalar_prefetch=1,
            grid=(1,),
            in_specs=[ANYWHERE] * len(chunks),
            out_specs=[whole(a) for a in outs],
            scratch_shapes=landing(chunks),
        ),
        out_shape=outs,
        compiler_params=params(1),
        cost_estimate=SMALL,
        name="plan_and_pack",
    )(expert, *chunks)


def pack(pick, chunks):
    features = chunks[0].shape[1]
    groups, room, length = pick.shape[0], pick.shape[1] // 2, pick.shape[2]
    each = len(chunks) // groups

    def body(pick_ref, *refs):
        mine_ref, theirs_ref, rows_ref, sems = refs[len(chunks) :]
        copies = load(refs[: len(chunks)], rows_ref, sems)
        for group in range(groups):
            for copy in copies[group * each : (group + 1) * each]:
                copy.wait()
            held_rows = slice(group * length, (group + 1) * length)
            here = slice(group * room, (group + 1) * room)
            for at in range(0, features, 512):
                cols = slice(at, at + 512)
                packed = dot(pick_ref[group], rows_ref[held_rows, cols]).astype(BF)
                mine_ref[here, cols] = packed[:room]
                theirs_ref[here, cols] = packed[room:]

    out = jax.ShapeDtypeStruct((groups * room, features), BF)
    return pl.pallas_call(
        body,
        in_specs=[pl.BlockSpec(memory_space=pltpu.VMEM)] + [ANYWHERE] * len(chunks),
        out_shape=(out, out),
        scratch_shapes=landing(chunks),
        compiler_params=params(),
        cost_estimate=SMALL,
        name="pack",
    )(pick, *chunks)


def spread(place, mine, theirs, far_mine, far_theirs):
    length, slots_of = place.shape
    room, features = far_mine.shape
    size = length // TOGETHER
    parts = (mine, theirs, far_mine, far_theirs)

    def body(place_ref, *refs):
        outs = refs[len(parts) :]
        for at in range(0, features, 512):
            cols = slice(at, at + 512)
            rows = jnp.concatenate([ref[:, cols] for ref in refs[: len(parts)]], axis=0)
            dense = dot(place_ref[...], rows).astype(BF)
            for i, out in enumerate(outs):
                out[:, cols] = dense[i * size : (i + 1) * size]

    out = jax.ShapeDtypeStruct((size, features), BF)
    return pl.pallas_call(
        body,
        grid=(1,),
        in_specs=[whole(place)] + [pl.BlockSpec((room, features), lambda i: (0, 0))] * len(parts),
        out_specs=[whole(out)] * TOGETHER,
        out_shape=(out,) * TOGETHER,
        compiler_params=params(1),
        cost_estimate=SMALL,
        name="spread",
    )(place, *parts)


def split3(value):
    high = value.astype(BF)
    rest = value - high.astype(F32)
    mid = rest.astype(BF)
    low = (rest - mid.astype(F32)).astype(BF)
    return high, mid, low


def after(value, *earlier):
    return lax.optimization_barrier((value, *earlier))[0]


def dense_plan(tokens, route_ids, gate_probs, out_cot, w_gate, w_up, w_down):
    experts = lax.axis_size("expert")
    tok_rows, features = tokens.shape
    hidden = w_gate.shape[2]
    top_count = route_ids.shape[1]
    capacity = max(2, tok_rows * top_count * 4 // (3 * experts))
    expert = lax.axis_index("expert").astype(jnp.int32)
    replica = lax.axis_index("replica").astype(jnp.int32)
    w_gate, w_up, w_down = w_gate[0], w_up[0], w_down[0]

    def to_core(rows):
        return lax.ppermute(rows, "expert", [(i, i ^ 1) for i in range(experts)])

    def to_x(rows):
        return lax.ppermute(rows, "expert", [(i, i ^ 2) for i in range(experts)])

    def to_z(rows, step):
        return lax.ppermute(
            rows, "expert", [(i, (i + 4 * step) % experts) for i in range(experts)]
        )

    def to_y(rows):
        return lax.ppermute(rows, "replica", [(0, 1), (1, 0)])

    chosen = route_ids[:, :, None] == jnp.arange(experts, dtype=jnp.int32)
    share = jnp.sum(jnp.where(chosen, gate_probs[:, :, None], 0.0), axis=1)
    pad = jnp.zeros((tok_rows, LANES - 3 * experts), BF)

    cot_far, cot_relay = [to_x(out_cot)], to_y(out_cot)
    near = [jnp.concatenate([tokens, *split3(share), pad], axis=1)]
    near.append(after(to_z(near[0], 1), cot_far[0]))
    near.append(to_z(near[1], 1))
    near.append(to_z(near[2], 1))
    far = [to_x(a) for a in near]
    relay = [to_y(a) for pair in zip(near, far) for a in pair]
    token_sets = near + far
    token_other = relay[0::2] + relay[1::2]
    cot_near = [out_cot, to_z(after(out_cot, near[2]), 1)]
    cot_near.append(to_z(cot_near[1], 1))
    cot_near.append(to_z(cot_near[2], 1))
    cot_far += [to_x(a) for a in cot_near[1:]]
    cot_sets = cot_near + cot_far
    cot_relay_far = to_y(cot_far[0])
    cot_relay_ring = to_y(jnp.concatenate(cot_near[1:], axis=0))
    cot_relay_far_ring = to_y(jnp.concatenate(cot_far[1:], axis=0))
    expert_index = expert
    expert = expert.reshape(1)

    def enter(chunks, before_plan, before_dots):
        mine, theirs, mine_lanes, theirs_lanes, pick, place = plan_and_pack(
            after(expert, *before_plan), experts, capacity, chunks
        )
        theirs = after(to_core(theirs), *before_dots)
        x = jnp.concatenate([mine, theirs], axis=0)
        shares = jnp.concatenate([mine_lanes, to_core(theirs_lanes)], axis=0)
        held = (jnp.arange(LANES) % experts == expert_index) & (jnp.arange(LANES) < 3 * experts)
        weight = jnp.sum(jnp.where(held, shares.astype(F32), 0.0), axis=1, keepdims=True)
        pre_gate, pre_up = dot(x, w_gate), dot(x, w_up)
        act = (jax.nn.silu(pre_gate) * pre_up).astype(BF)
        return x, weight, pick, place, pre_gate, pre_up, act

    def enter_cot(pick, pieces, weight, pre_gate, pre_up, *before_dots):
        mine, theirs = pack(pick, pieces)
        theirs = after(to_core(theirs), *before_dots)
        cot = jnp.concatenate([mine, theirs], axis=0)
        cot = (cot.astype(F32) * weight).astype(BF)
        return cot, *hidden_grads(cot, pre_gate, pre_up, w_down)

    def leave(rows_of):
        half = TOGETHER * capacity
        theirs = to_core(rows_of(slice(2 * half, None)))
        mine = rows_of(slice(0, 2 * half))
        return mine, theirs, to_x(mine[half:]), to_x(theirs[half:])

    def home(place, parts):
        own, *others = spread(place, *parts)
        return [own] + [to_z(a, -step) for step, a in enumerate(others, 1)]

    def total(chunks):
        return sum(a.astype(F32) for a in chunks).astype(BF)

    def grads(x, act, cot, d_gate, d_up):
        x = lax.dynamic_slice_in_dim(x, replica * (features // 2), features // 2, 1)
        act = lax.dynamic_slice_in_dim(act, replica * (hidden // 2), hidden // 2, 1)
        return outer_sum(x, d_gate), outer_sum(x, d_up), outer_sum(act, cot)

    own_x, weight, pick, place, pre_gate, pre_up, act = enter(
        token_sets,
        (cot_relay, cot_relay_far, *relay[:4], *cot_near[1:3], cot_far[1]),
        (relay[4], cot_far[2]),
    )
    act = after(act, cot_near[3], relay[5])
    parts = leave(lambda rows: (dot(act[rows], w_down) * weight[rows]).astype(BF))
    cot, d_gate, d_up = enter_cot(
        after(pick, parts[0], relay[6]), cot_sets, weight, pre_gate, pre_up, relay[7]
    )
    own_grads = cot, d_gate, d_up
    d_gate, d_up = after((d_gate, d_up), parts[2], cot_relay_ring)
    grad_parts = leave(lambda rows: input_rows(d_gate[rows], d_up[rows], w_gate, w_up))
    chunks = home(after(place, grad_parts[0]), parts)
    parts = grad_parts

    x, weight, pick, _, pre_gate, pre_up, other_act = enter(
        token_other, (chunks[0], parts[1]), (parts[2], cot_relay_far_ring)
    )
    grad_chunks = home(after(place, other_act, *chunks[1:]), parts)
    own_grads = after(own_grads, grad_chunks[0])
    own = grads(own_x, act, *own_grads)
    cot, d_gate, d_up = enter_cot(
        after(pick, *own, grad_chunks[1]),
        (cot_relay, cot_relay_ring, cot_relay_far, cot_relay_far_ring),
        weight, pre_gate, pre_up, grad_chunks[2],
    )
    other = grads(x, other_act, cot, d_gate, d_up)
    grad_gate, grad_up, grad_down = ((a + b).astype(BF)[None] for a, b in zip(own, other))
    return (total(chunks), total(grad_chunks), grad_gate, grad_up, grad_down)


def dense_fits(mesh):
    experts, replicas = mesh.shape["expert"], mesh.shape["replica"]
    return replicas == 2 and experts == 4 * TOGETHER


def solution(mesh):
    placed = (
        P(("expert", "replica"), None),
        P(("expert", "replica"), None),
        P(("expert", "replica"), None),
        P(("expert", "replica"), None),
        P("expert", None, None),
        P("expert", None, None),
        P("expert", None, None),
    )
    return jax.shard_map(
        dense_plan if dense_fits(mesh) else routed_plan,
        mesh=mesh,
        in_specs=placed,
        out_specs=(
            P(("expert", "replica"), None),
            P(("expert", "replica"), None),
            P("expert", "replica", None),
            P("expert", "replica", None),
            P("expert", "replica", None),
        ),
        check_vma=False,
    )
```

```python
import jax
import jax.numpy as jnp
from jax import lax
from jax.experimental import pallas as pl
from jax.experimental.pallas import tpu as pltpu
from jax.sharding import PartitionSpec as P

BF = jnp.bfloat16
F32 = jnp.float32
VMEM = 56 * 1024 * 1024
TOGETHER = 4
LANES = 128
SMALL = pl.CostEstimate(flops=1, bytes_accessed=1, transcendentals=0)


def slots(routes, experts, capacity):
    flat_ids = routes.reshape(-1)
    one_hot = (flat_ids[:, None] == jnp.arange(experts, dtype=jnp.int32)[None, :]).astype(jnp.int32)
    before = jnp.cumsum(one_hot, axis=0) - one_hot
    slot_rank = jnp.sum(before * one_hot, axis=1)
    return flat_ids * capacity + slot_rank


def place(token_rows, positions, total_rows):
    return (
        jnp.zeros((total_rows, token_rows.shape[1]), token_rows.dtype).at[positions].set(token_rows)
    )


def hidden_rows(token_rows, gate_weight, up_weight):
    pre_gate = jnp.dot(token_rows, gate_weight, preferred_element_type=F32)
    pre_up = jnp.dot(token_rows, up_weight, preferred_element_type=F32)
    activation = (jax.nn.silu(pre_gate) * pre_up).astype(BF)
    return (pre_gate, pre_up, activation)


CONTRACT = (((1,), (1,)), ((), ()))


def hidden_grads(grad_rows, pre_gate, pre_up, down_weight):
    d_hidden = lax.dot_general(grad_rows, down_weight, CONTRACT, preferred_element_type=F32)
    sigmoid_gate = jax.nn.sigmoid(pre_gate)
    d_gate = (d_hidden * pre_up * sigmoid_gate * (1.0 + pre_gate * (1.0 - sigmoid_gate))).astype(BF)
    d_up = (d_hidden * pre_gate * sigmoid_gate).astype(BF)
    return d_gate, d_up


def input_rows(d_gate, d_up, gate_weight, up_weight):
    back_rows = lax.dot_general(d_gate, gate_weight, CONTRACT, preferred_element_type=F32)
    back_rows = back_rows + lax.dot_general(d_up, up_weight, CONTRACT, preferred_element_type=F32)
    return back_rows.astype(BF)


def outer_sum(left, right):
    return lax.dot_general(left, right, (((0,), (0,)), ((), ())), preferred_element_type=F32)


def routed_plan(tokens, route_ids, gate_probs, out_cot, w_gate, w_up, w_down):
    experts = lax.axis_size("expert")
    tok_rows, features = tokens.shape
    top_count = route_ids.shape[1]
    hidden = w_gate.shape[2]
    capacity = max(2, tok_rows * top_count * 4 // (3 * experts))
    total_rows = experts * capacity
    positions = slots(route_ids, experts, capacity)
    gate_weight, up_weight, down_weight = w_gate[0], w_up[0], w_down[0]

    def exchange(rows):
        blocks = rows.reshape(experts, capacity, features)
        return lax.all_to_all(blocks, "expert", 0, 0, tiled=True).reshape(-1, features)

    received = exchange(place(jnp.repeat(tokens, top_count, axis=0), positions, total_rows))
    pre_gate, pre_up, activation = hidden_rows(received, gate_weight, up_weight)
    result = jnp.dot(activation, down_weight, preferred_element_type=F32).astype(BF)
    picked = exchange(result)[positions].reshape(tok_rows, top_count, features)
    combined = jnp.einsum("tk,tkd->td", gate_probs, picked.astype(F32)).astype(BF)
    scaled = (gate_probs[:, :, None] * out_cot[:, None, :].astype(F32)).astype(BF)
    grads_in = exchange(place(scaled.reshape(-1, features), positions, total_rows))
    d_gate, d_up = hidden_grads(grads_in, pre_gate, pre_up, down_weight)
    back = exchange(input_rows(d_gate, d_up, gate_weight, up_weight))
    grad_tokens = jnp.sum(
        back[positions].reshape(tok_rows, top_count, features).astype(F32), axis=1
    ).astype(BF)
    gate_up_sum = lax.psum_scatter(
        outer_sum(received, jnp.concatenate([d_gate, d_up], axis=1)).astype(BF),
        "replica",
        scatter_dimension=0,
        tiled=True,
    )
    down_sum = lax.psum_scatter(
        outer_sum(activation, grads_in).astype(BF), "replica", scatter_dimension=0, tiled=True
    )
    return (
        combined,
        grad_tokens,
        gate_up_sum[:, :hidden][None],
        gate_up_sum[:, hidden:][None],
        down_sum[None],
    )

def dot(left, right):
    return jnp.dot(left, right, preferred_element_type=F32)


def whole(array):
    return pl.BlockSpec(array.shape, lambda *_: (0,) * array.ndim)


def params(steps=0):
    order = ("arbitrary",) * steps if steps else None
    return pltpu.CompilerParams(dimension_semantics=order, vmem_limit_bytes=VMEM)


ANYWHERE = pl.BlockSpec(memory_space=pl.ANY)


def landing(pieces):
    rows = sum(a.shape[0] for a in pieces)
    return [
        pltpu.VMEM((rows, pieces[0].shape[1]), BF),
        pltpu.SemaphoreType.DMA((len(pieces),)),
    ]


def load(piece_refs, rows_ref, sems):
    copies, at = [], 0
    for i, ref in enumerate(piece_refs):
        size = ref.shape[0]
        copies.append(pltpu.make_async_copy(ref, rows_ref.at[at : at + size], sems.at[i]))
        copies[-1].start()
        at += size
    return copies


def plan_and_pack(expert, experts, capacity, chunks):
    tok_rows, width = chunks[0].shape
    features = width - LANES
    groups, each = 2, len(chunks) // 2
    length, room = TOGETHER * tok_rows, TOGETHER * capacity

    def body(expert_ref, *refs):
        outs = refs[len(chunks) :]
        mine_ref, theirs_ref, mine_lanes, theirs_lanes, pick_ref, place_ref = outs[:6]
        rows_ref, sems = outs[6:]
        copies = load(refs[: len(chunks)], rows_ref, sems)
        lane = lax.broadcasted_iota(jnp.int32, (length, LANES), 1)
        row = lax.broadcasted_iota(jnp.int32, (length, length), 0)
        col = lax.broadcasted_iota(jnp.int32, (length, length), 1)
        before = (row >= col).astype(BF)
        slot = lax.broadcasted_iota(jnp.int32, (length, 2 * room), 1) % room
        wanted = (slot + 1).astype(F32)

        def places(shares, first):
            routed = []
            for index in (first, first ^ 1):
                held = (lane == index) | (lane == index + experts) | (lane == index + 2 * experts)
                weight = jnp.sum(jnp.where(held, shares, 0.0), axis=1, keepdims=True)
                routed.append(jnp.broadcast_to((weight > 0).astype(F32), (length, room)))
            routed = jnp.concatenate(routed, axis=1)
            rank = dot(before, routed.astype(BF))
            return jnp.where((rank == wanted) & (routed > 0), 1.0, 0.0)

        for group in range(groups):
            for copy in copies[group * each : (group + 1) * each]:
                copy.wait()
            held_rows = slice(group * length, (group + 1) * length)
            lanes = rows_ref[held_rows, features:]
            place = places(lanes.astype(F32), expert_ref[0])
            if group == 0:
                place_ref[:, : 2 * room] = place.astype(BF)
                place_ref[:, 2 * room :] = places(lanes.astype(F32), expert_ref[0] ^ 2).astype(BF)
            pick = place.T.astype(BF)
            pick_ref[group] = pick
            here = slice(group * room, (group + 1) * room)
            packed = dot(pick, lanes).astype(BF)
            mine_lanes[here] = packed[:room]
            theirs_lanes[here] = packed[room:]
            for at in range(0, features, 512):
                cols = slice(at, at + 512)
                packed = dot(pick, rows_ref[held_rows, cols]).astype(BF)
                mine_ref[here, cols] = packed[:room]
                theirs_ref[here, cols] = packed[room:]

    rows = jax.ShapeDtypeStruct((groups * room, features), BF)
    lanes = jax.ShapeDtypeStruct((groups * room, LANES), BF)
    pick = jax.ShapeDtypeStruct((groups, 2 * room, length), BF)
    place = jax.ShapeDtypeStruct((length, 4 * room), BF)
    outs = (rows, rows, lanes, lanes, pick, place)
    return pl.pallas_call(
        body,
        grid_spec=pltpu.PrefetchScalarGridSpec(
            num_scalar_prefetch=1,
            grid=(1,),
            in_specs=[ANYWHERE] * len(chunks),
            out_specs=[whole(a) for a in outs],
            scratch_shapes=landing(chunks),
        ),
        out_shape=outs,
        compiler_params=params(1),
        cost_estimate=SMALL,
        name="plan_and_pack",
    )(expert, *chunks)


def pack(pick, chunks):
    features = chunks[0].shape[1]
    groups, room, length = pick.shape[0], pick.shape[1] // 2, pick.shape[2]
    each = len(chunks) // groups

    def body(pick_ref, *refs):
        mine_ref, theirs_ref, rows_ref, sems = refs[len(chunks) :]
        copies = load(refs[: len(chunks)], rows_ref, sems)
        for group in range(groups):
            for copy in copies[group * each : (group + 1) * each]:
                copy.wait()
            held_rows = slice(group * length, (group + 1) * length)
            here = slice(group * room, (group + 1) * room)
            for at in range(0, features, 512):
                cols = slice(at, at + 512)
                packed = dot(pick_ref[group], rows_ref[held_rows, cols]).astype(BF)
                mine_ref[here, cols] = packed[:room]
                theirs_ref[here, cols] = packed[room:]

    out = jax.ShapeDtypeStruct((groups * room, features), BF)
    return pl.pallas_call(
        body,
        in_specs=[pl.BlockSpec(memory_space=pltpu.VMEM)] + [ANYWHERE] * len(chunks),
        out_shape=(out, out),
        scratch_shapes=landing(chunks),
        compiler_params=params(),
        cost_estimate=SMALL,
        name="pack",
    )(pick, *chunks)


def spread(place, mine, theirs, far_mine, far_theirs):
    length, slots_of = place.shape
    room, features = far_mine.shape
    size = length // TOGETHER
    parts = (mine, theirs, far_mine, far_theirs)

    def body(place_ref, *refs):
        outs = refs[len(parts) :]
        for at in range(0, features, 512):
            cols = slice(at, at + 512)
            rows = jnp.concatenate([ref[:, cols] for ref in refs[: len(parts)]], axis=0)
            dense = dot(place_ref[...], rows).astype(BF)
            for i, out in enumerate(outs):
                out[:, cols] = dense[i * size : (i + 1) * size]

    out = jax.ShapeDtypeStruct((size, features), BF)
    return pl.pallas_call(
        body,
        grid=(1,),
        in_specs=[whole(place)] + [pl.BlockSpec((room, features), lambda i: (0, 0))] * len(parts),
        out_specs=[whole(out)] * TOGETHER,
        out_shape=(out,) * TOGETHER,
        compiler_params=params(1),
        cost_estimate=SMALL,
        name="spread",
    )(place, *parts)


def split3(value):
    high = value.astype(BF)
    rest = value - high.astype(F32)
    mid = rest.astype(BF)
    low = (rest - mid.astype(F32)).astype(BF)
    return high, mid, low


def after(value, *earlier):
    return lax.optimization_barrier((value, *earlier))[0]


def dense_plan(tokens, route_ids, gate_probs, out_cot, w_gate, w_up, w_down):
    experts = lax.axis_size("expert")
    tok_rows, features = tokens.shape
    hidden = w_gate.shape[2]
    top_count = route_ids.shape[1]
    capacity = max(2, tok_rows * top_count * 4 // (3 * experts))
    expert = lax.axis_index("expert").astype(jnp.int32)
    replica = lax.axis_index("replica").astype(jnp.int32)
    w_gate, w_up, w_down = w_gate[0], w_up[0], w_down[0]

    def to_core(rows):
        return lax.ppermute(rows, "expert", [(i, i ^ 1) for i in range(experts)])

    def to_x(rows):
        return lax.ppermute(rows, "expert", [(i, i ^ 2) for i in range(experts)])

    def to_z(rows, step):
        return lax.ppermute(
            rows, "expert", [(i, (i + 4 * step) % experts) for i in range(experts)]
        )

    def to_y(rows):
        return lax.ppermute(rows, "replica", [(0, 1), (1, 0)])

    chosen = route_ids[:, :, None] == jnp.arange(experts, dtype=jnp.int32)
    share = jnp.sum(jnp.where(chosen, gate_probs[:, :, None], 0.0), axis=1)
    pad = jnp.zeros((tok_rows, LANES - 3 * experts), BF)

    cot_far, cot_relay = [to_x(out_cot)], to_y(out_cot)
    near = [jnp.concatenate([tokens, *split3(share), pad], axis=1)]
    near.append(after(to_z(near[0], 1), cot_far[0]))
    near.append(to_z(near[1], 1))
    near.append(to_z(near[2], 1))
    far = [to_x(a) for a in near]
    relay = [to_y(a) for pair in zip(near, far) for a in pair]
    token_sets = near + far
    token_other = relay[0::2] + relay[1::2]
    cot_near = [out_cot, to_z(after(out_cot, near[2]), 1)]
    cot_near.append(to_z(cot_near[1], 1))
    cot_near.append(to_z(cot_near[2], 1))
    cot_far += [to_x(a) for a in cot_near[1:]]
    cot_sets = cot_near + cot_far
    cot_relay_far = to_y(cot_far[0])
    cot_relay_ring = to_y(jnp.concatenate(cot_near[1:], axis=0))
    cot_relay_far_ring = to_y(jnp.concatenate(cot_far[1:], axis=0))
    expert_index = expert
    expert = expert.reshape(1)

    def enter(chunks, before_plan, before_dots):
        mine, theirs, mine_lanes, theirs_lanes, pick, place = plan_and_pack(
            after(expert, *before_plan), experts, capacity, chunks
        )
        theirs = after(to_core(theirs), *before_dots)
        x = jnp.concatenate([mine, theirs], axis=0)
        shares = jnp.concatenate([mine_lanes, to_core(theirs_lanes)], axis=0)
        held = (jnp.arange(LANES) % experts == expert_index) & (jnp.arange(LANES) < 3 * experts)
        weight = jnp.sum(jnp.where(held, shares.astype(F32), 0.0), axis=1, keepdims=True)
        pre_gate, pre_up = dot(x, w_gate), dot(x, w_up)
        act = (jax.nn.silu(pre_gate) * pre_up).astype(BF)
        return x, weight, pick, place, pre_gate, pre_up, act

    def enter_cot(pick, pieces, weight, pre_gate, pre_up, *before_dots):
        mine, theirs = pack(pick, pieces)
        theirs = after(to_core(theirs), *before_dots)
        cot = jnp.concatenate([mine, theirs], axis=0)
        cot = (cot.astype(F32) * weight).astype(BF)
        return cot, *hidden_grads(cot, pre_gate, pre_up, w_down)

    def leave(rows_of):
        half = TOGETHER * capacity
        theirs = to_core(rows_of(slice(2 * half, None)))
        mine = rows_of(slice(0, 2 * half))
        return mine, theirs, to_x(mine[half:]), to_x(theirs[half:])

    def home(place, parts):
        own, *others = spread(place, *parts)
        return [own] + [to_z(a, -step) for step, a in enumerate(others, 1)]

    def total(chunks):
        return sum(a.astype(F32) for a in chunks).astype(BF)

    def grads(x, act, cot, d_gate, d_up):
        x = lax.dynamic_slice_in_dim(x, replica * (features // 2), features // 2, 1)
        act = lax.dynamic_slice_in_dim(act, replica * (hidden // 2), hidden // 2, 1)
        return outer_sum(x, d_gate), outer_sum(x, d_up), outer_sum(act, cot)

    own_x, weight, pick, place, pre_gate, pre_up, act = enter(
        token_sets,
        (*relay[:3], cot_relay, cot_near[1]),
        (relay[3], cot_relay_far, cot_near[2], cot_far[1]),
    )
    act = after(act, relay[4], cot_near[3], cot_far[2])
    parts = leave(lambda rows: (dot(act[rows], w_down) * weight[rows]).astype(BF))
    cot, d_gate, d_up = enter_cot(
        after(pick, parts[0], parts[1], relay[5]), cot_sets, weight, pre_gate, pre_up, relay[6]
    )
    own_grads = cot, d_gate, d_up
    d_gate, d_up = after((d_gate, d_up), parts[2], relay[7])
    grad_parts = leave(lambda rows: input_rows(d_gate[rows], d_up[rows], w_gate, w_up))
    chunks = home(after(place, grad_parts[0]), parts)

    x, weight, pick, _, pre_gate, pre_up, other_act = enter(
        token_other, (chunks[0], *grad_parts[1:3]), (grad_parts[3], cot_relay_ring)
    )
    grad_chunks = home(after(place, other_act, *chunks[1:]), grad_parts)
    own_grads = after(own_grads, grad_chunks[0])
    own = grads(own_x, act, *own_grads)
    cot, d_gate, d_up = enter_cot(
        after(pick, *own, grad_chunks[1]),
        (cot_relay, cot_relay_ring, cot_relay_far, cot_relay_far_ring),
        weight, pre_gate, pre_up,
    )
    other = grads(x, other_act, cot, d_gate, d_up)
    grad_gate, grad_up, grad_down = ((a + b).astype(BF)[None] for a, b in zip(own, other))
    return (total(chunks), total(grad_chunks), grad_gate, grad_up, grad_down)


def dense_fits(mesh):
    experts, replicas = mesh.shape["expert"], mesh.shape["replica"]
    return replicas == 2 and experts == 4 * TOGETHER


def solution(mesh):
    placed = (
        P(("expert", "replica"), None),
        P(("expert", "replica"), None),
        P(("expert", "replica"), None),
        P(("expert", "replica"), None),
        P("expert", None, None),
        P("expert", None, None),
        P("expert", None, None),
    )
    return jax.shard_map(
        dense_plan if dense_fits(mesh) else routed_plan,
        mesh=mesh,
        in_specs=placed,
        out_specs=(
            P(("expert", "replica"), None),
            P(("expert", "replica"), None),
            P("expert", "replica", None),
            P("expert", "replica", None),
            P("expert", "replica", None),
        ),
        check_vma=False,
    )
```

```python
import jax
import jax.numpy as jnp
from jax import lax
from jax.experimental import pallas as pl
from jax.experimental.pallas import tpu as pltpu
from jax.sharding import PartitionSpec as P

BF = jnp.bfloat16
F32 = jnp.float32
VMEM = 56 * 1024 * 1024
TOGETHER = 4
LANES = 128
SMALL = pl.CostEstimate(flops=1, bytes_accessed=1, transcendentals=0)


def slots(routes, experts, capacity):
    flat_ids = routes.reshape(-1)
    one_hot = (flat_ids[:, None] == jnp.arange(experts, dtype=jnp.int32)[None, :]).astype(jnp.int32)
    before = jnp.cumsum(one_hot, axis=0) - one_hot
    slot_rank = jnp.sum(before * one_hot, axis=1)
    return flat_ids * capacity + slot_rank


def place(token_rows, positions, total_rows):
    return (
        jnp.zeros((total_rows, token_rows.shape[1]), token_rows.dtype).at[positions].set(token_rows)
    )


def hidden_rows(token_rows, gate_weight, up_weight):
    pre_gate = jnp.dot(token_rows, gate_weight, preferred_element_type=F32)
    pre_up = jnp.dot(token_rows, up_weight, preferred_element_type=F32)
    activation = (jax.nn.silu(pre_gate) * pre_up).astype(BF)
    return (pre_gate, pre_up, activation)


CONTRACT = (((1,), (1,)), ((), ()))


def hidden_grads(grad_rows, pre_gate, pre_up, down_weight):
    d_hidden = lax.dot_general(grad_rows, down_weight, CONTRACT, preferred_element_type=F32)
    sigmoid_gate = jax.nn.sigmoid(pre_gate)
    d_gate = (d_hidden * pre_up * sigmoid_gate * (1.0 + pre_gate * (1.0 - sigmoid_gate))).astype(BF)
    d_up = (d_hidden * pre_gate * sigmoid_gate).astype(BF)
    return d_gate, d_up


def input_rows(d_gate, d_up, gate_weight, up_weight):
    back_rows = lax.dot_general(d_gate, gate_weight, CONTRACT, preferred_element_type=F32)
    back_rows = back_rows + lax.dot_general(d_up, up_weight, CONTRACT, preferred_element_type=F32)
    return back_rows.astype(BF)


def outer_sum(left, right):
    return lax.dot_general(left, right, (((0,), (0,)), ((), ())), preferred_element_type=F32)


def routed_plan(tokens, route_ids, gate_probs, out_cot, w_gate, w_up, w_down):
    experts = lax.axis_size("expert")
    tok_rows, features = tokens.shape
    top_count = route_ids.shape[1]
    hidden = w_gate.shape[2]
    capacity = max(2, tok_rows * top_count * 4 // (3 * experts))
    total_rows = experts * capacity
    positions = slots(route_ids, experts, capacity)
    gate_weight, up_weight, down_weight = w_gate[0], w_up[0], w_down[0]

    def exchange(rows):
        blocks = rows.reshape(experts, capacity, features)
        return lax.all_to_all(blocks, "expert", 0, 0, tiled=True).reshape(-1, features)

    received = exchange(place(jnp.repeat(tokens, top_count, axis=0), positions, total_rows))
    pre_gate, pre_up, activation = hidden_rows(received, gate_weight, up_weight)
    result = jnp.dot(activation, down_weight, preferred_element_type=F32).astype(BF)
    picked = exchange(result)[positions].reshape(tok_rows, top_count, features)
    combined = jnp.einsum("tk,tkd->td", gate_probs, picked.astype(F32)).astype(BF)
    scaled = (gate_probs[:, :, None] * out_cot[:, None, :].astype(F32)).astype(BF)
    grads_in = exchange(place(scaled.reshape(-1, features), positions, total_rows))
    d_gate, d_up = hidden_grads(grads_in, pre_gate, pre_up, down_weight)
    back = exchange(input_rows(d_gate, d_up, gate_weight, up_weight))
    grad_tokens = jnp.sum(
        back[positions].reshape(tok_rows, top_count, features).astype(F32), axis=1
    ).astype(BF)
    gate_up_sum = lax.psum_scatter(
        outer_sum(received, jnp.concatenate([d_gate, d_up], axis=1)).astype(BF),
        "replica",
        scatter_dimension=0,
        tiled=True,
    )
    down_sum = lax.psum_scatter(
        outer_sum(activation, grads_in).astype(BF), "replica", scatter_dimension=0, tiled=True
    )
    return (
        combined,
        grad_tokens,
        gate_up_sum[:, :hidden][None],
        gate_up_sum[:, hidden:][None],
        down_sum[None],
    )

def dot(left, right):
    return jnp.dot(left, right, preferred_element_type=F32)


def whole(array):
    return pl.BlockSpec(array.shape, lambda *_: (0,) * array.ndim)


def params(steps=0):
    order = ("arbitrary",) * steps if steps else None
    return pltpu.CompilerParams(dimension_semantics=order, vmem_limit_bytes=VMEM)


ANYWHERE = pl.BlockSpec(memory_space=pl.ANY)


def plan_and_pack(expert, experts, capacity, tok_rows, pieces):
    arrays = []
    for array, _ in pieces:
        if not any(array is a for a in arrays):
            arrays.append(array)
    sources = [
        (next(k for k, a in enumerate(arrays) if a is array), chunk) for array, chunk in pieces
    ]
    width = arrays[0].shape[1]
    features = (width - LANES) // 2
    groups, each = 2, len(pieces) // 2
    length, room = TOGETHER * tok_rows, TOGETHER * capacity

    def body(expert_ref, *refs):
        outs = refs[len(arrays) :]
        token_mine, token_theirs, cot_mine, cot_theirs, lane_mine, lane_theirs = outs[:6]
        place_ref, rows_ref, sems = outs[6:]
        copies = []
        for i, (source, chunk) in enumerate(sources):
            copies.append(
                pltpu.make_async_copy(
                    refs[source].at[chunk * tok_rows : (chunk + 1) * tok_rows],
                    rows_ref.at[i * tok_rows : (i + 1) * tok_rows],
                    sems.at[i],
                )
            )
            copies[-1].start()
        lane = lax.broadcasted_iota(jnp.int32, (length, LANES), 1)
        row = lax.broadcasted_iota(jnp.int32, (length, length), 0)
        col = lax.broadcasted_iota(jnp.int32, (length, length), 1)
        before = (row >= col).astype(BF)
        slot = lax.broadcasted_iota(jnp.int32, (length, 2 * room), 1) % room
        wanted = (slot + 1).astype(F32)

        def places(shares, first):
            routed = []
            for index in (first, first ^ 1):
                held = (lane == index) | (lane == index + experts) | (lane == index + 2 * experts)
                weight = jnp.sum(jnp.where(held, shares, 0.0), axis=1, keepdims=True)
                routed.append(jnp.broadcast_to((weight > 0).astype(F32), (length, room)))
            routed = jnp.concatenate(routed, axis=1)
            rank = dot(before, routed.astype(BF))
            return jnp.where((rank == wanted) & (routed > 0), 1.0, 0.0)

        for group in range(groups):
            for copy in copies[group * each : (group + 1) * each]:
                copy.wait()
            held_rows = slice(group * length, (group + 1) * length)
            lanes = rows_ref[held_rows, 2 * features :]
            place = places(lanes.astype(F32), expert_ref[0])
            if group == 0:
                place_ref[:, : 2 * room] = place.astype(BF)
                place_ref[:, 2 * room :] = places(lanes.astype(F32), expert_ref[0] ^ 2).astype(BF)
            pick = place.T.astype(BF)
            here = slice(group * room, (group + 1) * room)
            packed = dot(pick, lanes).astype(BF)
            lane_mine[here] = packed[:room]
            lane_theirs[here] = packed[room:]
            for at in range(0, 2 * features, 512):
                packed = dot(pick, rows_ref[held_rows, at : at + 512]).astype(BF)
                mine, theirs = (
                    (token_mine, token_theirs) if at < features else (cot_mine, cot_theirs)
                )
                cols = slice(at % features, at % features + 512)
                mine[here, cols] = packed[:room]
                theirs[here, cols] = packed[room:]

    rows = jax.ShapeDtypeStruct((groups * room, features), BF)
    lanes = jax.ShapeDtypeStruct((groups * room, LANES), BF)
    place = jax.ShapeDtypeStruct((length, 4 * room), BF)
    outs = (rows, rows, rows, rows, lanes, lanes, place)
    return pl.pallas_call(
        body,
        grid_spec=pltpu.PrefetchScalarGridSpec(
            num_scalar_prefetch=1,
            grid=(1,),
            in_specs=[ANYWHERE] * len(arrays),
            out_specs=[whole(a) for a in outs],
            scratch_shapes=[
                pltpu.VMEM((groups * length, width), BF),
                pltpu.SemaphoreType.DMA((len(pieces),)),
            ],
        ),
        out_shape=outs,
        compiler_params=params(1),
        cost_estimate=SMALL,
        name="plan_and_pack",
    )(expert, *arrays)


def spread(place, mine, theirs, far_mine, far_theirs):
    length, slots_of = place.shape
    room, features = far_mine.shape
    size = length // TOGETHER
    parts = (mine, theirs, far_mine, far_theirs)

    def body(place_ref, *refs):
        outs = refs[len(parts) :]
        for at in range(0, features, 512):
            cols = slice(at, at + 512)
            rows = jnp.concatenate([ref[:, cols] for ref in refs[: len(parts)]], axis=0)
            dense = dot(place_ref[...], rows).astype(BF)
            for i, out in enumerate(outs):
                out[:, cols] = dense[i * size : (i + 1) * size]

    out = jax.ShapeDtypeStruct((size, features), BF)
    return pl.pallas_call(
        body,
        grid=(1,),
        in_specs=[whole(place)] + [pl.BlockSpec((room, features), lambda i: (0, 0))] * len(parts),
        out_specs=[whole(out)] * TOGETHER,
        out_shape=(out,) * TOGETHER,
        compiler_params=params(1),
        cost_estimate=SMALL,
        name="spread",
    )(place, *parts)


def split3(value):
    high = value.astype(BF)
    rest = value - high.astype(F32)
    mid = rest.astype(BF)
    low = (rest - mid.astype(F32)).astype(BF)
    return high, mid, low


def after(value, *earlier):
    return lax.optimization_barrier((value, *earlier))[0]


def dense_plan(tokens, route_ids, gate_probs, out_cot, w_gate, w_up, w_down):
    experts = lax.axis_size("expert")
    tok_rows, features = tokens.shape
    hidden = w_gate.shape[2]
    top_count = route_ids.shape[1]
    capacity = max(2, tok_rows * top_count * 4 // (3 * experts))
    expert = lax.axis_index("expert").astype(jnp.int32)
    replica = lax.axis_index("replica").astype(jnp.int32)
    w_gate, w_up, w_down = w_gate[0], w_up[0], w_down[0]

    def to_core(rows):
        return lax.ppermute(rows, "expert", [(i, i ^ 1) for i in range(experts)])

    def to_x(rows):
        return lax.ppermute(rows, "expert", [(i, i ^ 2) for i in range(experts)])

    def to_z(rows, step):
        return lax.ppermute(
            rows, "expert", [(i, (i + 4 * step) % experts) for i in range(experts)]
        )

    def to_y(rows):
        return lax.ppermute(rows, "replica", [(0, 1), (1, 0)])

    chosen = route_ids[:, :, None] == jnp.arange(experts, dtype=jnp.int32)
    share = jnp.sum(jnp.where(chosen, gate_probs[:, :, None], 0.0), axis=1)
    pad = jnp.zeros((tok_rows, LANES - 3 * experts), BF)

    near = [jnp.concatenate([tokens, out_cot, *split3(share), pad], axis=1)]
    far, relay = [to_x(near[0])], [to_y(near[0])]
    near.append(to_z(near[0], 1))
    far.append(to_x(near[1]))
    near.append(after(to_z(near[1], 1), far[0], relay[0]))
    far.append(to_x(near[2]))
    near.append(to_z(near[2], 1))
    far.append(to_x(near[3]))
    relay += [to_y(far[0]), to_y(near[1]), to_y(far[1])]
    joined = jnp.concatenate([near[2], near[3], far[2], far[3]], axis=0)
    last = to_y(joined)
    own_pieces = [(a, 0) for a in near + far]
    other_pieces = [(relay[0], 0), (relay[2], 0), (last, 0), (last, 1)]
    other_pieces += [(relay[1], 0), (relay[3], 0), (last, 2), (last, 3)]
    expert_index = expert
    expert = expert.reshape(1)

    def enter(pieces, *earlier):
        mine, theirs, cot_mine, cot_theirs, mine_lanes, theirs_lanes, place = plan_and_pack(
            after(expert, *earlier), experts, capacity, tok_rows, pieces
        )
        x = jnp.concatenate([mine, to_core(theirs)], axis=0)
        shares = jnp.concatenate([mine_lanes, to_core(theirs_lanes)], axis=0)
        held = (jnp.arange(LANES) % experts == expert_index) & (jnp.arange(LANES) < 3 * experts)
        weight = jnp.sum(jnp.where(held, shares.astype(F32), 0.0), axis=1, keepdims=True)
        cot = jnp.concatenate([cot_mine, to_core(cot_theirs)], axis=0)
        cot = (cot.astype(F32) * weight).astype(BF)
        pre_gate, pre_up = dot(x, w_gate), dot(x, w_up)
        act = (jax.nn.silu(pre_gate) * pre_up).astype(BF)
        return x, weight, place, pre_gate, pre_up, act, cot

    def leave(rows_of):
        half = TOGETHER * capacity
        theirs = to_core(rows_of(slice(2 * half, None)))
        mine = rows_of(slice(0, 2 * half))
        return mine, theirs, to_x(mine[half:]), to_x(theirs[half:])

    def home(place, parts):
        own, *others = spread(place, *parts)
        return [own] + [to_z(a, -step) for step, a in enumerate(others, 1)]

    def total(chunks):
        return sum(a.astype(F32) for a in chunks).astype(BF)

    def grads(x, act, cot, d_gate, d_up):
        x = lax.dynamic_slice_in_dim(x, replica * (features // 2), features // 2, 1)
        act = lax.dynamic_slice_in_dim(act, replica * (hidden // 2), hidden // 2, 1)
        return outer_sum(x, d_gate), outer_sum(x, d_up), outer_sum(act, cot)

    own_x, weight, place, pre_gate, pre_up, act, cot = enter(own_pieces, *relay[1:4], joined)
    parts = leave(lambda rows: (dot(act[rows], w_down) * weight[rows]).astype(BF))
    cot = after(cot, parts[0], parts[1])
    own_grads = cot, *hidden_grads(cot, pre_gate, pre_up, w_down)
    d_gate, d_up = after(own_grads[1:], parts[2])
    grad_parts = leave(lambda rows: input_rows(d_gate[rows], d_up[rows], w_gate, w_up))
    chunks = home(after(place, grad_parts[0], grad_parts[1]), parts)
    own_grads = after(own_grads[0], grad_parts[2]), *after(own_grads[1:], chunks[0])
    own = grads(own_x, act, *own_grads)
    grad_chunks = home(after(place, *own), grad_parts)

    x, weight, _, pre_gate, pre_up, act, cot = enter(other_pieces, grad_chunks[0], *chunks[1:])
    cot = after(cot, act, grad_chunks[1], grad_chunks[2])
    d_gate, d_up = hidden_grads(cot, pre_gate, pre_up, w_down)
    other = grads(x, act, cot, d_gate, d_up)
    grad_gate, grad_up, grad_down = ((a + b).astype(BF)[None] for a, b in zip(own, other))
    return (total(chunks), total(grad_chunks), grad_gate, grad_up, grad_down)


def dense_fits(mesh):
    experts, replicas = mesh.shape["expert"], mesh.shape["replica"]
    return replicas == 2 and experts == 4 * TOGETHER


def solution(mesh):
    placed = (
        P(("expert", "replica"), None),
        P(("expert", "replica"), None),
        P(("expert", "replica"), None),
        P(("expert", "replica"), None),
        P("expert", None, None),
        P("expert", None, None),
        P("expert", None, None),
    )
    return jax.shard_map(
        dense_plan if dense_fits(mesh) else routed_plan,
        mesh=mesh,
        in_specs=placed,
        out_specs=(
            P(("expert", "replica"), None),
            P(("expert", "replica"), None),
            P("expert", "replica", None),
            P("expert", "replica", None),
            P("expert", "replica", None),
        ),
        check_vma=False,
    )
```

```python
import jax
import jax.numpy as jnp
from jax import lax
from jax.experimental import pallas as pl
from jax.experimental.pallas import tpu as pltpu
from jax.sharding import PartitionSpec as P

BF = jnp.bfloat16
F32 = jnp.float32
VMEM = 56 * 1024 * 1024
TOGETHER = 4
LANES = 128
SMALL = pl.CostEstimate(flops=1, bytes_accessed=1, transcendentals=0)


def slots(routes, experts, capacity):
    flat_ids = routes.reshape(-1)
    one_hot = (flat_ids[:, None] == jnp.arange(experts, dtype=jnp.int32)[None, :]).astype(jnp.int32)
    before = jnp.cumsum(one_hot, axis=0) - one_hot
    slot_rank = jnp.sum(before * one_hot, axis=1)
    return flat_ids * capacity + slot_rank


def place(token_rows, positions, total_rows):
    return (
        jnp.zeros((total_rows, token_rows.shape[1]), token_rows.dtype).at[positions].set(token_rows)
    )


def hidden_rows(token_rows, gate_weight, up_weight):
    pre_gate = jnp.dot(token_rows, gate_weight, preferred_element_type=F32)
    pre_up = jnp.dot(token_rows, up_weight, preferred_element_type=F32)
    activation = (jax.nn.silu(pre_gate) * pre_up).astype(BF)
    return (pre_gate, pre_up, activation)


CONTRACT = (((1,), (1,)), ((), ()))


def hidden_grads(grad_rows, pre_gate, pre_up, down_weight):
    d_hidden = lax.dot_general(grad_rows, down_weight, CONTRACT, preferred_element_type=F32)
    sigmoid_gate = jax.nn.sigmoid(pre_gate)
    d_gate = (d_hidden * pre_up * sigmoid_gate * (1.0 + pre_gate * (1.0 - sigmoid_gate))).astype(BF)
    d_up = (d_hidden * pre_gate * sigmoid_gate).astype(BF)
    return d_gate, d_up


def input_rows(d_gate, d_up, gate_weight, up_weight):
    back_rows = lax.dot_general(d_gate, gate_weight, CONTRACT, preferred_element_type=F32)
    back_rows = back_rows + lax.dot_general(d_up, up_weight, CONTRACT, preferred_element_type=F32)
    return back_rows.astype(BF)


def outer_sum(left, right):
    return lax.dot_general(left, right, (((0,), (0,)), ((), ())), preferred_element_type=F32)


def routed_plan(tokens, route_ids, gate_probs, out_cot, w_gate, w_up, w_down):
    experts = lax.axis_size("expert")
    tok_rows, features = tokens.shape
    top_count = route_ids.shape[1]
    hidden = w_gate.shape[2]
    capacity = max(2, tok_rows * top_count * 4 // (3 * experts))
    total_rows = experts * capacity
    positions = slots(route_ids, experts, capacity)
    gate_weight, up_weight, down_weight = w_gate[0], w_up[0], w_down[0]

    def exchange(rows):
        blocks = rows.reshape(experts, capacity, features)
        return lax.all_to_all(blocks, "expert", 0, 0, tiled=True).reshape(-1, features)

    received = exchange(place(jnp.repeat(tokens, top_count, axis=0), positions, total_rows))
    pre_gate, pre_up, activation = hidden_rows(received, gate_weight, up_weight)
    result = jnp.dot(activation, down_weight, preferred_element_type=F32).astype(BF)
    picked = exchange(result)[positions].reshape(tok_rows, top_count, features)
    combined = jnp.einsum("tk,tkd->td", gate_probs, picked.astype(F32)).astype(BF)
    scaled = (gate_probs[:, :, None] * out_cot[:, None, :].astype(F32)).astype(BF)
    grads_in = exchange(place(scaled.reshape(-1, features), positions, total_rows))
    d_gate, d_up = hidden_grads(grads_in, pre_gate, pre_up, down_weight)
    back = exchange(input_rows(d_gate, d_up, gate_weight, up_weight))
    grad_tokens = jnp.sum(
        back[positions].reshape(tok_rows, top_count, features).astype(F32), axis=1
    ).astype(BF)
    gate_up_sum = lax.psum_scatter(
        outer_sum(received, jnp.concatenate([d_gate, d_up], axis=1)).astype(BF),
        "replica",
        scatter_dimension=0,
        tiled=True,
    )
    down_sum = lax.psum_scatter(
        outer_sum(activation, grads_in).astype(BF), "replica", scatter_dimension=0, tiled=True
    )
    return (
        combined,
        grad_tokens,
        gate_up_sum[:, :hidden][None],
        gate_up_sum[:, hidden:][None],
        down_sum[None],
    )

def dot(left, right):
    return jnp.dot(left, right, preferred_element_type=F32)


def whole(array):
    return pl.BlockSpec(array.shape, lambda *_: (0,) * array.ndim)


def params(steps=0):
    order = ("arbitrary",) * steps if steps else None
    return pltpu.CompilerParams(dimension_semantics=order, vmem_limit_bytes=VMEM)


ANYWHERE = pl.BlockSpec(memory_space=pl.ANY)


def plan_and_pack(expert, experts, capacity, tok_rows, pieces):
    arrays = []
    for array, _ in pieces:
        if not any(array is a for a in arrays):
            arrays.append(array)
    sources = [
        (next(k for k, a in enumerate(arrays) if a is array), chunk) for array, chunk in pieces
    ]
    width = arrays[0].shape[1]
    features = (width - LANES) // 2
    groups, each = 2, len(pieces) // 2
    length, room = TOGETHER * tok_rows, TOGETHER * capacity

    def body(expert_ref, *refs):
        outs = refs[len(arrays) :]
        token_mine, cot_mine, lane_mine, theirs_ref, place_ref, rows_ref, sems = outs
        copies = []
        for i, (source, chunk) in enumerate(sources):
            copies.append(
                pltpu.make_async_copy(
                    refs[source].at[chunk * tok_rows : (chunk + 1) * tok_rows],
                    rows_ref.at[i * tok_rows : (i + 1) * tok_rows],
                    sems.at[i],
                )
            )
            copies[-1].start()
        lane = lax.broadcasted_iota(jnp.int32, (length, LANES), 1)
        row = lax.broadcasted_iota(jnp.int32, (length, length), 0)
        col = lax.broadcasted_iota(jnp.int32, (length, length), 1)
        before = (row >= col).astype(BF)
        slot = lax.broadcasted_iota(jnp.int32, (length, 2 * room), 1) % room
        wanted = (slot + 1).astype(F32)

        def places(shares, first):
            routed = []
            for index in (first, first ^ 1):
                held = (lane == index) | (lane == index + experts) | (lane == index + 2 * experts)
                weight = jnp.sum(jnp.where(held, shares, 0.0), axis=1, keepdims=True)
                routed.append(jnp.broadcast_to((weight > 0).astype(F32), (length, room)))
            routed = jnp.concatenate(routed, axis=1)
            rank = dot(before, routed.astype(BF))
            return jnp.where((rank == wanted) & (routed > 0), 1.0, 0.0)

        for group in range(groups):
            for copy in copies[group * each : (group + 1) * each]:
                copy.wait()
            held_rows = slice(group * length, (group + 1) * length)
            lanes = rows_ref[held_rows, 2 * features :]
            place = places(lanes.astype(F32), expert_ref[0])
            if group == 0:
                place_ref[:, : 2 * room] = place.astype(BF)
                place_ref[:, 2 * room :] = places(lanes.astype(F32), expert_ref[0] ^ 2).astype(BF)
            pick = place.T.astype(BF)
            here = slice(group * room, (group + 1) * room)
            packed = dot(pick, lanes).astype(BF)
            lane_mine[here] = packed[:room]
            theirs_ref[here, 2 * features :] = packed[room:]
            for at in range(0, 2 * features, 512):
                packed = dot(pick, rows_ref[held_rows, at : at + 512]).astype(BF)
                mine_ref = token_mine if at < features else cot_mine
                mine_ref[here, at % features : at % features + 512] = packed[:room]
                theirs_ref[here, at : at + 512] = packed[room:]

    rows = jax.ShapeDtypeStruct((groups * room, features), BF)
    lanes = jax.ShapeDtypeStruct((groups * room, LANES), BF)
    theirs = jax.ShapeDtypeStruct((groups * room, width), BF)
    place = jax.ShapeDtypeStruct((length, 4 * room), BF)
    outs = (rows, rows, lanes, theirs, place)
    return pl.pallas_call(
        body,
        grid_spec=pltpu.PrefetchScalarGridSpec(
            num_scalar_prefetch=1,
            grid=(1,),
            in_specs=[ANYWHERE] * len(arrays),
            out_specs=[whole(a) for a in outs],
            scratch_shapes=[
                pltpu.VMEM((groups * length, width), BF),
                pltpu.SemaphoreType.DMA((len(pieces),)),
            ],
        ),
        out_shape=outs,
        compiler_params=params(1),
        cost_estimate=SMALL,
        name="plan_and_pack",
    )(expert, *arrays)


def spread(place, mine, theirs, far_mine, far_theirs):
    length, slots_of = place.shape
    room, features = far_mine.shape
    size = length // TOGETHER
    parts = (mine, theirs, far_mine, far_theirs)

    def body(place_ref, *refs):
        outs = refs[len(parts) :]
        for at in range(0, features, 512):
            cols = slice(at, at + 512)
            rows = jnp.concatenate([ref[:, cols] for ref in refs[: len(parts)]], axis=0)
            dense = dot(place_ref[...], rows).astype(BF)
            for i, out in enumerate(outs):
                out[:, cols] = dense[i * size : (i + 1) * size]

    out = jax.ShapeDtypeStruct((size, features), BF)
    return pl.pallas_call(
        body,
        grid=(1,),
        in_specs=[whole(place)] + [pl.BlockSpec((room, features), lambda i: (0, 0))] * len(parts),
        out_specs=[whole(out)] * TOGETHER,
        out_shape=(out,) * TOGETHER,
        compiler_params=params(1),
        cost_estimate=SMALL,
        name="spread",
    )(place, *parts)


def split3(value):
    high = value.astype(BF)
    rest = value - high.astype(F32)
    mid = rest.astype(BF)
    low = (rest - mid.astype(F32)).astype(BF)
    return high, mid, low


def after(value, *earlier):
    return lax.optimization_barrier((value, *earlier))[0]


def dense_plan(tokens, route_ids, gate_probs, out_cot, w_gate, w_up, w_down):
    experts = lax.axis_size("expert")
    tok_rows, features = tokens.shape
    hidden = w_gate.shape[2]
    top_count = route_ids.shape[1]
    capacity = max(2, tok_rows * top_count * 4 // (3 * experts))
    expert = lax.axis_index("expert").astype(jnp.int32)
    replica = lax.axis_index("replica").astype(jnp.int32)
    w_gate, w_up, w_down = w_gate[0], w_up[0], w_down[0]

    def to_core(rows):
        return lax.ppermute(rows, "expert", [(i, i ^ 1) for i in range(experts)])

    def to_x(rows):
        return lax.ppermute(rows, "expert", [(i, i ^ 2) for i in range(experts)])

    def to_z(rows, step):
        return lax.ppermute(
            rows, "expert", [(i, (i + 4 * step) % experts) for i in range(experts)]
        )

    def to_y(rows):
        return lax.ppermute(rows, "replica", [(0, 1), (1, 0)])

    chosen = route_ids[:, :, None] == jnp.arange(experts, dtype=jnp.int32)
    share = jnp.sum(jnp.where(chosen, gate_probs[:, :, None], 0.0), axis=1)
    pad = jnp.zeros((tok_rows, LANES - 3 * experts), BF)

    near = [jnp.concatenate([tokens, out_cot, *split3(share), pad], axis=1)]
    far, relay = [to_x(near[0])], [to_y(near[0])]
    near.append(to_z(near[0], 1))
    far.append(to_x(near[1]))
    near.append(after(to_z(near[1], 1), far[0], relay[0]))
    far.append(to_x(near[2]))
    near.append(to_z(near[2], 1))
    far.append(to_x(near[3]))
    relay += [to_y(far[0]), to_y(near[1]), to_y(far[1]), to_y(near[2])]
    joined = jnp.concatenate([near[3], far[2], far[3]], axis=0)
    last = to_y(joined)
    own_pieces = [(a, 0) for a in near + far]
    other_pieces = [(relay[0], 0), (relay[2], 0), (relay[4], 0), (last, 0)]
    other_pieces += [(relay[1], 0), (relay[3], 0), (last, 1), (last, 2)]
    expert_index = expert
    expert = expert.reshape(1)

    def plan(pieces, *earlier):
        return plan_and_pack(after(expert, *earlier), experts, capacity, tok_rows, pieces)

    def enter(packed):
        mine, cot_mine, mine_lanes, theirs, _ = packed
        theirs = to_core(theirs)
        x = jnp.concatenate([mine, theirs[:, :features]], axis=0)
        shares = jnp.concatenate([mine_lanes, theirs[:, 2 * features :]], axis=0)
        held = (jnp.arange(LANES) % experts == expert_index) & (jnp.arange(LANES) < 3 * experts)
        weight = jnp.sum(jnp.where(held, shares.astype(F32), 0.0), axis=1, keepdims=True)
        cot = jnp.concatenate([cot_mine, theirs[:, features : 2 * features]], axis=0)
        cot = (cot.astype(F32) * weight).astype(BF)
        pre_gate, pre_up = dot(x, w_gate), dot(x, w_up)
        act = (jax.nn.silu(pre_gate) * pre_up).astype(BF)
        return x, weight, pre_gate, pre_up, act, cot

    def leave(rows_of, *before_mine):
        half = TOGETHER * capacity
        theirs = to_core(rows_of(slice(2 * half, None)))
        mine = rows_of(slice(0, 2 * half), *before_mine)
        return mine, theirs, to_x(mine[half:]), to_x(theirs[half:])

    def home(place, parts):
        own, *others = spread(place, *parts)
        return [own] + [to_z(a, -step) for step, a in enumerate(others, 1)]

    def total(chunks):
        return sum(a.astype(F32) for a in chunks).astype(BF)

    def grads(x, act, cot, d_gate, d_up):
        x = lax.dynamic_slice_in_dim(x, replica * (features // 2), features // 2, 1)
        act = lax.dynamic_slice_in_dim(act, replica * (hidden // 2), hidden // 2, 1)
        return outer_sum(x, d_gate), outer_sum(x, d_up), outer_sum(act, cot)

    packed = plan(own_pieces, *relay[1:5], joined)
    place = packed[-1]
    own_x, weight, pre_gate, pre_up, act, cot = enter(packed)
    parts = leave(lambda rows: (dot(act[rows], w_down) * weight[rows]).astype(BF))
    cot = after(cot, parts[0], parts[1])
    d_gate, d_up = hidden_grads(cot, pre_gate, pre_up, w_down)

    def token_grads(rows, *earlier):
        return input_rows(*after((d_gate[rows], d_up[rows]), *earlier), w_gate, w_up)

    grad_parts = leave(token_grads, parts[2])
    chunks = home(after(place, grad_parts[0], grad_parts[1]), parts)
    own_grads = after((cot, d_gate, d_up), chunks[0], last)
    own = grads(own_x, act, after(own_grads[0], chunks[1]), *own_grads[1:])
    packed = list(plan(other_pieces, *own, grad_parts[2]))
    packed[0] = after(packed[0], grad_parts[3])
    x, weight, pre_gate, pre_up, act, cot = enter(packed)
    grad_chunks = home(after(place, act, *chunks[1:]), grad_parts)
    cot = after(cot, grad_chunks[0])
    d_gate, d_up = hidden_grads(cot, pre_gate, pre_up, w_down)
    other = grads(x, act, cot, d_gate, after(d_up, grad_chunks[1]))
    grad_gate, grad_up, grad_down = ((a + b).astype(BF)[None] for a, b in zip(own, other))
    return (total(chunks), total(grad_chunks), grad_gate, grad_up, grad_down)


def dense_fits(mesh):
    experts, replicas = mesh.shape["expert"], mesh.shape["replica"]
    return replicas == 2 and experts == 4 * TOGETHER


def solution(mesh):
    placed = (
        P(("expert", "replica"), None),
        P(("expert", "replica"), None),
        P(("expert", "replica"), None),
        P(("expert", "replica"), None),
        P("expert", None, None),
        P("expert", None, None),
        P("expert", None, None),
    )
    return jax.shard_map(
        dense_plan if dense_fits(mesh) else routed_plan,
        mesh=mesh,
        in_specs=placed,
        out_specs=(
            P(("expert", "replica"), None),
            P(("expert", "replica"), None),
            P("expert", "replica", None),
            P("expert", "replica", None),
            P("expert", "replica", None),
        ),
        check_vma=False,
    )
```

```python
import jax
import jax.numpy as jnp
from jax import lax
from jax.experimental import pallas as pl
from jax.experimental.pallas import tpu as pltpu
from jax.sharding import PartitionSpec as P

BF = jnp.bfloat16
F32 = jnp.float32
VMEM = 56 * 1024 * 1024
TOGETHER = 4
LANES = 128
SMALL = pl.CostEstimate(flops=1, bytes_accessed=1, transcendentals=0)


def slots(routes, experts, capacity):
    flat_ids = routes.reshape(-1)
    one_hot = (flat_ids[:, None] == jnp.arange(experts, dtype=jnp.int32)[None, :]).astype(jnp.int32)
    before = jnp.cumsum(one_hot, axis=0) - one_hot
    slot_rank = jnp.sum(before * one_hot, axis=1)
    return flat_ids * capacity + slot_rank


def place(token_rows, positions, total_rows):
    return (
        jnp.zeros((total_rows, token_rows.shape[1]), token_rows.dtype).at[positions].set(token_rows)
    )


def hidden_rows(token_rows, gate_weight, up_weight):
    pre_gate = jnp.dot(token_rows, gate_weight, preferred_element_type=F32)
    pre_up = jnp.dot(token_rows, up_weight, preferred_element_type=F32)
    activation = (jax.nn.silu(pre_gate) * pre_up).astype(BF)
    return (pre_gate, pre_up, activation)


CONTRACT = (((1,), (1,)), ((), ()))


def hidden_grads(grad_rows, pre_gate, pre_up, down_weight):
    d_hidden = lax.dot_general(grad_rows, down_weight, CONTRACT, preferred_element_type=F32)
    sigmoid_gate = jax.nn.sigmoid(pre_gate)
    d_gate = (d_hidden * pre_up * sigmoid_gate * (1.0 + pre_gate * (1.0 - sigmoid_gate))).astype(BF)
    d_up = (d_hidden * pre_gate * sigmoid_gate).astype(BF)
    return d_gate, d_up


def input_rows(d_gate, d_up, gate_weight, up_weight):
    back_rows = lax.dot_general(d_gate, gate_weight, CONTRACT, preferred_element_type=F32)
    back_rows = back_rows + lax.dot_general(d_up, up_weight, CONTRACT, preferred_element_type=F32)
    return back_rows.astype(BF)


def outer_sum(left, right):
    return lax.dot_general(left, right, (((0,), (0,)), ((), ())), preferred_element_type=F32)


def routed_plan(tokens, route_ids, gate_probs, out_cot, w_gate, w_up, w_down):
    experts = lax.axis_size("expert")
    tok_rows, features = tokens.shape
    top_count = route_ids.shape[1]
    hidden = w_gate.shape[2]
    capacity = max(2, tok_rows * top_count * 4 // (3 * experts))
    total_rows = experts * capacity
    positions = slots(route_ids, experts, capacity)
    gate_weight, up_weight, down_weight = w_gate[0], w_up[0], w_down[0]

    def exchange(rows):
        blocks = rows.reshape(experts, capacity, features)
        return lax.all_to_all(blocks, "expert", 0, 0, tiled=True).reshape(-1, features)

    received = exchange(place(jnp.repeat(tokens, top_count, axis=0), positions, total_rows))
    pre_gate, pre_up, activation = hidden_rows(received, gate_weight, up_weight)
    result = jnp.dot(activation, down_weight, preferred_element_type=F32).astype(BF)
    picked = exchange(result)[positions].reshape(tok_rows, top_count, features)
    combined = jnp.einsum("tk,tkd->td", gate_probs, picked.astype(F32)).astype(BF)
    scaled = (gate_probs[:, :, None] * out_cot[:, None, :].astype(F32)).astype(BF)
    grads_in = exchange(place(scaled.reshape(-1, features), positions, total_rows))
    d_gate, d_up = hidden_grads(grads_in, pre_gate, pre_up, down_weight)
    back = exchange(input_rows(d_gate, d_up, gate_weight, up_weight))
    grad_tokens = jnp.sum(
        back[positions].reshape(tok_rows, top_count, features).astype(F32), axis=1
    ).astype(BF)
    gate_up_sum = lax.psum_scatter(
        outer_sum(received, jnp.concatenate([d_gate, d_up], axis=1)).astype(BF),
        "replica",
        scatter_dimension=0,
        tiled=True,
    )
    down_sum = lax.psum_scatter(
        outer_sum(activation, grads_in).astype(BF), "replica", scatter_dimension=0, tiled=True
    )
    return (
        combined,
        grad_tokens,
        gate_up_sum[:, :hidden][None],
        gate_up_sum[:, hidden:][None],
        down_sum[None],
    )

def dot(left, right):
    return jnp.dot(left, right, preferred_element_type=F32)


def whole(array):
    return pl.BlockSpec(array.shape, lambda *_: (0,) * array.ndim)


def params(steps=0):
    order = ("arbitrary",) * steps if steps else None
    return pltpu.CompilerParams(dimension_semantics=order, vmem_limit_bytes=VMEM)


ANYWHERE = pl.BlockSpec(memory_space=pl.ANY)


def plan_and_pack(expert, experts, capacity, tok_rows, pieces):
    arrays = []
    for array, _ in pieces:
        if not any(array is a for a in arrays):
            arrays.append(array)
    sources = [
        (next(k for k, a in enumerate(arrays) if a is array), chunk) for array, chunk in pieces
    ]
    width = arrays[0].shape[1]
    features = (width - LANES) // 2
    groups, each = 2, len(pieces) // 2
    length, room = TOGETHER * tok_rows, TOGETHER * capacity

    def body(expert_ref, *refs):
        outs = refs[len(arrays) :]
        token_mine, cot_mine, lane_mine, theirs_ref, place_ref, rows_ref, sems = outs
        copies = []
        for i, (source, chunk) in enumerate(sources):
            copies.append(
                pltpu.make_async_copy(
                    refs[source].at[chunk * tok_rows : (chunk + 1) * tok_rows],
                    rows_ref.at[i * tok_rows : (i + 1) * tok_rows],
                    sems.at[i],
                )
            )
            copies[-1].start()
        lane = lax.broadcasted_iota(jnp.int32, (length, LANES), 1)
        row = lax.broadcasted_iota(jnp.int32, (length, length), 0)
        col = lax.broadcasted_iota(jnp.int32, (length, length), 1)
        before = (row >= col).astype(BF)
        slot = lax.broadcasted_iota(jnp.int32, (length, 2 * room), 1) % room
        wanted = (slot + 1).astype(F32)

        def places(shares, first):
            routed = []
            for index in (first, first ^ 1):
                held = (lane == index) | (lane == index + experts) | (lane == index + 2 * experts)
                weight = jnp.sum(jnp.where(held, shares, 0.0), axis=1, keepdims=True)
                routed.append(jnp.broadcast_to((weight > 0).astype(F32), (length, room)))
            routed = jnp.concatenate(routed, axis=1)
            rank = dot(before, routed.astype(BF))
            return jnp.where((rank == wanted) & (routed > 0), 1.0, 0.0)

        for group in range(groups):
            for copy in copies[group * each : (group + 1) * each]:
                copy.wait()
            held_rows = slice(group * length, (group + 1) * length)
            lanes = rows_ref[held_rows, 2 * features :]
            place = places(lanes.astype(F32), expert_ref[0])
            if group == 0:
                place_ref[:, : 2 * room] = place.astype(BF)
                place_ref[:, 2 * room :] = places(lanes.astype(F32), expert_ref[0] ^ 2).astype(BF)
            pick = place.T.astype(BF)
            here = slice(group * room, (group + 1) * room)
            packed = dot(pick, lanes).astype(BF)
            lane_mine[here] = packed[:room]
            theirs_ref[here, 2 * features :] = packed[room:]
            for at in range(0, 2 * features, 512):
                packed = dot(pick, rows_ref[held_rows, at : at + 512]).astype(BF)
                mine_ref = token_mine if at < features else cot_mine
                mine_ref[here, at % features : at % features + 512] = packed[:room]
                theirs_ref[here, at : at + 512] = packed[room:]

    rows = jax.ShapeDtypeStruct((groups * room, features), BF)
    lanes = jax.ShapeDtypeStruct((groups * room, LANES), BF)
    theirs = jax.ShapeDtypeStruct((groups * room, width), BF)
    place = jax.ShapeDtypeStruct((length, 4 * room), BF)
    outs = (rows, rows, lanes, theirs, place)
    return pl.pallas_call(
        body,
        grid_spec=pltpu.PrefetchScalarGridSpec(
            num_scalar_prefetch=1,
            grid=(1,),
            in_specs=[ANYWHERE] * len(arrays),
            out_specs=[whole(a) for a in outs],
            scratch_shapes=[
                pltpu.VMEM((groups * length, width), BF),
                pltpu.SemaphoreType.DMA((len(pieces),)),
            ],
        ),
        out_shape=outs,
        compiler_params=params(1),
        cost_estimate=SMALL,
        name="plan_and_pack",
    )(expert, *arrays)


def spread(place, mine, theirs, far_mine, far_theirs):
    length, slots_of = place.shape
    room, features = far_mine.shape
    size = length // TOGETHER
    parts = (mine, theirs, far_mine, far_theirs)

    def body(place_ref, *refs):
        outs = refs[len(parts) :]
        for at in range(0, features, 512):
            cols = slice(at, at + 512)
            rows = jnp.concatenate([ref[:, cols] for ref in refs[: len(parts)]], axis=0)
            dense = dot(place_ref[...], rows).astype(BF)
            for i, out in enumerate(outs):
                out[:, cols] = dense[i * size : (i + 1) * size]

    out = jax.ShapeDtypeStruct((size, features), BF)
    return pl.pallas_call(
        body,
        grid=(1,),
        in_specs=[whole(place)] + [pl.BlockSpec((room, features), lambda i: (0, 0))] * len(parts),
        out_specs=[whole(out)] * TOGETHER,
        out_shape=(out,) * TOGETHER,
        compiler_params=params(1),
        cost_estimate=SMALL,
        name="spread",
    )(place, *parts)


def split3(value):
    high = value.astype(BF)
    rest = value - high.astype(F32)
    mid = rest.astype(BF)
    low = (rest - mid.astype(F32)).astype(BF)
    return high, mid, low


def after(value, *earlier):
    return lax.optimization_barrier((value, *earlier))[0]


def dense_plan(tokens, route_ids, gate_probs, out_cot, w_gate, w_up, w_down):
    experts = lax.axis_size("expert")
    tok_rows, features = tokens.shape
    hidden = w_gate.shape[2]
    top_count = route_ids.shape[1]
    capacity = max(2, tok_rows * top_count * 4 // (3 * experts))
    expert = lax.axis_index("expert").astype(jnp.int32)
    replica = lax.axis_index("replica").astype(jnp.int32)
    w_gate, w_up, w_down = w_gate[0], w_up[0], w_down[0]

    def to_core(rows):
        return lax.ppermute(rows, "expert", [(i, i ^ 1) for i in range(experts)])

    def to_x(rows):
        return lax.ppermute(rows, "expert", [(i, i ^ 2) for i in range(experts)])

    def to_z(rows, step):
        return lax.ppermute(
            rows, "expert", [(i, (i + 4 * step) % experts) for i in range(experts)]
        )

    def to_y(rows):
        return lax.ppermute(rows, "replica", [(0, 1), (1, 0)])

    chosen = route_ids[:, :, None] == jnp.arange(experts, dtype=jnp.int32)
    share = jnp.sum(jnp.where(chosen, gate_probs[:, :, None], 0.0), axis=1)
    pad = jnp.zeros((tok_rows, LANES - 3 * experts), BF)

    near = [jnp.concatenate([tokens, out_cot, *split3(share), pad], axis=1)]
    far, relay = [to_x(near[0])], [to_y(near[0])]
    near.append(to_z(near[0], 1))
    far.append(to_x(near[1]))
    near.append(after(to_z(near[1], 1), far[0], relay[0]))
    far.append(to_x(near[2]))
    relay += [to_y(far[0]), to_y(near[1]), to_y(far[1]), to_y(near[2])]
    near.append(after(to_z(near[2], 1), relay[1], relay[2]))
    far.append(to_x(near[3]))
    joined = jnp.concatenate([near[3], far[2], far[3]], axis=0)
    last = to_y(joined)
    own_pieces = [(a, 0) for a in near + far]
    other_pieces = [(relay[0], 0), (relay[2], 0), (relay[4], 0), (last, 0)]
    other_pieces += [(relay[1], 0), (relay[3], 0), (last, 1), (last, 2)]
    expert_index = expert
    expert = expert.reshape(1)

    def plan(pieces, *earlier):
        return plan_and_pack(after(expert, *earlier), experts, capacity, tok_rows, pieces)

    def enter(packed):
        mine, cot_mine, mine_lanes, theirs, _ = packed
        theirs = to_core(theirs)
        x = jnp.concatenate([mine, theirs[:, :features]], axis=0)
        shares = jnp.concatenate([mine_lanes, theirs[:, 2 * features :]], axis=0)
        held = (jnp.arange(LANES) % experts == expert_index) & (jnp.arange(LANES) < 3 * experts)
        weight = jnp.sum(jnp.where(held, shares.astype(F32), 0.0), axis=1, keepdims=True)
        cot = jnp.concatenate([cot_mine, theirs[:, features : 2 * features]], axis=0)
        cot = (cot.astype(F32) * weight).astype(BF)
        pre_gate, pre_up = dot(x, w_gate), dot(x, w_up)
        act = (jax.nn.silu(pre_gate) * pre_up).astype(BF)
        return x, weight, pre_gate, pre_up, act, cot

    def leave(rows_of, before_mine=(), before_far=()):
        half = TOGETHER * capacity
        theirs = to_core(rows_of(slice(2 * half, None)))
        mine = rows_of(slice(0, 2 * half), *before_mine)
        return mine, theirs, to_x(after(mine[half:], *before_far)), to_x(theirs[half:])

    def home(place, parts):
        own, *others = spread(place, *parts)
        return [own] + [to_z(a, -step) for step, a in enumerate(others, 1)]

    def total(chunks):
        return sum(a.astype(F32) for a in chunks).astype(BF)

    def grads(x, act, cot, d_gate, d_up):
        x = lax.dynamic_slice_in_dim(x, replica * (features // 2), features // 2, 1)
        act = lax.dynamic_slice_in_dim(act, replica * (hidden // 2), hidden // 2, 1)
        return outer_sum(x, d_gate), outer_sum(x, d_up), outer_sum(act, cot)

    packed = plan(own_pieces, *relay[3:5], joined)
    place = packed[-1]
    own_x, weight, pre_gate, pre_up, act, cot = enter(packed)
    parts = leave(lambda rows: (dot(act[rows], w_down) * weight[rows]).astype(BF))
    cot = after(cot, parts[0], parts[1])
    d_gate, d_up = hidden_grads(cot, pre_gate, pre_up, w_down)

    def token_grads(rows, *earlier):
        return input_rows(*after((d_gate[rows], d_up[rows]), *earlier), w_gate, w_up)

    grad_parts = leave(token_grads, parts[2:3], parts[3:4])
    chunks = home(after(place, grad_parts[0], grad_parts[1]), parts)
    own_grads = after((cot, d_gate, d_up), chunks[0])
    own = grads(own_x, act, *own_grads)
    grad_chunks = home(after(place, *own, *chunks[1:]), grad_parts)

    packed = plan(other_pieces, grad_chunks[0])
    x, weight, pre_gate, pre_up, act, cot = enter(packed)
    d_gate, d_up = hidden_grads(cot, pre_gate, pre_up, w_down)
    other = grads(x, act, cot, d_gate, after(d_up, grad_chunks[1]))
    grad_chunks = after(grad_chunks, other[0])
    grad_gate, grad_up, grad_down = ((a + b).astype(BF)[None] for a, b in zip(own, other))
    return (total(chunks), total(grad_chunks), grad_gate, grad_up, grad_down)


def dense_fits(mesh):
    experts, replicas = mesh.shape["expert"], mesh.shape["replica"]
    return replicas == 2 and experts == 4 * TOGETHER


def solution(mesh):
    placed = (
        P(("expert", "replica"), None),
        P(("expert", "replica"), None),
        P(("expert", "replica"), None),
        P(("expert", "replica"), None),
        P("expert", None, None),
        P("expert", None, None),
        P("expert", None, None),
    )
    return jax.shard_map(
        dense_plan if dense_fits(mesh) else routed_plan,
        mesh=mesh,
        in_specs=placed,
        out_specs=(
            P(("expert", "replica"), None),
            P(("expert", "replica"), None),
            P("expert", "replica", None),
            P("expert", "replica", None),
            P("expert", "replica", None),
        ),
        check_vma=False,
    )
```

```python
import jax
import jax.numpy as jnp
from jax import lax
from jax.experimental import pallas as pl
from jax.experimental.pallas import tpu as pltpu
from jax.sharding import PartitionSpec as P

BF = jnp.bfloat16
F32 = jnp.float32
VMEM = 56 * 1024 * 1024
TOGETHER = 4
LANES = 128
SMALL = pl.CostEstimate(flops=1, bytes_accessed=1, transcendentals=0)


def slots(routes, experts, capacity):
    flat_ids = routes.reshape(-1)
    one_hot = (flat_ids[:, None] == jnp.arange(experts, dtype=jnp.int32)[None, :]).astype(jnp.int32)
    before = jnp.cumsum(one_hot, axis=0) - one_hot
    slot_rank = jnp.sum(before * one_hot, axis=1)
    return flat_ids * capacity + slot_rank


def place(token_rows, positions, total_rows):
    return (
        jnp.zeros((total_rows, token_rows.shape[1]), token_rows.dtype).at[positions].set(token_rows)
    )


def hidden_rows(token_rows, gate_weight, up_weight):
    pre_gate = jnp.dot(token_rows, gate_weight, preferred_element_type=F32)
    pre_up = jnp.dot(token_rows, up_weight, preferred_element_type=F32)
    activation = (jax.nn.silu(pre_gate) * pre_up).astype(BF)
    return (pre_gate, pre_up, activation)


CONTRACT = (((1,), (1,)), ((), ()))


def hidden_grads(grad_rows, pre_gate, pre_up, down_weight):
    d_hidden = lax.dot_general(grad_rows, down_weight, CONTRACT, preferred_element_type=F32)
    sigmoid_gate = jax.nn.sigmoid(pre_gate)
    d_gate = (d_hidden * pre_up * sigmoid_gate * (1.0 + pre_gate * (1.0 - sigmoid_gate))).astype(BF)
    d_up = (d_hidden * pre_gate * sigmoid_gate).astype(BF)
    return d_gate, d_up


def input_rows(d_gate, d_up, gate_weight, up_weight):
    back_rows = lax.dot_general(d_gate, gate_weight, CONTRACT, preferred_element_type=F32)
    back_rows = back_rows + lax.dot_general(d_up, up_weight, CONTRACT, preferred_element_type=F32)
    return back_rows.astype(BF)


def outer_sum(left, right):
    return lax.dot_general(left, right, (((0,), (0,)), ((), ())), preferred_element_type=F32)


def routed_plan(tokens, route_ids, gate_probs, out_cot, w_gate, w_up, w_down):
    experts = lax.axis_size("expert")
    tok_rows, features = tokens.shape
    top_count = route_ids.shape[1]
    hidden = w_gate.shape[2]
    capacity = max(2, tok_rows * top_count * 4 // (3 * experts))
    total_rows = experts * capacity
    positions = slots(route_ids, experts, capacity)
    gate_weight, up_weight, down_weight = w_gate[0], w_up[0], w_down[0]

    def exchange(rows):
        blocks = rows.reshape(experts, capacity, features)
        return lax.all_to_all(blocks, "expert", 0, 0, tiled=True).reshape(-1, features)

    received = exchange(place(jnp.repeat(tokens, top_count, axis=0), positions, total_rows))
    pre_gate, pre_up, activation = hidden_rows(received, gate_weight, up_weight)
    result = jnp.dot(activation, down_weight, preferred_element_type=F32).astype(BF)
    picked = exchange(result)[positions].reshape(tok_rows, top_count, features)
    combined = jnp.einsum("tk,tkd->td", gate_probs, picked.astype(F32)).astype(BF)
    scaled = (gate_probs[:, :, None] * out_cot[:, None, :].astype(F32)).astype(BF)
    grads_in = exchange(place(scaled.reshape(-1, features), positions, total_rows))
    d_gate, d_up = hidden_grads(grads_in, pre_gate, pre_up, down_weight)
    back = exchange(input_rows(d_gate, d_up, gate_weight, up_weight))
    grad_tokens = jnp.sum(
        back[positions].reshape(tok_rows, top_count, features).astype(F32), axis=1
    ).astype(BF)
    gate_up_sum = lax.psum_scatter(
        outer_sum(received, jnp.concatenate([d_gate, d_up], axis=1)).astype(BF),
        "replica",
        scatter_dimension=0,
        tiled=True,
    )
    down_sum = lax.psum_scatter(
        outer_sum(activation, grads_in).astype(BF), "replica", scatter_dimension=0, tiled=True
    )
    return (
        combined,
        grad_tokens,
        gate_up_sum[:, :hidden][None],
        gate_up_sum[:, hidden:][None],
        down_sum[None],
    )

def dot(left, right):
    return jnp.dot(left, right, preferred_element_type=F32)


def whole(array):
    return pl.BlockSpec(array.shape, lambda *_: (0,) * array.ndim)


def params(steps=0):
    order = ("arbitrary",) * steps if steps else None
    return pltpu.CompilerParams(dimension_semantics=order, vmem_limit_bytes=VMEM)


ANYWHERE = pl.BlockSpec(memory_space=pl.ANY)


def plan_and_pack(expert, experts, capacity, tok_rows, pieces):
    arrays = []
    for array, _ in pieces:
        if not any(array is a for a in arrays):
            arrays.append(array)
    sources = [
        (next(k for k, a in enumerate(arrays) if a is array), chunk) for array, chunk in pieces
    ]
    width = arrays[0].shape[1]
    features = (width - LANES) // 2
    groups, each = 2, len(pieces) // 2
    length, room = TOGETHER * tok_rows, TOGETHER * capacity

    def body(expert_ref, *refs):
        outs = refs[len(arrays) :]
        token_mine, cot_mine, lane_mine, theirs_ref, place_ref, rows_ref, sems = outs
        copies = []
        for i, (source, chunk) in enumerate(sources):
            copies.append(
                pltpu.make_async_copy(
                    refs[source].at[chunk * tok_rows : (chunk + 1) * tok_rows],
                    rows_ref.at[i * tok_rows : (i + 1) * tok_rows],
                    sems.at[i],
                )
            )
            copies[-1].start()
        lane = lax.broadcasted_iota(jnp.int32, (length, LANES), 1)
        row = lax.broadcasted_iota(jnp.int32, (length, length), 0)
        col = lax.broadcasted_iota(jnp.int32, (length, length), 1)
        before = (row >= col).astype(BF)
        slot = lax.broadcasted_iota(jnp.int32, (length, 2 * room), 1) % room
        wanted = (slot + 1).astype(F32)

        def places(shares, first):
            routed = []
            for index in (first, first ^ 1):
                held = (lane == index) | (lane == index + experts) | (lane == index + 2 * experts)
                weight = jnp.sum(jnp.where(held, shares, 0.0), axis=1, keepdims=True)
                routed.append(jnp.broadcast_to((weight > 0).astype(F32), (length, room)))
            routed = jnp.concatenate(routed, axis=1)
            rank = dot(before, routed.astype(BF))
            return jnp.where((rank == wanted) & (routed > 0), 1.0, 0.0)

        for group in range(groups):
            for copy in copies[group * each : (group + 1) * each]:
                copy.wait()
            held_rows = slice(group * length, (group + 1) * length)
            lanes = rows_ref[held_rows, 2 * features :]
            place = places(lanes.astype(F32), expert_ref[0])
            if group == 0:
                place_ref[:, : 2 * room] = place.astype(BF)
                place_ref[:, 2 * room :] = places(lanes.astype(F32), expert_ref[0] ^ 2).astype(BF)
            pick = place.T.astype(BF)
            here = slice(group * room, (group + 1) * room)
            packed = dot(pick, lanes).astype(BF)
            lane_mine[here] = packed[:room]
            theirs_ref[here, 2 * features :] = packed[room:]
            for at in range(0, 2 * features, 512):
                packed = dot(pick, rows_ref[held_rows, at : at + 512]).astype(BF)
                mine_ref = token_mine if at < features else cot_mine
                mine_ref[here, at % features : at % features + 512] = packed[:room]
                theirs_ref[here, at : at + 512] = packed[room:]

    rows = jax.ShapeDtypeStruct((groups * room, features), BF)
    lanes = jax.ShapeDtypeStruct((groups * room, LANES), BF)
    theirs = jax.ShapeDtypeStruct((groups * room, width), BF)
    place = jax.ShapeDtypeStruct((length, 4 * room), BF)
    outs = (rows, rows, lanes, theirs, place)
    return pl.pallas_call(
        body,
        grid_spec=pltpu.PrefetchScalarGridSpec(
            num_scalar_prefetch=1,
            grid=(1,),
            in_specs=[ANYWHERE] * len(arrays),
            out_specs=[whole(a) for a in outs],
            scratch_shapes=[
                pltpu.VMEM((groups * length, width), BF),
                pltpu.SemaphoreType.DMA((len(pieces),)),
            ],
        ),
        out_shape=outs,
        compiler_params=params(1),
        cost_estimate=SMALL,
        name="plan_and_pack",
    )(expert, *arrays)


def spread(line, place, mine, theirs, far_mine, far_theirs):
    length, slots_of = place.shape
    room, features = far_mine.shape
    size = length // TOGETHER
    parts = (mine, theirs, far_mine, far_theirs)

    def body(line_ref, place_ref, *refs):
        out_ref = refs[-1]
        for at in range(0, features, 512):
            cols = slice(at, at + 512)
            rows = jnp.concatenate([ref[:, cols] for ref in refs[: len(parts)]], axis=0)
            dense = dot(place_ref[...], rows).astype(BF)
            for i in range(TOGETHER):
                home = (line_ref[0] + TOGETHER - i) % TOGETHER
                out_ref[home, :, cols] = dense[i * size : (i + 1) * size]

    out = jax.ShapeDtypeStruct((TOGETHER, size, features), BF)
    part_spec = pl.BlockSpec((room, features), lambda i, e: (0, 0))
    return pl.pallas_call(
        body,
        grid_spec=pltpu.PrefetchScalarGridSpec(
            num_scalar_prefetch=1,
            grid=(1,),
            in_specs=[whole(place)] + [part_spec] * len(parts),
            out_specs=whole(out),
        ),
        out_shape=out,
        compiler_params=params(1),
        cost_estimate=SMALL,
        name="spread",
    )(line, place, *parts)


def split3(value):
    high = value.astype(BF)
    rest = value - high.astype(F32)
    mid = rest.astype(BF)
    low = (rest - mid.astype(F32)).astype(BF)
    return high, mid, low


def after(value, *earlier):
    return lax.optimization_barrier((value, *earlier))[0]


def dense_plan(tokens, route_ids, gate_probs, out_cot, w_gate, w_up, w_down):
    experts = lax.axis_size("expert")
    tok_rows, features = tokens.shape
    hidden = w_gate.shape[2]
    top_count = route_ids.shape[1]
    capacity = max(2, tok_rows * top_count * 4 // (3 * experts))
    expert = lax.axis_index("expert").astype(jnp.int32)
    replica = lax.axis_index("replica").astype(jnp.int32)
    w_gate, w_up, w_down = w_gate[0], w_up[0], w_down[0]

    def to_core(rows):
        return lax.ppermute(rows, "expert", [(i, i ^ 1) for i in range(experts)])

    def to_x(rows):
        return lax.ppermute(rows, "expert", [(i, i ^ 2) for i in range(experts)])

    def to_z(rows, step):
        return lax.ppermute(
            rows, "expert", [(i, (i + 4 * step) % experts) for i in range(experts)]
        )

    def to_y(rows):
        return lax.ppermute(rows, "replica", [(0, 1), (1, 0)])

    chosen = route_ids[:, :, None] == jnp.arange(experts, dtype=jnp.int32)
    share = jnp.sum(jnp.where(chosen, gate_probs[:, :, None], 0.0), axis=1)
    pad = jnp.zeros((tok_rows, LANES - 3 * experts), BF)

    near = [jnp.concatenate([tokens, out_cot, *split3(share), pad], axis=1)]
    far, relay = [to_x(near[0])], [to_y(near[0])]
    near.append(to_z(near[0], 1))
    far.append(to_x(near[1]))
    near.append(after(to_z(near[1], 1), far[0], relay[0]))
    far.append(to_x(near[2]))
    relay += [to_y(far[0]), to_y(near[1]), to_y(far[1]), to_y(near[2])]
    near.append(to_z(near[2], 1))
    far.append(to_x(near[3]))
    joined = jnp.concatenate([near[3], far[2], far[3]], axis=0)
    last = to_y(joined)
    own_pieces = [(a, 0) for a in near + far]
    other_pieces = [(relay[0], 0), (relay[2], 0), (relay[4], 0), (last, 0)]
    other_pieces += [(relay[1], 0), (relay[3], 0), (last, 1), (last, 2)]
    expert_index = expert
    expert = expert.reshape(1)

    def plan(pieces, *earlier):
        return plan_and_pack(after(expert, *earlier), experts, capacity, tok_rows, pieces)

    def enter(packed):
        mine, cot_mine, mine_lanes, theirs, _ = packed
        theirs = to_core(theirs)
        x = jnp.concatenate([mine, theirs[:, :features]], axis=0)
        shares = jnp.concatenate([mine_lanes, theirs[:, 2 * features :]], axis=0)
        held = (jnp.arange(LANES) % experts == expert_index) & (jnp.arange(LANES) < 3 * experts)
        weight = jnp.sum(jnp.where(held, shares.astype(F32), 0.0), axis=1, keepdims=True)
        cot = jnp.concatenate([cot_mine, theirs[:, features : 2 * features]], axis=0)
        cot = (cot.astype(F32) * weight).astype(BF)
        pre_gate, pre_up = dot(x, w_gate), dot(x, w_up)
        act = (jax.nn.silu(pre_gate) * pre_up).astype(BF)
        return x, weight, pre_gate, pre_up, act, cot

    def leave(rows_of, before_mine=(), before_far=()):
        half = TOGETHER * capacity
        theirs = to_core(rows_of(slice(2 * half, None)))
        mine = rows_of(slice(0, 2 * half), *before_mine)
        return mine, theirs, to_x(after(mine[half:], *before_far)), to_x(theirs[half:])

    lines = [list(range(first, experts, 4)) for first in range(4)]

    def home(place, parts):
        dense = spread(expert // 4, place, *parts)
        return dense, lax.all_to_all(dense, "expert", 0, 0, axis_index_groups=lines, tiled=True)

    def total(chunks):
        return jnp.sum(chunks.astype(F32), axis=0).astype(BF)

    def grads(x, act, cot, d_gate, d_up):
        x = lax.dynamic_slice_in_dim(x, replica * (features // 2), features // 2, 1)
        act = lax.dynamic_slice_in_dim(act, replica * (hidden // 2), hidden // 2, 1)
        return outer_sum(x, d_gate), outer_sum(x, d_up), outer_sum(act, cot)

    packed = plan(own_pieces, *relay[1:4], joined)
    place = packed[-1]
    own_x, weight, pre_gate, pre_up, act, cot = enter(packed)
    parts = leave(lambda rows: (dot(act[rows], w_down) * weight[rows]).astype(BF))
    cot = after(cot, parts[0], parts[1], relay[4])
    d_gate, d_up = hidden_grads(cot, pre_gate, pre_up, w_down)

    def token_grads(rows, *earlier):
        return input_rows(*after((d_gate[rows], d_up[rows]), *earlier), w_gate, w_up)

    grad_parts = leave(token_grads, parts[2:3], parts[3:4])
    dense, chunks = home(after(place, grad_parts[0], grad_parts[1]), parts)
    own = grads(own_x, act, *after((cot, d_gate, d_up), dense))
    dense, grad_chunks = home(after(place, *own), grad_parts)

    packed = plan(other_pieces, dense)
    x, weight, pre_gate, pre_up, act, cot = enter(packed)
    d_gate, d_up = hidden_grads(cot, pre_gate, pre_up, w_down)
    other = grads(x, act, cot, d_gate, d_up)
    chunks, grad_chunks = after(chunks, other[0]), after(grad_chunks, other[0])
    grad_gate, grad_up, grad_down = ((a + b).astype(BF)[None] for a, b in zip(own, other))
    return (total(chunks), total(grad_chunks), grad_gate, grad_up, grad_down)


def dense_fits(mesh):
    experts, replicas = mesh.shape["expert"], mesh.shape["replica"]
    return replicas == 2 and experts == 4 * TOGETHER


def solution(mesh):
    placed = (
        P(("expert", "replica"), None),
        P(("expert", "replica"), None),
        P(("expert", "replica"), None),
        P(("expert", "replica"), None),
        P("expert", None, None),
        P("expert", None, None),
        P("expert", None, None),
    )
    return jax.shard_map(
        dense_plan if dense_fits(mesh) else routed_plan,
        mesh=mesh,
        in_specs=placed,
        out_specs=(
            P(("expert", "replica"), None),
            P(("expert", "replica"), None),
            P("expert", "replica", None),
            P("expert", "replica", None),
            P("expert", "replica", None),
        ),
        check_vma=False,
    )
```

```python
import jax
import jax.numpy as jnp
from jax import lax
from jax.experimental import pallas as pl
from jax.experimental.pallas import tpu as pltpu
from jax.sharding import PartitionSpec as P

BF = jnp.bfloat16
F32 = jnp.float32
VMEM = 56 * 1024 * 1024
TOGETHER = 4
LANES = 128
SMALL = pl.CostEstimate(flops=1, bytes_accessed=1, transcendentals=0)


def slots(routes, experts, capacity):
    flat_ids = routes.reshape(-1)
    one_hot = (flat_ids[:, None] == jnp.arange(experts, dtype=jnp.int32)[None, :]).astype(jnp.int32)
    before = jnp.cumsum(one_hot, axis=0) - one_hot
    slot_rank = jnp.sum(before * one_hot, axis=1)
    return flat_ids * capacity + slot_rank


def place(token_rows, positions, total_rows):
    return (
        jnp.zeros((total_rows, token_rows.shape[1]), token_rows.dtype).at[positions].set(token_rows)
    )


def hidden_rows(token_rows, gate_weight, up_weight):
    pre_gate = jnp.dot(token_rows, gate_weight, preferred_element_type=F32)
    pre_up = jnp.dot(token_rows, up_weight, preferred_element_type=F32)
    activation = (jax.nn.silu(pre_gate) * pre_up).astype(BF)
    return (pre_gate, pre_up, activation)


CONTRACT = (((1,), (1,)), ((), ()))


def hidden_grads(grad_rows, pre_gate, pre_up, down_weight):
    d_hidden = lax.dot_general(grad_rows, down_weight, CONTRACT, preferred_element_type=F32)
    sigmoid_gate = jax.nn.sigmoid(pre_gate)
    d_gate = (d_hidden * pre_up * sigmoid_gate * (1.0 + pre_gate * (1.0 - sigmoid_gate))).astype(BF)
    d_up = (d_hidden * pre_gate * sigmoid_gate).astype(BF)
    return d_gate, d_up


def input_rows(d_gate, d_up, gate_weight, up_weight):
    back_rows = lax.dot_general(d_gate, gate_weight, CONTRACT, preferred_element_type=F32)
    back_rows = back_rows + lax.dot_general(d_up, up_weight, CONTRACT, preferred_element_type=F32)
    return back_rows.astype(BF)


def outer_sum(left, right):
    return lax.dot_general(left, right, (((0,), (0,)), ((), ())), preferred_element_type=F32)


def routed_plan(tokens, route_ids, gate_probs, out_cot, w_gate, w_up, w_down):
    experts = lax.axis_size("expert")
    tok_rows, features = tokens.shape
    top_count = route_ids.shape[1]
    hidden = w_gate.shape[2]
    capacity = max(2, tok_rows * top_count * 4 // (3 * experts))
    total_rows = experts * capacity
    positions = slots(route_ids, experts, capacity)
    gate_weight, up_weight, down_weight = w_gate[0], w_up[0], w_down[0]

    def exchange(rows):
        blocks = rows.reshape(experts, capacity, features)
        return lax.all_to_all(blocks, "expert", 0, 0, tiled=True).reshape(-1, features)

    received = exchange(place(jnp.repeat(tokens, top_count, axis=0), positions, total_rows))
    pre_gate, pre_up, activation = hidden_rows(received, gate_weight, up_weight)
    result = jnp.dot(activation, down_weight, preferred_element_type=F32).astype(BF)
    picked = exchange(result)[positions].reshape(tok_rows, top_count, features)
    combined = jnp.einsum("tk,tkd->td", gate_probs, picked.astype(F32)).astype(BF)
    scaled = (gate_probs[:, :, None] * out_cot[:, None, :].astype(F32)).astype(BF)
    grads_in = exchange(place(scaled.reshape(-1, features), positions, total_rows))
    d_gate, d_up = hidden_grads(grads_in, pre_gate, pre_up, down_weight)
    back = exchange(input_rows(d_gate, d_up, gate_weight, up_weight))
    grad_tokens = jnp.sum(
        back[positions].reshape(tok_rows, top_count, features).astype(F32), axis=1
    ).astype(BF)
    gate_up_sum = lax.psum_scatter(
        outer_sum(received, jnp.concatenate([d_gate, d_up], axis=1)).astype(BF),
        "replica",
        scatter_dimension=0,
        tiled=True,
    )
    down_sum = lax.psum_scatter(
        outer_sum(activation, grads_in).astype(BF), "replica", scatter_dimension=0, tiled=True
    )
    return (
        combined,
        grad_tokens,
        gate_up_sum[:, :hidden][None],
        gate_up_sum[:, hidden:][None],
        down_sum[None],
    )

def dot(left, right):
    return jnp.dot(left, right, preferred_element_type=F32)


def whole(array):
    return pl.BlockSpec(array.shape, lambda *_: (0,) * array.ndim)


def params(steps=0):
    order = ("arbitrary",) * steps if steps else None
    return pltpu.CompilerParams(dimension_semantics=order, vmem_limit_bytes=VMEM)


ANYWHERE = pl.BlockSpec(memory_space=pl.ANY)


def plan_and_pack(expert, experts, capacity, tok_rows, pieces):
    arrays = []
    for array, _ in pieces:
        if not any(array is a for a in arrays):
            arrays.append(array)
    sources = [
        (next(k for k, a in enumerate(arrays) if a is array), chunk) for array, chunk in pieces
    ]
    width = arrays[0].shape[1]
    features = (width - LANES) // 2
    groups, each = 2, len(pieces) // 2
    length, room = TOGETHER * tok_rows, TOGETHER * capacity

    def body(expert_ref, *refs):
        outs = refs[len(arrays) :]
        token_mine, cot_mine, lane_mine, theirs_ref, place_ref, rows_ref, sems = outs
        copies = []
        for i, (source, chunk) in enumerate(sources):
            copies.append(
                pltpu.make_async_copy(
                    refs[source].at[chunk * tok_rows : (chunk + 1) * tok_rows],
                    rows_ref.at[i * tok_rows : (i + 1) * tok_rows],
                    sems.at[i],
                )
            )
            copies[-1].start()
        lane = lax.broadcasted_iota(jnp.int32, (length, LANES), 1)
        row = lax.broadcasted_iota(jnp.int32, (length, length), 0)
        col = lax.broadcasted_iota(jnp.int32, (length, length), 1)
        before = (row >= col).astype(BF)
        slot = lax.broadcasted_iota(jnp.int32, (length, 2 * room), 1) % room
        wanted = (slot + 1).astype(F32)

        def places(shares, first):
            routed = []
            for index in (first, first ^ 1):
                held = (lane == index) | (lane == index + experts) | (lane == index + 2 * experts)
                weight = jnp.sum(jnp.where(held, shares, 0.0), axis=1, keepdims=True)
                routed.append(jnp.broadcast_to((weight > 0).astype(F32), (length, room)))
            routed = jnp.concatenate(routed, axis=1)
            rank = dot(before, routed.astype(BF))
            return jnp.where((rank == wanted) & (routed > 0), 1.0, 0.0)

        for group in range(groups):
            for copy in copies[group * each : (group + 1) * each]:
                copy.wait()
            held_rows = slice(group * length, (group + 1) * length)
            lanes = rows_ref[held_rows, 2 * features :]
            place = places(lanes.astype(F32), expert_ref[0])
            if group == 0:
                place_ref[:, : 2 * room] = place.astype(BF)
                place_ref[:, 2 * room :] = places(lanes.astype(F32), expert_ref[0] ^ 2).astype(BF)
            pick = place.T.astype(BF)
            here = slice(group * room, (group + 1) * room)
            packed = dot(pick, lanes).astype(BF)
            lane_mine[here] = packed[:room]
            theirs_ref[here, 2 * features :] = packed[room:]
            for at in range(0, 2 * features, 512):
                packed = dot(pick, rows_ref[held_rows, at : at + 512]).astype(BF)
                mine_ref = token_mine if at < features else cot_mine
                mine_ref[here, at % features : at % features + 512] = packed[:room]
                theirs_ref[here, at : at + 512] = packed[room:]

    rows = jax.ShapeDtypeStruct((groups * room, features), BF)
    lanes = jax.ShapeDtypeStruct((groups * room, LANES), BF)
    theirs = jax.ShapeDtypeStruct((groups * room, width), BF)
    place = jax.ShapeDtypeStruct((length, 4 * room), BF)
    outs = (rows, rows, lanes, theirs, place)
    return pl.pallas_call(
        body,
        grid_spec=pltpu.PrefetchScalarGridSpec(
            num_scalar_prefetch=1,
            grid=(1,),
            in_specs=[ANYWHERE] * len(arrays),
            out_specs=[whole(a) for a in outs],
            scratch_shapes=[
                pltpu.VMEM((groups * length, width), BF),
                pltpu.SemaphoreType.DMA((len(pieces),)),
            ],
        ),
        out_shape=outs,
        compiler_params=params(1),
        cost_estimate=SMALL,
        name="plan_and_pack",
    )(expert, *arrays)


def spread(place, mine, theirs, far_mine, far_theirs):
    length, slots_of = place.shape
    room, features = far_mine.shape
    size = length // TOGETHER
    parts = (mine, theirs, far_mine, far_theirs)

    def body(place_ref, *refs):
        outs = refs[len(parts) :]
        for at in range(0, features, 512):
            cols = slice(at, at + 512)
            rows = jnp.concatenate([ref[:, cols] for ref in refs[: len(parts)]], axis=0)
            dense = dot(place_ref[...], rows).astype(BF)
            for i, out in enumerate(outs):
                out[:, cols] = dense[i * size : (i + 1) * size]

    out = jax.ShapeDtypeStruct((size, features), BF)
    return pl.pallas_call(
        body,
        grid=(1,),
        in_specs=[whole(place)] + [pl.BlockSpec((room, features), lambda i: (0, 0))] * len(parts),
        out_specs=[whole(out)] * TOGETHER,
        out_shape=(out,) * TOGETHER,
        compiler_params=params(1),
        cost_estimate=SMALL,
        name="spread",
    )(place, *parts)


def split3(value):
    high = value.astype(BF)
    rest = value - high.astype(F32)
    mid = rest.astype(BF)
    low = (rest - mid.astype(F32)).astype(BF)
    return high, mid, low


def after(value, *earlier):
    return lax.optimization_barrier((value, *earlier))[0]


def dense_plan(tokens, route_ids, gate_probs, out_cot, w_gate, w_up, w_down):
    experts = lax.axis_size("expert")
    tok_rows, features = tokens.shape
    hidden = w_gate.shape[2]
    top_count = route_ids.shape[1]
    capacity = max(2, tok_rows * top_count * 4 // (3 * experts))
    expert = lax.axis_index("expert").astype(jnp.int32)
    replica = lax.axis_index("replica").astype(jnp.int32)
    w_gate, w_up, w_down = w_gate[0], w_up[0], w_down[0]

    def to_core(rows):
        return lax.ppermute(rows, "expert", [(i, i ^ 1) for i in range(experts)])

    def to_x(rows):
        return lax.ppermute(rows, "expert", [(i, i ^ 2) for i in range(experts)])

    def to_z(rows, step):
        return lax.ppermute(
            rows, "expert", [(i, (i + 4 * step) % experts) for i in range(experts)]
        )

    def to_y(rows):
        return lax.ppermute(rows, "replica", [(0, 1), (1, 0)])

    chosen = route_ids[:, :, None] == jnp.arange(experts, dtype=jnp.int32)
    share = jnp.sum(jnp.where(chosen, gate_probs[:, :, None], 0.0), axis=1)
    pad = jnp.zeros((tok_rows, LANES - 3 * experts), BF)

    near = [jnp.concatenate([tokens, out_cot, *split3(share), pad], axis=1)]
    far, relay = [to_x(near[0])], [to_y(near[0])]
    near.append(to_z(near[0], 1))
    far.append(to_x(near[1]))
    near.append(after(to_z(near[1], 1), far[0], relay[0]))
    far.append(to_x(near[2]))
    near.append(to_z(near[2], 1))
    far.append(to_x(near[3]))
    relay += [to_y(far[0]), to_y(near[1]), to_y(far[1])]
    joined = jnp.concatenate([near[2], near[3], far[2], far[3]], axis=0)
    last = to_y(joined)
    own_pieces = [(a, 0) for a in near + far]
    other_pieces = [(relay[0], 0), (relay[2], 0), (last, 0), (last, 1)]
    other_pieces += [(relay[1], 0), (relay[3], 0), (last, 2), (last, 3)]
    expert_index = expert
    expert = expert.reshape(1)

    def plan(pieces, *earlier):
        return plan_and_pack(after(expert, *earlier), experts, capacity, tok_rows, pieces)

    def enter(packed):
        mine, cot_mine, mine_lanes, theirs, _ = packed
        theirs = to_core(theirs)
        x = jnp.concatenate([mine, theirs[:, :features]], axis=0)
        shares = jnp.concatenate([mine_lanes, theirs[:, 2 * features :]], axis=0)
        held = (jnp.arange(LANES) % experts == expert_index) & (jnp.arange(LANES) < 3 * experts)
        weight = jnp.sum(jnp.where(held, shares.astype(F32), 0.0), axis=1, keepdims=True)
        cot = jnp.concatenate([cot_mine, theirs[:, features : 2 * features]], axis=0)
        cot = (cot.astype(F32) * weight).astype(BF)
        pre_gate, pre_up = dot(x, w_gate), dot(x, w_up)
        act = (jax.nn.silu(pre_gate) * pre_up).astype(BF)
        return x, weight, pre_gate, pre_up, act, cot

    def leave(rows_of, before_mine=(), before_far=()):
        half = TOGETHER * capacity
        theirs = to_core(rows_of(slice(2 * half, None)))
        mine = rows_of(slice(0, 2 * half), *before_mine)
        return mine, theirs, to_x(after(mine[half:], *before_far)), to_x(theirs[half:])

    def home(place, parts):
        own, *others = spread(place, *parts)
        return [own] + [to_z(a, -step) for step, a in enumerate(others, 1)]

    def total(chunks):
        return sum(a.astype(F32) for a in chunks).astype(BF)

    def grads(x, act, cot, d_gate, d_up):
        x = lax.dynamic_slice_in_dim(x, replica * (features // 2), features // 2, 1)
        act = lax.dynamic_slice_in_dim(act, replica * (hidden // 2), hidden // 2, 1)
        return outer_sum(x, d_gate), outer_sum(x, d_up), outer_sum(act, cot)

    packed = plan(own_pieces, *relay[1:4], joined)
    place = packed[-1]
    own_x, weight, pre_gate, pre_up, act, cot = enter(packed)
    parts = leave(lambda rows: (dot(act[rows], w_down) * weight[rows]).astype(BF))
    cot = after(cot, parts[0], parts[1])
    d_gate, d_up = hidden_grads(cot, pre_gate, pre_up, w_down)

    def token_grads(rows, *earlier):
        return input_rows(*after((d_gate[rows], d_up[rows]), *earlier), w_gate, w_up)

    grad_parts = leave(token_grads, parts[2:3], parts[3:4])
    chunks = home(after(place, grad_parts[0], grad_parts[1]), parts)
    own_grads = after((cot, d_gate, d_up), chunks[0])
    own = grads(own_x, act, *own_grads)
    packed = plan(other_pieces, *own, *grad_parts[2:], *chunks[1:])
    grad_chunks = home(after(place, packed[-1]), grad_parts)

    x, weight, pre_gate, pre_up, act, cot = enter(packed)
    d_gate, d_up = hidden_grads(cot, pre_gate, pre_up, w_down)
    other = grads(x, act, cot, d_gate, after(d_up, grad_chunks[1]))
    chunks, grad_chunks = after((chunks, grad_chunks), other[0])
    grad_gate, grad_up, grad_down = ((a + b).astype(BF)[None] for a, b in zip(own, other))
    return (total(chunks), total(grad_chunks), grad_gate, grad_up, grad_down)


def dense_fits(mesh):
    experts, replicas = mesh.shape["expert"], mesh.shape["replica"]
    return replicas == 2 and experts == 4 * TOGETHER


def solution(mesh):
    placed = (
        P(("expert", "replica"), None),
        P(("expert", "replica"), None),
        P(("expert", "replica"), None),
        P(("expert", "replica"), None),
        P("expert", None, None),
        P("expert", None, None),
        P("expert", None, None),
    )
    return jax.shard_map(
        dense_plan if dense_fits(mesh) else routed_plan,
        mesh=mesh,
        in_specs=placed,
        out_specs=(
            P(("expert", "replica"), None),
            P(("expert", "replica"), None),
            P("expert", "replica", None),
            P("expert", "replica", None),
            P("expert", "replica", None),
        ),
        check_vma=False,
    )
```

```python
import jax
import jax.numpy as jnp
from jax import lax
from jax.experimental import pallas as pl
from jax.experimental.pallas import tpu as pltpu
from jax.sharding import PartitionSpec as P

BF = jnp.bfloat16
F32 = jnp.float32
VMEM = 56 * 1024 * 1024
TOGETHER = 4
LANES = 128
SMALL = pl.CostEstimate(flops=1, bytes_accessed=1, transcendentals=0)


def slots(routes, experts, capacity):
    flat_ids = routes.reshape(-1)
    one_hot = (flat_ids[:, None] == jnp.arange(experts, dtype=jnp.int32)[None, :]).astype(jnp.int32)
    before = jnp.cumsum(one_hot, axis=0) - one_hot
    slot_rank = jnp.sum(before * one_hot, axis=1)
    return flat_ids * capacity + slot_rank


def place(token_rows, positions, total_rows):
    return (
        jnp.zeros((total_rows, token_rows.shape[1]), token_rows.dtype).at[positions].set(token_rows)
    )


def hidden_rows(token_rows, gate_weight, up_weight):
    pre_gate = jnp.dot(token_rows, gate_weight, preferred_element_type=F32)
    pre_up = jnp.dot(token_rows, up_weight, preferred_element_type=F32)
    activation = (jax.nn.silu(pre_gate) * pre_up).astype(BF)
    return (pre_gate, pre_up, activation)


CONTRACT = (((1,), (1,)), ((), ()))


def hidden_grads(grad_rows, pre_gate, pre_up, down_weight):
    d_hidden = lax.dot_general(grad_rows, down_weight, CONTRACT, preferred_element_type=F32)
    sigmoid_gate = jax.nn.sigmoid(pre_gate)
    d_gate = (d_hidden * pre_up * sigmoid_gate * (1.0 + pre_gate * (1.0 - sigmoid_gate))).astype(BF)
    d_up = (d_hidden * pre_gate * sigmoid_gate).astype(BF)
    return d_gate, d_up


def input_rows(d_gate, d_up, gate_weight, up_weight):
    back_rows = lax.dot_general(d_gate, gate_weight, CONTRACT, preferred_element_type=F32)
    back_rows = back_rows + lax.dot_general(d_up, up_weight, CONTRACT, preferred_element_type=F32)
    return back_rows.astype(BF)


def outer_sum(left, right):
    return lax.dot_general(left, right, (((0,), (0,)), ((), ())), preferred_element_type=F32)


def routed_plan(tokens, route_ids, gate_probs, out_cot, w_gate, w_up, w_down):
    experts = lax.axis_size("expert")
    tok_rows, features = tokens.shape
    top_count = route_ids.shape[1]
    hidden = w_gate.shape[2]
    capacity = max(2, tok_rows * top_count * 4 // (3 * experts))
    total_rows = experts * capacity
    positions = slots(route_ids, experts, capacity)
    gate_weight, up_weight, down_weight = w_gate[0], w_up[0], w_down[0]

    def exchange(rows):
        blocks = rows.reshape(experts, capacity, features)
        return lax.all_to_all(blocks, "expert", 0, 0, tiled=True).reshape(-1, features)

    received = exchange(place(jnp.repeat(tokens, top_count, axis=0), positions, total_rows))
    pre_gate, pre_up, activation = hidden_rows(received, gate_weight, up_weight)
    result = jnp.dot(activation, down_weight, preferred_element_type=F32).astype(BF)
    picked = exchange(result)[positions].reshape(tok_rows, top_count, features)
    combined = jnp.einsum("tk,tkd->td", gate_probs, picked.astype(F32)).astype(BF)
    scaled = (gate_probs[:, :, None] * out_cot[:, None, :].astype(F32)).astype(BF)
    grads_in = exchange(place(scaled.reshape(-1, features), positions, total_rows))
    d_gate, d_up = hidden_grads(grads_in, pre_gate, pre_up, down_weight)
    back = exchange(input_rows(d_gate, d_up, gate_weight, up_weight))
    grad_tokens = jnp.sum(
        back[positions].reshape(tok_rows, top_count, features).astype(F32), axis=1
    ).astype(BF)
    gate_up_sum = lax.psum_scatter(
        outer_sum(received, jnp.concatenate([d_gate, d_up], axis=1)).astype(BF),
        "replica",
        scatter_dimension=0,
        tiled=True,
    )
    down_sum = lax.psum_scatter(
        outer_sum(activation, grads_in).astype(BF), "replica", scatter_dimension=0, tiled=True
    )
    return (
        combined,
        grad_tokens,
        gate_up_sum[:, :hidden][None],
        gate_up_sum[:, hidden:][None],
        down_sum[None],
    )

def dot(left, right):
    return jnp.dot(left, right, preferred_element_type=F32)


def whole(array):
    return pl.BlockSpec(array.shape, lambda *_: (0,) * array.ndim)


def params(steps=0):
    order = ("arbitrary",) * steps if steps else None
    return pltpu.CompilerParams(dimension_semantics=order, vmem_limit_bytes=VMEM)


ANYWHERE = pl.BlockSpec(memory_space=pl.ANY)


def plan_and_pack(expert, experts, capacity, tok_rows, pieces):
    arrays = []
    for array, _ in pieces:
        if not any(array is a for a in arrays):
            arrays.append(array)
    sources = [
        (next(k for k, a in enumerate(arrays) if a is array), chunk) for array, chunk in pieces
    ]
    width = arrays[0].shape[1]
    features = (width - LANES) // 2
    groups, each = 2, len(pieces) // 2
    length, room = TOGETHER * tok_rows, TOGETHER * capacity

    def body(expert_ref, *refs):
        outs = refs[len(arrays) :]
        token_mine, cot_mine, lane_mine, theirs_ref, place_ref, rows_ref, sems = outs
        copies = []
        for i, (source, chunk) in enumerate(sources):
            copies.append(
                pltpu.make_async_copy(
                    refs[source].at[chunk * tok_rows : (chunk + 1) * tok_rows],
                    rows_ref.at[i * tok_rows : (i + 1) * tok_rows],
                    sems.at[i],
                )
            )
            copies[-1].start()
        lane = lax.broadcasted_iota(jnp.int32, (length, LANES), 1)
        row = lax.broadcasted_iota(jnp.int32, (length, length), 0)
        col = lax.broadcasted_iota(jnp.int32, (length, length), 1)
        before = (row >= col).astype(BF)
        slot = lax.broadcasted_iota(jnp.int32, (length, 2 * room), 1) % room
        wanted = (slot + 1).astype(F32)

        def places(shares, first):
            routed = []
            for index in (first, first ^ 1):
                held = (lane == index) | (lane == index + experts) | (lane == index + 2 * experts)
                weight = jnp.sum(jnp.where(held, shares, 0.0), axis=1, keepdims=True)
                routed.append(jnp.broadcast_to((weight > 0).astype(F32), (length, room)))
            routed = jnp.concatenate(routed, axis=1)
            rank = dot(before, routed.astype(BF))
            return jnp.where((rank == wanted) & (routed > 0), 1.0, 0.0)

        for group in range(groups):
            for copy in copies[group * each : (group + 1) * each]:
                copy.wait()
            held_rows = slice(group * length, (group + 1) * length)
            lanes = rows_ref[held_rows, 2 * features :]
            place = places(lanes.astype(F32), expert_ref[0])
            if group == 0:
                place_ref[:, : 2 * room] = place.astype(BF)
                place_ref[:, 2 * room :] = places(lanes.astype(F32), expert_ref[0] ^ 2).astype(BF)
            pick = place.T.astype(BF)
            here = slice(group * room, (group + 1) * room)
            packed = dot(pick, lanes).astype(BF)
            lane_mine[here] = packed[:room]
            theirs_ref[here, 2 * features :] = packed[room:]
            for at in range(0, 2 * features, 512):
                packed = dot(pick, rows_ref[held_rows, at : at + 512]).astype(BF)
                mine_ref = token_mine if at < features else cot_mine
                mine_ref[here, at % features : at % features + 512] = packed[:room]
                theirs_ref[here, at : at + 512] = packed[room:]

    rows = jax.ShapeDtypeStruct((groups * room, features), BF)
    lanes = jax.ShapeDtypeStruct((groups * room, LANES), BF)
    theirs = jax.ShapeDtypeStruct((groups * room, width), BF)
    place = jax.ShapeDtypeStruct((length, 4 * room), BF)
    outs = (rows, rows, lanes, theirs, place)
    return pl.pallas_call(
        body,
        grid_spec=pltpu.PrefetchScalarGridSpec(
            num_scalar_prefetch=1,
            grid=(1,),
            in_specs=[ANYWHERE] * len(arrays),
            out_specs=[whole(a) for a in outs],
            scratch_shapes=[
                pltpu.VMEM((groups * length, width), BF),
                pltpu.SemaphoreType.DMA((len(pieces),)),
            ],
        ),
        out_shape=outs,
        compiler_params=params(1),
        cost_estimate=SMALL,
        name="plan_and_pack",
    )(expert, *arrays)


def spread(place, mine, theirs, far_mine, far_theirs):
    length, slots_of = place.shape
    room, features = far_mine.shape
    size = length // TOGETHER
    parts = (mine, theirs, far_mine, far_theirs)

    def body(place_ref, *refs):
        outs = refs[len(parts) :]
        for at in range(0, features, 512):
            cols = slice(at, at + 512)
            rows = jnp.concatenate([ref[:, cols] for ref in refs[: len(parts)]], axis=0)
            dense = dot(place_ref[...], rows).astype(BF)
            for i, out in enumerate(outs):
                out[:, cols] = dense[i * size : (i + 1) * size]

    out = jax.ShapeDtypeStruct((size, features), BF)
    return pl.pallas_call(
        body,
        grid=(1,),
        in_specs=[whole(place)] + [pl.BlockSpec((room, features), lambda i: (0, 0))] * len(parts),
        out_specs=[whole(out)] * TOGETHER,
        out_shape=(out,) * TOGETHER,
        compiler_params=params(1),
        cost_estimate=SMALL,
        name="spread",
    )(place, *parts)


def split3(value):
    high = value.astype(BF)
    rest = value - high.astype(F32)
    mid = rest.astype(BF)
    low = (rest - mid.astype(F32)).astype(BF)
    return high, mid, low


def after(value, *earlier):
    return lax.optimization_barrier((value, *earlier))[0]


def dense_plan(tokens, route_ids, gate_probs, out_cot, w_gate, w_up, w_down):
    experts = lax.axis_size("expert")
    tok_rows, features = tokens.shape
    hidden = w_gate.shape[2]
    top_count = route_ids.shape[1]
    capacity = max(2, tok_rows * top_count * 4 // (3 * experts))
    expert = lax.axis_index("expert").astype(jnp.int32)
    replica = lax.axis_index("replica").astype(jnp.int32)
    w_gate, w_up, w_down = w_gate[0], w_up[0], w_down[0]

    def to_core(rows):
        return lax.ppermute(rows, "expert", [(i, i ^ 1) for i in range(experts)])

    def to_x(rows):
        return lax.ppermute(rows, "expert", [(i, i ^ 2) for i in range(experts)])

    def to_z(rows, step):
        return lax.ppermute(
            rows, "expert", [(i, (i + 4 * step) % experts) for i in range(experts)]
        )

    def to_y(rows):
        return lax.ppermute(rows, "replica", [(0, 1), (1, 0)])

    chosen = route_ids[:, :, None] == jnp.arange(experts, dtype=jnp.int32)
    share = jnp.sum(jnp.where(chosen, gate_probs[:, :, None], 0.0), axis=1)
    pad = jnp.zeros((tok_rows, LANES - 3 * experts), BF)

    near = [jnp.concatenate([tokens, out_cot, *split3(share), pad], axis=1)]
    far, relay = [to_x(near[0])], [to_y(near[0])]
    near.append(to_z(near[0], 1))
    far.append(to_x(near[1]))
    near.append(after(to_z(near[1], 1), far[0], relay[0]))
    far.append(to_x(near[2]))
    near.append(to_z(near[2], 1))
    far.append(to_x(near[3]))
    relay += [to_y(far[0]), to_y(near[1]), to_y(far[1])]
    joined = jnp.concatenate([near[2], near[3], far[2], far[3]], axis=0)
    last = to_y(joined)
    own_pieces = [(a, 0) for a in near + far]
    other_pieces = [(relay[0], 0), (relay[2], 0), (last, 0), (last, 1)]
    other_pieces += [(relay[1], 0), (relay[3], 0), (last, 2), (last, 3)]
    expert_index = expert
    expert = expert.reshape(1)

    def plan(pieces, *earlier):
        return plan_and_pack(after(expert, *earlier), experts, capacity, tok_rows, pieces)

    def enter(packed):
        mine, cot_mine, mine_lanes, theirs, _ = packed
        theirs = to_core(theirs)
        x = jnp.concatenate([mine, theirs[:, :features]], axis=0)
        shares = jnp.concatenate([mine_lanes, theirs[:, 2 * features :]], axis=0)
        held = (jnp.arange(LANES) % experts == expert_index) & (jnp.arange(LANES) < 3 * experts)
        weight = jnp.sum(jnp.where(held, shares.astype(F32), 0.0), axis=1, keepdims=True)
        cot = jnp.concatenate([cot_mine, theirs[:, features : 2 * features]], axis=0)
        cot = (cot.astype(F32) * weight).astype(BF)
        pre_gate, pre_up = dot(x, w_gate), dot(x, w_up)
        act = (jax.nn.silu(pre_gate) * pre_up).astype(BF)
        return x, weight, pre_gate, pre_up, act, cot

    def leave(rows_of, before_mine=(), before_theirs=()):
        room = TOGETHER * capacity
        far_theirs = to_core(rows_of(slice(3 * room, None)))
        far_mine = rows_of(slice(room, 2 * room))
        theirs = to_core(rows_of(slice(2 * room, 3 * room)))
        mine = rows_of(slice(0, room))
        far_mine = to_x(after(far_mine, *before_mine))
        return mine, theirs, far_mine, to_x(after(far_theirs, *before_theirs))

    def home(place, parts):
        own, *others = spread(place, *parts)
        return [own] + [to_z(a, -step) for step, a in enumerate(others, 1)]

    def total(chunks):
        return sum(a.astype(F32) for a in chunks).astype(BF)

    def grads(x, act, cot, d_gate, d_up):
        x = lax.dynamic_slice_in_dim(x, replica * (features // 2), features // 2, 1)
        act = lax.dynamic_slice_in_dim(act, replica * (hidden // 2), hidden // 2, 1)
        return outer_sum(x, d_gate), outer_sum(x, d_up), outer_sum(act, cot)

    packed = plan(own_pieces, *relay[1:4])
    place = packed[-1]
    own_x, weight, pre_gate, pre_up, act, cot = enter(packed)
    parts = leave(lambda rows: (dot(act[rows], w_down) * weight[rows]).astype(BF))
    cot = after(cot, parts[0], parts[1])
    d_gate, d_up = hidden_grads(cot, pre_gate, pre_up, w_down)

    grad_parts = leave(
        lambda rows: input_rows(d_gate[rows], d_up[rows], w_gate, w_up), parts[2:3], parts[3:4]
    )
    chunks = home(after(place, grad_parts[0], grad_parts[1]), parts)
    own_grads = after((cot, d_gate, d_up), chunks[0])
    own = grads(own_x, act, *own_grads)
    packed = plan(other_pieces, *own, *grad_parts[2:], *chunks[1:])
    grad_chunks = home(after(place, packed[-1]), grad_parts)

    x, weight, pre_gate, pre_up, act, cot = enter(packed)
    d_gate, d_up = hidden_grads(cot, pre_gate, pre_up, w_down)
    other = grads(x, act, cot, d_gate, after(d_up, grad_chunks[1]))
    chunks, grad_chunks = after((chunks, grad_chunks), other[0])
    grad_gate, grad_up, grad_down = ((a + b).astype(BF)[None] for a, b in zip(own, other))
    return (total(chunks), total(grad_chunks), grad_gate, grad_up, grad_down)


def dense_fits(mesh):
    experts, replicas = mesh.shape["expert"], mesh.shape["replica"]
    return replicas == 2 and experts == 4 * TOGETHER


def solution(mesh):
    placed = (
        P(("expert", "replica"), None),
        P(("expert", "replica"), None),
        P(("expert", "replica"), None),
        P(("expert", "replica"), None),
        P("expert", None, None),
        P("expert", None, None),
        P("expert", None, None),
    )
    return jax.shard_map(
        dense_plan if dense_fits(mesh) else routed_plan,
        mesh=mesh,
        in_specs=placed,
        out_specs=(
            P(("expert", "replica"), None),
            P(("expert", "replica"), None),
            P("expert", "replica", None),
            P("expert", "replica", None),
            P("expert", "replica", None),
        ),
        check_vma=False,
    )
```

```python
import jax
import jax.numpy as jnp
from jax import lax
from jax.experimental import pallas as pl
from jax.experimental.pallas import tpu as pltpu
from jax.sharding import PartitionSpec as P

BF = jnp.bfloat16
F32 = jnp.float32
VMEM = 56 * 1024 * 1024
TOGETHER = 4
LANES = 128
SMALL = pl.CostEstimate(flops=1, bytes_accessed=1, transcendentals=0)


def slots(routes, experts, capacity):
    flat_ids = routes.reshape(-1)
    one_hot = (flat_ids[:, None] == jnp.arange(experts, dtype=jnp.int32)[None, :]).astype(jnp.int32)
    before = jnp.cumsum(one_hot, axis=0) - one_hot
    slot_rank = jnp.sum(before * one_hot, axis=1)
    return flat_ids * capacity + slot_rank


def place(token_rows, positions, total_rows):
    return (
        jnp.zeros((total_rows, token_rows.shape[1]), token_rows.dtype).at[positions].set(token_rows)
    )


def hidden_rows(token_rows, gate_weight, up_weight):
    pre_gate = jnp.dot(token_rows, gate_weight, preferred_element_type=F32)
    pre_up = jnp.dot(token_rows, up_weight, preferred_element_type=F32)
    activation = (jax.nn.silu(pre_gate) * pre_up).astype(BF)
    return (pre_gate, pre_up, activation)


CONTRACT = (((1,), (1,)), ((), ()))


def hidden_grads(grad_rows, pre_gate, pre_up, down_weight):
    d_hidden = lax.dot_general(grad_rows, down_weight, CONTRACT, preferred_element_type=F32)
    sigmoid_gate = jax.nn.sigmoid(pre_gate)
    d_gate = (d_hidden * pre_up * sigmoid_gate * (1.0 + pre_gate * (1.0 - sigmoid_gate))).astype(BF)
    d_up = (d_hidden * pre_gate * sigmoid_gate).astype(BF)
    return d_gate, d_up


def input_rows(d_gate, d_up, gate_weight, up_weight):
    back_rows = lax.dot_general(d_gate, gate_weight, CONTRACT, preferred_element_type=F32)
    back_rows = back_rows + lax.dot_general(d_up, up_weight, CONTRACT, preferred_element_type=F32)
    return back_rows.astype(BF)


def outer_sum(left, right):
    return lax.dot_general(left, right, (((0,), (0,)), ((), ())), preferred_element_type=F32)


def routed_plan(tokens, route_ids, gate_probs, out_cot, w_gate, w_up, w_down):
    experts = lax.axis_size("expert")
    tok_rows, features = tokens.shape
    top_count = route_ids.shape[1]
    hidden = w_gate.shape[2]
    capacity = max(2, tok_rows * top_count * 4 // (3 * experts))
    total_rows = experts * capacity
    positions = slots(route_ids, experts, capacity)
    gate_weight, up_weight, down_weight = w_gate[0], w_up[0], w_down[0]

    def exchange(rows):
        blocks = rows.reshape(experts, capacity, features)
        return lax.all_to_all(blocks, "expert", 0, 0, tiled=True).reshape(-1, features)

    received = exchange(place(jnp.repeat(tokens, top_count, axis=0), positions, total_rows))
    pre_gate, pre_up, activation = hidden_rows(received, gate_weight, up_weight)
    result = jnp.dot(activation, down_weight, preferred_element_type=F32).astype(BF)
    picked = exchange(result)[positions].reshape(tok_rows, top_count, features)
    combined = jnp.einsum("tk,tkd->td", gate_probs, picked.astype(F32)).astype(BF)
    scaled = (gate_probs[:, :, None] * out_cot[:, None, :].astype(F32)).astype(BF)
    grads_in = exchange(place(scaled.reshape(-1, features), positions, total_rows))
    d_gate, d_up = hidden_grads(grads_in, pre_gate, pre_up, down_weight)
    back = exchange(input_rows(d_gate, d_up, gate_weight, up_weight))
    grad_tokens = jnp.sum(
        back[positions].reshape(tok_rows, top_count, features).astype(F32), axis=1
    ).astype(BF)
    gate_up_sum = lax.psum_scatter(
        outer_sum(received, jnp.concatenate([d_gate, d_up], axis=1)).astype(BF),
        "replica",
        scatter_dimension=0,
        tiled=True,
    )
    down_sum = lax.psum_scatter(
        outer_sum(activation, grads_in).astype(BF), "replica", scatter_dimension=0, tiled=True
    )
    return (
        combined,
        grad_tokens,
        gate_up_sum[:, :hidden][None],
        gate_up_sum[:, hidden:][None],
        down_sum[None],
    )

def dot(left, right):
    return jnp.dot(left, right, preferred_element_type=F32)


def whole(array):
    return pl.BlockSpec(array.shape, lambda *_: (0,) * array.ndim)


def params(steps=0):
    order = ("arbitrary",) * steps if steps else None
    return pltpu.CompilerParams(dimension_semantics=order, vmem_limit_bytes=VMEM)


ANYWHERE = pl.BlockSpec(memory_space=pl.ANY)


def plan_and_pack(expert, experts, capacity, tok_rows, pieces):
    arrays = []
    for array, _ in pieces:
        if not any(array is a for a in arrays):
            arrays.append(array)
    sources = [
        (next(k for k, a in enumerate(arrays) if a is array), chunk) for array, chunk in pieces
    ]
    width = arrays[0].shape[1]
    features = (width - LANES) // 2
    groups, each = 2, len(pieces) // 2
    length, room = TOGETHER * tok_rows, TOGETHER * capacity

    def body(expert_ref, *refs):
        outs = refs[len(arrays) :]
        token_mine, cot_mine, lane_mine, theirs_ref, place_ref, rows_ref, sems = outs
        copies = []
        for i, (source, chunk) in enumerate(sources):
            copies.append(
                pltpu.make_async_copy(
                    refs[source].at[chunk * tok_rows : (chunk + 1) * tok_rows],
                    rows_ref.at[i * tok_rows : (i + 1) * tok_rows],
                    sems.at[i],
                )
            )
            copies[-1].start()
        lane = lax.broadcasted_iota(jnp.int32, (length, LANES), 1)
        row = lax.broadcasted_iota(jnp.int32, (length, length), 0)
        col = lax.broadcasted_iota(jnp.int32, (length, length), 1)
        before = (row >= col).astype(BF)
        slot = lax.broadcasted_iota(jnp.int32, (length, 2 * room), 1) % room
        wanted = (slot + 1).astype(F32)

        def places(shares, first):
            routed = []
            for index in (first, first ^ 1):
                held = (lane == index) | (lane == index + experts) | (lane == index + 2 * experts)
                weight = jnp.sum(jnp.where(held, shares, 0.0), axis=1, keepdims=True)
                routed.append(jnp.broadcast_to((weight > 0).astype(F32), (length, room)))
            routed = jnp.concatenate(routed, axis=1)
            rank = dot(before, routed.astype(BF))
            return jnp.where((rank == wanted) & (routed > 0), 1.0, 0.0)

        for group in range(groups):
            for copy in copies[group * each : (group + 1) * each]:
                copy.wait()
            held_rows = slice(group * length, (group + 1) * length)
            lanes = rows_ref[held_rows, 2 * features :]
            place = places(lanes.astype(F32), expert_ref[0])
            if group == 0:
                place_ref[:, : 2 * room] = place.astype(BF)
                place_ref[:, 2 * room :] = places(lanes.astype(F32), expert_ref[0] ^ 2).astype(BF)
            pick = place.T.astype(BF)
            here = slice(group * room, (group + 1) * room)
            packed = dot(pick, lanes).astype(BF)
            lane_mine[here] = packed[:room]
            theirs_ref[here, 2 * features :] = packed[room:]
            for at in range(0, 2 * features, 512):
                packed = dot(pick, rows_ref[held_rows, at : at + 512]).astype(BF)
                mine_ref = token_mine if at < features else cot_mine
                mine_ref[here, at % features : at % features + 512] = packed[:room]
                theirs_ref[here, at : at + 512] = packed[room:]

    rows = jax.ShapeDtypeStruct((groups * room, features), BF)
    lanes = jax.ShapeDtypeStruct((groups * room, LANES), BF)
    theirs = jax.ShapeDtypeStruct((groups * room, width), BF)
    place = jax.ShapeDtypeStruct((length, 4 * room), BF)
    outs = (rows, rows, lanes, theirs, place)
    return pl.pallas_call(
        body,
        grid_spec=pltpu.PrefetchScalarGridSpec(
            num_scalar_prefetch=1,
            grid=(1,),
            in_specs=[ANYWHERE] * len(arrays),
            out_specs=[whole(a) for a in outs],
            scratch_shapes=[
                pltpu.VMEM((groups * length, width), BF),
                pltpu.SemaphoreType.DMA((len(pieces),)),
            ],
        ),
        out_shape=outs,
        compiler_params=params(1),
        cost_estimate=SMALL,
        name="plan_and_pack",
    )(expert, *arrays)


def spread(place, mine, theirs, far_mine, far_theirs):
    length, slots_of = place.shape
    room, features = far_mine.shape
    size = length // TOGETHER
    parts = (mine, theirs, far_mine, far_theirs)

    def body(place_ref, *refs):
        outs = refs[len(parts) :]
        for at in range(0, features, 512):
            cols = slice(at, at + 512)
            rows = jnp.concatenate([ref[:, cols] for ref in refs[: len(parts)]], axis=0)
            dense = dot(place_ref[...], rows).astype(BF)
            for i, out in enumerate(outs):
                out[:, cols] = dense[i * size : (i + 1) * size]

    out = jax.ShapeDtypeStruct((size, features), BF)
    return pl.pallas_call(
        body,
        grid=(1,),
        in_specs=[whole(place)] + [pl.BlockSpec((room, features), lambda i: (0, 0))] * len(parts),
        out_specs=[whole(out)] * TOGETHER,
        out_shape=(out,) * TOGETHER,
        compiler_params=params(1),
        cost_estimate=SMALL,
        name="spread",
    )(place, *parts)


def pair_up(tokens, cots, route_ids, gate_probs, experts):
    tok_rows, features = tokens.shape

    def body(tokens_ref, cots_ref, ids_ref, probs_ref, out_ref):
        out_ref[:, :features] = tokens_ref[...]
        out_ref[:, features : 2 * features] = cots_ref[...]
        lane = lax.broadcasted_iota(jnp.int32, (tok_rows, LANES), 1)
        share = jnp.zeros((tok_rows, LANES), F32)
        for k in range(ids_ref.shape[1]):
            chosen = ids_ref[:, k : k + 1] == lane % experts
            share = share + jnp.where(chosen, probs_ref[:, k : k + 1], 0.0)
        high = share.astype(BF).astype(F32)
        mid = (share - high).astype(BF).astype(F32)
        low = share - high - mid
        term = jnp.where(lane < experts, high, jnp.where(lane < 2 * experts, mid, low))
        out_ref[:, 2 * features :] = jnp.where(lane < 3 * experts, term, 0.0).astype(BF)

    out = jax.ShapeDtypeStruct((tok_rows, 2 * features + LANES), BF)
    return pl.pallas_call(
        body,
        out_shape=out,
        compiler_params=params(),
        cost_estimate=SMALL,
        name="pair_up",
    )(tokens, cots, route_ids, gate_probs)


def after(value, *earlier):
    return lax.optimization_barrier((value, *earlier))[0]


def dense_plan(tokens, route_ids, gate_probs, out_cot, w_gate, w_up, w_down):
    experts = lax.axis_size("expert")
    tok_rows, features = tokens.shape
    hidden = w_gate.shape[2]
    capacity = max(2, tok_rows * route_ids.shape[1] * 4 // (3 * experts))
    expert = lax.axis_index("expert").astype(jnp.int32)
    replica = lax.axis_index("replica").astype(jnp.int32)
    w_gate, w_up, w_down = w_gate[0], w_up[0], w_down[0]

    def to_core(rows):
        return lax.ppermute(rows, "expert", [(i, i ^ 1) for i in range(experts)])

    def to_x(rows):
        return lax.ppermute(rows, "expert", [(i, i ^ 2) for i in range(experts)])

    def to_z(rows, step):
        return lax.ppermute(
            rows, "expert", [(i, (i + 4 * step) % experts) for i in range(experts)]
        )

    def to_y(rows):
        return lax.ppermute(rows, "replica", [(0, 1), (1, 0)])

    near = [pair_up(tokens, out_cot, route_ids, gate_probs, experts)]
    far, relay = [to_x(near[0])], [to_y(near[0])]
    near.append(to_z(near[0], 1))
    far.append(to_x(near[1]))
    near.append(after(to_z(near[1], 1), far[0], relay[0]))
    far.append(to_x(near[2]))
    near.append(to_z(near[2], 1))
    far.append(to_x(near[3]))
    relay += [to_y(far[0]), to_y(near[1]), to_y(far[1])]
    joined = jnp.concatenate([near[2], near[3], far[2], far[3]], axis=0)
    last = to_y(joined)
    own_pieces = [(a, 0) for a in near + far]
    other_pieces = [(relay[0], 0), (relay[2], 0), (last, 0), (last, 1)]
    other_pieces += [(relay[1], 0), (relay[3], 0), (last, 2), (last, 3)]
    expert_index = expert
    expert = expert.reshape(1)

    def plan(pieces, *earlier):
        return plan_and_pack(after(expert, *earlier), experts, capacity, tok_rows, pieces)

    def enter(packed):
        mine, cot_mine, mine_lanes, theirs, _ = packed
        theirs = to_core(theirs)
        x = jnp.concatenate([mine, theirs[:, :features]], axis=0)
        shares = jnp.concatenate([mine_lanes, theirs[:, 2 * features :]], axis=0)
        held = (jnp.arange(LANES) % experts == expert_index) & (jnp.arange(LANES) < 3 * experts)
        weight = jnp.sum(jnp.where(held, shares.astype(F32), 0.0), axis=1, keepdims=True)
        cot = jnp.concatenate([cot_mine, theirs[:, features : 2 * features]], axis=0)
        cot = (cot.astype(F32) * weight).astype(BF)
        pre_gate, pre_up = dot(x, w_gate), dot(x, w_up)
        act = (jax.nn.silu(pre_gate) * pre_up).astype(BF)
        return x, weight, pre_gate, pre_up, act, cot

    def leave(rows_of, before_mine=(), before_far=()):
        half = TOGETHER * capacity
        theirs = to_core(rows_of(slice(2 * half, None)))
        mine = rows_of(slice(0, 2 * half), *before_mine)
        return mine, theirs, to_x(after(mine[half:], *before_far)), to_x(theirs[half:])

    def home(place, parts):
        own, *others = spread(place, *parts)
        return [own] + [to_z(a, -step) for step, a in enumerate(others, 1)]

    def total(chunks):
        return sum(a.astype(F32) for a in chunks).astype(BF)

    def grads(x, act, cot, d_gate, d_up):
        x = lax.dynamic_slice_in_dim(x, replica * (features // 2), features // 2, 1)
        act = lax.dynamic_slice_in_dim(act, replica * (hidden // 2), hidden // 2, 1)
        return outer_sum(x, d_gate), outer_sum(x, d_up), outer_sum(act, cot)

    packed = plan(own_pieces, *relay[1:4], joined)
    place = packed[-1]
    own_x, weight, pre_gate, pre_up, act, cot = enter(packed)
    parts = leave(lambda rows: (dot(act[rows], w_down) * weight[rows]).astype(BF))
    cot = after(cot, parts[0], parts[1])
    d_gate, d_up = hidden_grads(cot, pre_gate, pre_up, w_down)

    def token_grads(rows, *earlier):
        return input_rows(*after((d_gate[rows], d_up[rows]), *earlier), w_gate, w_up)

    grad_parts = leave(token_grads, parts[2:3])
    chunks = home(after(place, grad_parts[0], grad_parts[1]), parts)
    own_grads = after((cot, d_gate, d_up), chunks[0])
    own = grads(own_x, act, *own_grads)
    packed = plan(other_pieces, *own, *grad_parts[2:], *chunks[1:3])
    grad_chunks = home(after(place, packed[-1]), grad_parts)

    x, weight, pre_gate, pre_up, act, cot = enter(packed)
    d_gate, d_up = hidden_grads(cot, pre_gate, pre_up, w_down)
    other = grads(x, act, cot, d_gate, after(d_up, grad_chunks[1]))
    chunks, grad_chunks = after((chunks, grad_chunks), other[0])
    grad_gate, grad_up, grad_down = ((a + b).astype(BF)[None] for a, b in zip(own, other))
    return (total(chunks), total(grad_chunks), grad_gate, grad_up, grad_down)


def dense_fits(mesh):
    experts, replicas = mesh.shape["expert"], mesh.shape["replica"]
    return replicas == 2 and experts == 4 * TOGETHER


def solution(mesh):
    placed = (
        P(("expert", "replica"), None),
        P(("expert", "replica"), None),
        P(("expert", "replica"), None),
        P(("expert", "replica"), None),
        P("expert", None, None),
        P("expert", None, None),
        P("expert", None, None),
    )
    return jax.shard_map(
        dense_plan if dense_fits(mesh) else routed_plan,
        mesh=mesh,
        in_specs=placed,
        out_specs=(
            P(("expert", "replica"), None),
            P(("expert", "replica"), None),
            P("expert", "replica", None),
            P("expert", "replica", None),
            P("expert", "replica", None),
        ),
        check_vma=False,
    )
```

```python
import jax
import jax.numpy as jnp
from jax import lax
from jax.experimental import pallas as pl
from jax.experimental.pallas import tpu as pltpu
from jax.sharding import PartitionSpec as P

BF = jnp.bfloat16
F32 = jnp.float32
VMEM = 56 * 1024 * 1024
TOGETHER = 4
LANES = 128
SMALL = pl.CostEstimate(flops=1, bytes_accessed=1, transcendentals=0)


def slots(routes, experts, capacity):
    flat_ids = routes.reshape(-1)
    one_hot = (flat_ids[:, None] == jnp.arange(experts, dtype=jnp.int32)[None, :]).astype(jnp.int32)
    before = jnp.cumsum(one_hot, axis=0) - one_hot
    slot_rank = jnp.sum(before * one_hot, axis=1)
    return flat_ids * capacity + slot_rank


def place(token_rows, positions, total_rows):
    return (
        jnp.zeros((total_rows, token_rows.shape[1]), token_rows.dtype).at[positions].set(token_rows)
    )


def hidden_rows(token_rows, gate_weight, up_weight):
    pre_gate = jnp.dot(token_rows, gate_weight, preferred_element_type=F32)
    pre_up = jnp.dot(token_rows, up_weight, preferred_element_type=F32)
    activation = (jax.nn.silu(pre_gate) * pre_up).astype(BF)
    return (pre_gate, pre_up, activation)


CONTRACT = (((1,), (1,)), ((), ()))


def hidden_grads(grad_rows, pre_gate, pre_up, down_weight):
    d_hidden = lax.dot_general(grad_rows, down_weight, CONTRACT, preferred_element_type=F32)
    sigmoid_gate = jax.nn.sigmoid(pre_gate)
    d_gate = (d_hidden * pre_up * sigmoid_gate * (1.0 + pre_gate * (1.0 - sigmoid_gate))).astype(BF)
    d_up = (d_hidden * pre_gate * sigmoid_gate).astype(BF)
    return d_gate, d_up


def input_rows(d_gate, d_up, gate_weight, up_weight):
    back_rows = lax.dot_general(d_gate, gate_weight, CONTRACT, preferred_element_type=F32)
    back_rows = back_rows + lax.dot_general(d_up, up_weight, CONTRACT, preferred_element_type=F32)
    return back_rows.astype(BF)


def outer_sum(left, right):
    return lax.dot_general(left, right, (((0,), (0,)), ((), ())), preferred_element_type=F32)


def routed_plan(tokens, route_ids, gate_probs, out_cot, w_gate, w_up, w_down):
    experts = lax.axis_size("expert")
    tok_rows, features = tokens.shape
    top_count = route_ids.shape[1]
    hidden = w_gate.shape[2]
    capacity = max(2, tok_rows * top_count * 4 // (3 * experts))
    total_rows = experts * capacity
    positions = slots(route_ids, experts, capacity)
    gate_weight, up_weight, down_weight = w_gate[0], w_up[0], w_down[0]

    def exchange(rows):
        blocks = rows.reshape(experts, capacity, features)
        return lax.all_to_all(blocks, "expert", 0, 0, tiled=True).reshape(-1, features)

    received = exchange(place(jnp.repeat(tokens, top_count, axis=0), positions, total_rows))
    pre_gate, pre_up, activation = hidden_rows(received, gate_weight, up_weight)
    result = jnp.dot(activation, down_weight, preferred_element_type=F32).astype(BF)
    picked = exchange(result)[positions].reshape(tok_rows, top_count, features)
    combined = jnp.einsum("tk,tkd->td", gate_probs, picked.astype(F32)).astype(BF)
    scaled = (gate_probs[:, :, None] * out_cot[:, None, :].astype(F32)).astype(BF)
    grads_in = exchange(place(scaled.reshape(-1, features), positions, total_rows))
    d_gate, d_up = hidden_grads(grads_in, pre_gate, pre_up, down_weight)
    back = exchange(input_rows(d_gate, d_up, gate_weight, up_weight))
    grad_tokens = jnp.sum(
        back[positions].reshape(tok_rows, top_count, features).astype(F32), axis=1
    ).astype(BF)
    gate_up_sum = lax.psum_scatter(
        outer_sum(received, jnp.concatenate([d_gate, d_up], axis=1)).astype(BF),
        "replica",
        scatter_dimension=0,
        tiled=True,
    )
    down_sum = lax.psum_scatter(
        outer_sum(activation, grads_in).astype(BF), "replica", scatter_dimension=0, tiled=True
    )
    return (
        combined,
        grad_tokens,
        gate_up_sum[:, :hidden][None],
        gate_up_sum[:, hidden:][None],
        down_sum[None],
    )

def dot(left, right):
    return jnp.dot(left, right, preferred_element_type=F32)


def whole(array):
    return pl.BlockSpec(array.shape, lambda *_: (0,) * array.ndim)


def params(steps=0):
    order = ("arbitrary",) * steps if steps else None
    return pltpu.CompilerParams(dimension_semantics=order, vmem_limit_bytes=VMEM)


ANYWHERE = pl.BlockSpec(memory_space=pl.ANY)


def plan_and_pack(expert, experts, capacity, tok_rows, pieces):
    arrays = []
    for array, _ in pieces:
        if not any(array is a for a in arrays):
            arrays.append(array)
    sources = [
        (next(k for k, a in enumerate(arrays) if a is array), chunk) for array, chunk in pieces
    ]
    width = arrays[0].shape[1]
    features = (width - LANES) // 2
    groups, each = 2, len(pieces) // 2
    length, room = TOGETHER * tok_rows, TOGETHER * capacity

    def body(expert_ref, *refs):
        outs = refs[len(arrays) :]
        token_mine, cot_mine, lane_mine, theirs_ref, place_ref, rows_ref, sems = outs
        copies = []
        for i, (source, chunk) in enumerate(sources):
            copies.append(
                pltpu.make_async_copy(
                    refs[source].at[chunk * tok_rows : (chunk + 1) * tok_rows],
                    rows_ref.at[i * tok_rows : (i + 1) * tok_rows],
                    sems.at[i],
                )
            )
            copies[-1].start()
        lane = lax.broadcasted_iota(jnp.int32, (length, LANES), 1)
        row = lax.broadcasted_iota(jnp.int32, (length, length), 0)
        col = lax.broadcasted_iota(jnp.int32, (length, length), 1)
        before = (row >= col).astype(BF)
        slot = lax.broadcasted_iota(jnp.int32, (length, 2 * room), 1) % room
        wanted = (slot + 1).astype(F32)

        def places(shares, first):
            routed = []
            for index in (first, first ^ 1):
                held = (lane == index) | (lane == index + experts) | (lane == index + 2 * experts)
                weight = jnp.sum(jnp.where(held, shares, 0.0), axis=1, keepdims=True)
                routed.append(jnp.broadcast_to((weight > 0).astype(F32), (length, room)))
            routed = jnp.concatenate(routed, axis=1)
            rank = dot(before, routed.astype(BF))
            return jnp.where((rank == wanted) & (routed > 0), 1.0, 0.0)

        for group in range(groups):
            for copy in copies[group * each : (group + 1) * each]:
                copy.wait()
            held_rows = slice(group * length, (group + 1) * length)
            lanes = rows_ref[held_rows, 2 * features :]
            place = places(lanes.astype(F32), expert_ref[0])
            if group == 0:
                place_ref[:, : 2 * room] = place.astype(BF)
                place_ref[:, 2 * room :] = places(lanes.astype(F32), expert_ref[0] ^ 2).astype(BF)
            pick = place.T.astype(BF)
            here = slice(group * room, (group + 1) * room)
            packed = dot(pick, lanes).astype(BF)
            lane_mine[here] = packed[:room]
            theirs_ref[here, 2 * features :] = packed[room:]
            for at in range(0, 2 * features, 512):
                packed = dot(pick, rows_ref[held_rows, at : at + 512]).astype(BF)
                mine_ref = token_mine if at < features else cot_mine
                mine_ref[here, at % features : at % features + 512] = packed[:room]
                theirs_ref[here, at : at + 512] = packed[room:]

    rows = jax.ShapeDtypeStruct((groups * room, features), BF)
    lanes = jax.ShapeDtypeStruct((groups * room, LANES), BF)
    theirs = jax.ShapeDtypeStruct((groups * room, width), BF)
    place = jax.ShapeDtypeStruct((length, 4 * room), BF)
    outs = (rows, rows, lanes, theirs, place)
    return pl.pallas_call(
        body,
        grid_spec=pltpu.PrefetchScalarGridSpec(
            num_scalar_prefetch=1,
            grid=(1,),
            in_specs=[ANYWHERE] * len(arrays),
            out_specs=[whole(a) for a in outs],
            scratch_shapes=[
                pltpu.VMEM((groups * length, width), BF),
                pltpu.SemaphoreType.DMA((len(pieces),)),
            ],
        ),
        out_shape=outs,
        compiler_params=params(1),
        cost_estimate=SMALL,
        name="plan_and_pack",
    )(expert, *arrays)


def spread(place, mine, theirs, far_mine, far_theirs):
    length, slots_of = place.shape
    room, features = far_mine.shape
    size = length // TOGETHER
    parts = (mine, theirs, far_mine, far_theirs)

    def body(place_ref, *refs):
        outs = refs[len(parts) :]
        for at in range(0, features, 512):
            cols = slice(at, at + 512)
            rows = jnp.concatenate([ref[:, cols] for ref in refs[: len(parts)]], axis=0)
            dense = dot(place_ref[...], rows).astype(BF)
            for i, out in enumerate(outs):
                out[:, cols] = dense[i * size : (i + 1) * size]

    out = jax.ShapeDtypeStruct((size, features), BF)
    return pl.pallas_call(
        body,
        grid=(1,),
        in_specs=[whole(place)] + [pl.BlockSpec((room, features), lambda i: (0, 0))] * len(parts),
        out_specs=[whole(out)] * TOGETHER,
        out_shape=(out,) * TOGETHER,
        compiler_params=params(1),
        cost_estimate=SMALL,
        name="spread",
    )(place, *parts)


def pair_up(tokens, cots, route_ids, gate_probs, experts):
    tok_rows, features = tokens.shape

    def body(tokens_ref, cots_ref, ids_ref, probs_ref, out_ref):
        out_ref[:, :features] = tokens_ref[...]
        out_ref[:, features : 2 * features] = cots_ref[...]
        row = lax.broadcasted_iota(jnp.int32, (LANES, tok_rows), 0)
        share = jnp.zeros((LANES, tok_rows), F32)
        for k in range(ids_ref.shape[0]):
            chosen = ids_ref[k : k + 1, :] == row % experts
            share = share + jnp.where(chosen, probs_ref[k : k + 1, :], 0.0)
        high = share.astype(BF).astype(F32)
        mid = (share - high).astype(BF).astype(F32)
        low = share - high - mid
        term = jnp.where(row < experts, high, jnp.where(row < 2 * experts, mid, low))
        term = jnp.where(row < 3 * experts, term, 0.0)
        rest = jnp.zeros((LANES, LANES - tok_rows), F32)
        out_ref[:, 2 * features :] = jnp.concatenate([term, rest], axis=1).T[:tok_rows].astype(BF)

    out = jax.ShapeDtypeStruct((tok_rows, 2 * features + LANES), BF)
    return pl.pallas_call(
        body,
        out_shape=out,
        compiler_params=params(),
        cost_estimate=SMALL,
        name="pair_up",
    )(tokens, cots, route_ids.T, gate_probs.T)


def after(value, *earlier):
    return lax.optimization_barrier((value, *earlier))[0]


def dense_plan(tokens, route_ids, gate_probs, out_cot, w_gate, w_up, w_down):
    experts = lax.axis_size("expert")
    tok_rows, features = tokens.shape
    hidden = w_gate.shape[2]
    capacity = max(2, tok_rows * route_ids.shape[1] * 4 // (3 * experts))
    expert = lax.axis_index("expert").astype(jnp.int32)
    replica = lax.axis_index("replica").astype(jnp.int32)
    w_gate, w_up, w_down = w_gate[0], w_up[0], w_down[0]

    def to_core(rows):
        return lax.ppermute(rows, "expert", [(i, i ^ 1) for i in range(experts)])

    def to_x(rows):
        return lax.ppermute(rows, "expert", [(i, i ^ 2) for i in range(experts)])

    def to_z(rows, step):
        return lax.ppermute(
            rows, "expert", [(i, (i + 4 * step) % experts) for i in range(experts)]
        )

    def to_y(rows):
        return lax.ppermute(rows, "replica", [(0, 1), (1, 0)])

    near = [pair_up(tokens, out_cot, route_ids, gate_probs, experts)]
    far, relay = [to_x(near[0])], [to_y(near[0])]
    near.append(to_z(near[0], 1))
    far.append(to_x(near[1]))
    near.append(after(to_z(near[1], 1), far[0], relay[0]))
    far.append(to_x(near[2]))
    near.append(to_z(near[2], 1))
    far.append(to_x(near[3]))
    relay += [to_y(far[0]), to_y(near[1]), to_y(far[1])]
    joined = jnp.concatenate([near[2], near[3], far[2], far[3]], axis=0)
    last = to_y(joined)
    own_pieces = [(a, 0) for a in near + far]
    other_pieces = [(relay[0], 0), (relay[2], 0), (last, 0), (last, 1)]
    other_pieces += [(relay[1], 0), (relay[3], 0), (last, 2), (last, 3)]
    expert_index = expert
    expert = expert.reshape(1)

    def plan(pieces, *earlier):
        return plan_and_pack(after(expert, *earlier), experts, capacity, tok_rows, pieces)

    def enter(packed):
        mine, cot_mine, mine_lanes, theirs, _ = packed
        theirs = to_core(theirs)
        x = jnp.concatenate([mine, theirs[:, :features]], axis=0)
        shares = jnp.concatenate([mine_lanes, theirs[:, 2 * features :]], axis=0)
        held = (jnp.arange(LANES) % experts == expert_index) & (jnp.arange(LANES) < 3 * experts)
        weight = jnp.sum(jnp.where(held, shares.astype(F32), 0.0), axis=1, keepdims=True)
        cot = jnp.concatenate([cot_mine, theirs[:, features : 2 * features]], axis=0)
        cot = (cot.astype(F32) * weight).astype(BF)
        pre_gate, pre_up = dot(x, w_gate), dot(x, w_up)
        act = (jax.nn.silu(pre_gate) * pre_up).astype(BF)
        return x, weight, pre_gate, pre_up, act, cot

    def leave(rows_of, before_mine=(), before_far=()):
        half = TOGETHER * capacity
        theirs = to_core(rows_of(slice(2 * half, None)))
        mine = rows_of(slice(0, 2 * half), *before_mine)
        return mine, theirs, to_x(after(mine[half:], *before_far)), to_x(theirs[half:])

    def home(place, parts):
        own, *others = spread(place, *parts)
        return [own] + [to_z(a, -step) for step, a in enumerate(others, 1)]

    def total(chunks):
        return sum(a.astype(F32) for a in chunks).astype(BF)

    def grads(x, act, cot, d_gate, d_up):
        x = lax.dynamic_slice_in_dim(x, replica * (features // 2), features // 2, 1)
        act = lax.dynamic_slice_in_dim(act, replica * (hidden // 2), hidden // 2, 1)
        return outer_sum(x, d_gate), outer_sum(x, d_up), outer_sum(act, cot)

    packed = plan(own_pieces, *relay[1:4], joined)
    place = packed[-1]
    own_x, weight, pre_gate, pre_up, act, cot = enter(packed)
    parts = leave(lambda rows: (dot(act[rows], w_down) * weight[rows]).astype(BF))
    cot = after(cot, parts[0], parts[1])
    d_gate, d_up = hidden_grads(cot, pre_gate, pre_up, w_down)

    def token_grads(rows, *earlier):
        return input_rows(*after((d_gate[rows], d_up[rows]), *earlier), w_gate, w_up)

    grad_parts = leave(token_grads, parts[2:3])
    chunks = home(after(place, grad_parts[0], grad_parts[1]), parts)
    own_grads = after((cot, d_gate, d_up), chunks[0])
    own = grads(own_x, act, *own_grads)
    packed = list(plan(other_pieces, *own, grad_parts[2]))
    packed[3] = after(packed[3], grad_parts[3], *chunks[1:])
    grad_chunks = home(after(place, packed[-1]), grad_parts)

    x, weight, pre_gate, pre_up, act, cot = enter(packed)
    d_gate, d_up = hidden_grads(cot, pre_gate, pre_up, w_down)
    other = grads(x, act, cot, d_gate, after(d_up, grad_chunks[1]))
    chunks, grad_chunks = after((chunks, grad_chunks), other[0])
    grad_gate, grad_up, grad_down = ((a + b).astype(BF)[None] for a, b in zip(own, other))
    return (total(chunks), total(grad_chunks), grad_gate, grad_up, grad_down)


def dense_fits(mesh):
    experts, replicas = mesh.shape["expert"], mesh.shape["replica"]
    return replicas == 2 and experts == 4 * TOGETHER


def solution(mesh):
    placed = (
        P(("expert", "replica"), None),
        P(("expert", "replica"), None),
        P(("expert", "replica"), None),
        P(("expert", "replica"), None),
        P("expert", None, None),
        P("expert", None, None),
        P("expert", None, None),
    )
    return jax.shard_map(
        dense_plan if dense_fits(mesh) else routed_plan,
        mesh=mesh,
        in_specs=placed,
        out_specs=(
            P(("expert", "replica"), None),
            P(("expert", "replica"), None),
            P("expert", "replica", None),
            P("expert", "replica", None),
            P("expert", "replica", None),
        ),
        check_vma=False,
    )
```

```python
import jax
import jax.numpy as jnp
from jax import lax
from jax.experimental import pallas as pl
from jax.experimental.pallas import tpu as pltpu
from jax.sharding import PartitionSpec as P

BF = jnp.bfloat16
F32 = jnp.float32
VMEM = 56 * 1024 * 1024
TOGETHER = 4
LANES = 128
SMALL = pl.CostEstimate(flops=1, bytes_accessed=1, transcendentals=0)


def slots(routes, experts, capacity):
    flat_ids = routes.reshape(-1)
    one_hot = (flat_ids[:, None] == jnp.arange(experts, dtype=jnp.int32)[None, :]).astype(jnp.int32)
    before = jnp.cumsum(one_hot, axis=0) - one_hot
    slot_rank = jnp.sum(before * one_hot, axis=1)
    return flat_ids * capacity + slot_rank


def place(token_rows, positions, total_rows):
    return (
        jnp.zeros((total_rows, token_rows.shape[1]), token_rows.dtype).at[positions].set(token_rows)
    )


def hidden_rows(token_rows, gate_weight, up_weight):
    pre_gate = jnp.dot(token_rows, gate_weight, preferred_element_type=F32)
    pre_up = jnp.dot(token_rows, up_weight, preferred_element_type=F32)
    activation = (jax.nn.silu(pre_gate) * pre_up).astype(BF)
    return (pre_gate, pre_up, activation)


CONTRACT = (((1,), (1,)), ((), ()))


def hidden_grads(grad_rows, pre_gate, pre_up, down_weight):
    d_hidden = lax.dot_general(grad_rows, down_weight, CONTRACT, preferred_element_type=F32)
    sigmoid_gate = jax.nn.sigmoid(pre_gate)
    d_gate = (d_hidden * pre_up * sigmoid_gate * (1.0 + pre_gate * (1.0 - sigmoid_gate))).astype(BF)
    d_up = (d_hidden * pre_gate * sigmoid_gate).astype(BF)
    return d_gate, d_up


def input_rows(d_gate, d_up, gate_weight, up_weight):
    back_rows = lax.dot_general(d_gate, gate_weight, CONTRACT, preferred_element_type=F32)
    back_rows = back_rows + lax.dot_general(d_up, up_weight, CONTRACT, preferred_element_type=F32)
    return back_rows.astype(BF)


def outer_sum(left, right):
    return lax.dot_general(left, right, (((0,), (0,)), ((), ())), preferred_element_type=F32)


def routed_plan(tokens, route_ids, gate_probs, out_cot, w_gate, w_up, w_down):
    experts = lax.axis_size("expert")
    tok_rows, features = tokens.shape
    top_count = route_ids.shape[1]
    hidden = w_gate.shape[2]
    capacity = max(2, tok_rows * top_count * 4 // (3 * experts))
    total_rows = experts * capacity
    positions = slots(route_ids, experts, capacity)
    gate_weight, up_weight, down_weight = w_gate[0], w_up[0], w_down[0]

    def exchange(rows):
        blocks = rows.reshape(experts, capacity, features)
        return lax.all_to_all(blocks, "expert", 0, 0, tiled=True).reshape(-1, features)

    received = exchange(place(jnp.repeat(tokens, top_count, axis=0), positions, total_rows))
    pre_gate, pre_up, activation = hidden_rows(received, gate_weight, up_weight)
    result = jnp.dot(activation, down_weight, preferred_element_type=F32).astype(BF)
    picked = exchange(result)[positions].reshape(tok_rows, top_count, features)
    combined = jnp.einsum("tk,tkd->td", gate_probs, picked.astype(F32)).astype(BF)
    scaled = (gate_probs[:, :, None] * out_cot[:, None, :].astype(F32)).astype(BF)
    grads_in = exchange(place(scaled.reshape(-1, features), positions, total_rows))
    d_gate, d_up = hidden_grads(grads_in, pre_gate, pre_up, down_weight)
    back = exchange(input_rows(d_gate, d_up, gate_weight, up_weight))
    grad_tokens = jnp.sum(
        back[positions].reshape(tok_rows, top_count, features).astype(F32), axis=1
    ).astype(BF)
    gate_up_sum = lax.psum_scatter(
        outer_sum(received, jnp.concatenate([d_gate, d_up], axis=1)).astype(BF),
        "replica",
        scatter_dimension=0,
        tiled=True,
    )
    down_sum = lax.psum_scatter(
        outer_sum(activation, grads_in).astype(BF), "replica", scatter_dimension=0, tiled=True
    )
    return (
        combined,
        grad_tokens,
        gate_up_sum[:, :hidden][None],
        gate_up_sum[:, hidden:][None],
        down_sum[None],
    )

def dot(left, right):
    return jnp.dot(left, right, preferred_element_type=F32)


def whole(array):
    return pl.BlockSpec(array.shape, lambda *_: (0,) * array.ndim)


def params(steps=0):
    order = ("arbitrary",) * steps if steps else None
    return pltpu.CompilerParams(dimension_semantics=order, vmem_limit_bytes=VMEM)


ANYWHERE = pl.BlockSpec(memory_space=pl.ANY)


def plan_and_pack(expert, experts, capacity, tok_rows, pieces):
    arrays = []
    for array, _ in pieces:
        if not any(array is a for a in arrays):
            arrays.append(array)
    sources = [
        (next(k for k, a in enumerate(arrays) if a is array), chunk) for array, chunk in pieces
    ]
    width = arrays[0].shape[1]
    features = (width - LANES) // 2
    groups, each = 2, len(pieces) // 2
    length, room = TOGETHER * tok_rows, TOGETHER * capacity

    def body(expert_ref, *refs):
        outs = refs[len(arrays) :]
        token_mine, cot_mine, lane_mine, theirs_ref, place_ref, rows_ref, sems = outs
        copies = []
        for i, (source, chunk) in enumerate(sources):
            copies.append(
                pltpu.make_async_copy(
                    refs[source].at[chunk * tok_rows : (chunk + 1) * tok_rows],
                    rows_ref.at[i * tok_rows : (i + 1) * tok_rows],
                    sems.at[i],
                )
            )
            copies[-1].start()
        lane = lax.broadcasted_iota(jnp.int32, (length, LANES), 1)
        row = lax.broadcasted_iota(jnp.int32, (length, length), 0)
        col = lax.broadcasted_iota(jnp.int32, (length, length), 1)
        before = (row >= col).astype(BF)
        slot = lax.broadcasted_iota(jnp.int32, (length, 2 * room), 1) % room
        wanted = (slot + 1).astype(F32)

        def places(shares, first):
            routed = []
            for index in (first, first ^ 1):
                held = (lane == index) | (lane == index + experts) | (lane == index + 2 * experts)
                weight = jnp.sum(jnp.where(held, shares, 0.0), axis=1, keepdims=True)
                routed.append(jnp.broadcast_to((weight > 0).astype(F32), (length, room)))
            routed = jnp.concatenate(routed, axis=1)
            rank = dot(before, routed.astype(BF))
            return jnp.where((rank == wanted) & (routed > 0), 1.0, 0.0)

        for group in range(groups):
            for copy in copies[group * each : (group + 1) * each]:
                copy.wait()
            held_rows = slice(group * length, (group + 1) * length)
            lanes = rows_ref[held_rows, 2 * features :]
            place = places(lanes.astype(F32), expert_ref[0])
            if group == 0:
                place_ref[:, : 2 * room] = place.astype(BF)
                place_ref[:, 2 * room :] = places(lanes.astype(F32), expert_ref[0] ^ 2).astype(BF)
            pick = place.T.astype(BF)
            here = slice(group * room, (group + 1) * room)
            packed = dot(pick, lanes).astype(BF)
            lane_mine[here] = packed[:room]
            theirs_ref[here, 2 * features :] = packed[room:]
            for at in range(0, 2 * features, 512):
                packed = dot(pick, rows_ref[held_rows, at : at + 512]).astype(BF)
                mine_ref = token_mine if at < features else cot_mine
                mine_ref[here, at % features : at % features + 512] = packed[:room]
                theirs_ref[here, at : at + 512] = packed[room:]

    rows = jax.ShapeDtypeStruct((groups * room, features), BF)
    lanes = jax.ShapeDtypeStruct((groups * room, LANES), BF)
    theirs = jax.ShapeDtypeStruct((groups * room, width), BF)
    place = jax.ShapeDtypeStruct((length, 4 * room), BF)
    outs = (rows, rows, lanes, theirs, place)
    return pl.pallas_call(
        body,
        grid_spec=pltpu.PrefetchScalarGridSpec(
            num_scalar_prefetch=1,
            grid=(1,),
            in_specs=[ANYWHERE] * len(arrays),
            out_specs=[whole(a) for a in outs],
            scratch_shapes=[
                pltpu.VMEM((groups * length, width), BF),
                pltpu.SemaphoreType.DMA((len(pieces),)),
            ],
        ),
        out_shape=outs,
        compiler_params=params(1),
        cost_estimate=SMALL,
        name="plan_and_pack",
    )(expert, *arrays)


def spread(place, mine, theirs, far_mine, far_theirs):
    length, slots_of = place.shape
    room, features = far_mine.shape
    size = length // TOGETHER
    parts = (mine, theirs, far_mine, far_theirs)

    def body(place_ref, *refs):
        outs = refs[len(parts) :]
        for at in range(0, features, 512):
            cols = slice(at, at + 512)
            rows = jnp.concatenate([ref[:, cols] for ref in refs[: len(parts)]], axis=0)
            dense = dot(place_ref[...], rows).astype(BF)
            for i, out in enumerate(outs):
                out[:, cols] = dense[i * size : (i + 1) * size]

    out = jax.ShapeDtypeStruct((size, features), BF)
    return pl.pallas_call(
        body,
        grid=(1,),
        in_specs=[whole(place)] + [pl.BlockSpec((room, features), lambda i: (0, 0))] * len(parts),
        out_specs=[whole(out)] * TOGETHER,
        out_shape=(out,) * TOGETHER,
        compiler_params=params(1),
        cost_estimate=SMALL,
        name="spread",
    )(place, *parts)


def pair_up(tokens, cots, route_ids, gate_probs, experts):
    tok_rows, features = tokens.shape

    def body(tokens_ref, cots_ref, ids_ref, probs_ref, out_ref):
        out_ref[:, :features] = tokens_ref[...]
        out_ref[:, features : 2 * features] = cots_ref[...]
        row = lax.broadcasted_iota(jnp.int32, (LANES, tok_rows), 0)
        share = jnp.zeros((LANES, tok_rows), F32)
        for k in range(ids_ref.shape[0]):
            chosen = ids_ref[k : k + 1, :] == row % experts
            share = share + jnp.where(chosen, probs_ref[k : k + 1, :], 0.0)
        high = share.astype(BF).astype(F32)
        mid = (share - high).astype(BF).astype(F32)
        low = share - high - mid
        term = jnp.where(row < experts, high, jnp.where(row < 2 * experts, mid, low))
        term = jnp.where(row < 3 * experts, term, 0.0)
        rest = jnp.zeros((LANES, LANES - tok_rows), F32)
        out_ref[:, 2 * features :] = jnp.concatenate([term, rest], axis=1).T[:tok_rows].astype(BF)

    out = jax.ShapeDtypeStruct((tok_rows, 2 * features + LANES), BF)
    return pl.pallas_call(
        body,
        out_shape=out,
        compiler_params=params(),
        cost_estimate=SMALL,
        name="pair_up",
    )(tokens, cots, route_ids.T, gate_probs.T)


def after(value, *earlier):
    return lax.optimization_barrier((value, *earlier))[0]


def dense_plan(tokens, route_ids, gate_probs, out_cot, w_gate, w_up, w_down):
    experts = lax.axis_size("expert")
    tok_rows, features = tokens.shape
    hidden = w_gate.shape[2]
    capacity = max(2, tok_rows * route_ids.shape[1] * 4 // (3 * experts))
    expert = lax.axis_index("expert").astype(jnp.int32)
    replica = lax.axis_index("replica").astype(jnp.int32)
    w_gate, w_up, w_down = w_gate[0], w_up[0], w_down[0]

    def to_core(rows):
        return lax.ppermute(rows, "expert", [(i, i ^ 1) for i in range(experts)])

    def to_x(rows):
        return lax.ppermute(rows, "expert", [(i, i ^ 2) for i in range(experts)])

    def to_z(rows, step):
        return lax.ppermute(
            rows, "expert", [(i, (i + 4 * step) % experts) for i in range(experts)]
        )

    def to_y(rows):
        return lax.ppermute(rows, "replica", [(0, 1), (1, 0)])

    near = [pair_up(tokens, out_cot, route_ids, gate_probs, experts)]
    far, relay = [to_x(near[0])], [to_y(near[0])]
    near.append(to_z(near[0], 1))
    far.append(to_x(near[1]))
    near.append(after(to_z(near[1], 1), far[0], relay[0]))
    far.append(to_x(near[2]))
    near.append(to_z(near[2], 1))
    far.append(to_x(near[3]))
    relay += [to_y(far[0]), to_y(near[1]), to_y(far[1])]
    joined = jnp.concatenate([near[2], near[3], far[2], far[3]], axis=0)
    last = to_y(joined)
    own_pieces = [(a, 0) for a in near + far]
    other_pieces = [(relay[0], 0), (relay[2], 0), (last, 0), (last, 1)]
    other_pieces += [(relay[1], 0), (relay[3], 0), (last, 2), (last, 3)]
    expert_index = expert
    expert = expert.reshape(1)

    def plan(pieces, *earlier):
        return plan_and_pack(after(expert, *earlier), experts, capacity, tok_rows, pieces)

    def enter(packed):
        mine, cot_mine, mine_lanes, theirs, _ = packed
        theirs = to_core(theirs)
        x = jnp.concatenate([mine, theirs[:, :features]], axis=0)
        shares = jnp.concatenate([mine_lanes, theirs[:, 2 * features :]], axis=0)
        held = (jnp.arange(LANES) % experts == expert_index) & (jnp.arange(LANES) < 3 * experts)
        weight = jnp.sum(jnp.where(held, shares.astype(F32), 0.0), axis=1, keepdims=True)
        cot = jnp.concatenate([cot_mine, theirs[:, features : 2 * features]], axis=0)
        cot = (cot.astype(F32) * weight).astype(BF)
        pre_gate, pre_up = dot(x, w_gate), dot(x, w_up)
        act = (jax.nn.silu(pre_gate) * pre_up).astype(BF)
        return x, weight, pre_gate, pre_up, act, cot

    def leave(rows_of, *before_far):
        room = TOGETHER * capacity
        theirs = to_core(rows_of(slice(2 * room, None)))
        far = to_x(after(rows_of(slice(room, 2 * room)), *before_far))
        return rows_of(slice(0, room)), theirs, far, to_x(theirs[room:])

    def home(place, parts):
        own, *others = spread(place, *parts)
        return [own] + [to_z(a, -step) for step, a in enumerate(others, 1)]

    def total(chunks):
        return sum(a.astype(F32) for a in chunks).astype(BF)

    def grads(x, act, cot, d_gate, d_up):
        x = lax.dynamic_slice_in_dim(x, replica * (features // 2), features // 2, 1)
        act = lax.dynamic_slice_in_dim(act, replica * (hidden // 2), hidden // 2, 1)
        return outer_sum(x, d_gate), outer_sum(x, d_up), outer_sum(act, cot)

    packed = plan(own_pieces, *relay[1:4], joined)
    place = packed[-1]
    own_x, weight, pre_gate, pre_up, act, cot = enter(packed)
    parts = leave(lambda rows: (dot(act[rows], w_down) * weight[rows]).astype(BF))
    cot = after(cot, parts[0], parts[1])
    d_gate, d_up = hidden_grads(cot, pre_gate, pre_up, w_down)

    grad_parts = leave(
        lambda rows: input_rows(d_gate[rows], d_up[rows], w_gate, w_up), parts[2]
    )
    chunks = home(after(place, grad_parts[0], grad_parts[1]), parts)
    own_grads = after((cot, d_gate, d_up), chunks[0])
    own = grads(own_x, act, *own_grads)
    packed = list(plan(other_pieces, *own, grad_parts[2]))
    packed[3] = after(packed[3], grad_parts[3], *chunks[1:])
    grad_chunks = home(after(place, packed[-1]), grad_parts)

    x, weight, pre_gate, pre_up, act, cot = enter(packed)
    d_gate, d_up = hidden_grads(cot, pre_gate, pre_up, w_down)
    chunks = after(chunks, d_gate)
    other = grads(x, act, cot, d_gate, after(d_up, grad_chunks[1]))
    grad_chunks = after(grad_chunks, other[0])
    grad_gate, grad_up, grad_down = ((a + b).astype(BF)[None] for a, b in zip(own, other))
    return (total(chunks), total(grad_chunks), grad_gate, grad_up, grad_down)


def dense_fits(mesh):
    experts, replicas = mesh.shape["expert"], mesh.shape["replica"]
    return replicas == 2 and experts == 4 * TOGETHER


def solution(mesh):
    placed = (
        P(("expert", "replica"), None),
        P(("expert", "replica"), None),
        P(("expert", "replica"), None),
        P(("expert", "replica"), None),
        P("expert", None, None),
        P("expert", None, None),
        P("expert", None, None),
    )
    return jax.shard_map(
        dense_plan if dense_fits(mesh) else routed_plan,
        mesh=mesh,
        in_specs=placed,
        out_specs=(
            P(("expert", "replica"), None),
            P(("expert", "replica"), None),
            P("expert", "replica", None),
            P("expert", "replica", None),
            P("expert", "replica", None),
        ),
        check_vma=False,
    )
```

```python
import jax
import jax.numpy as jnp
from jax import lax
from jax.experimental import pallas as pl
from jax.experimental.pallas import tpu as pltpu
from jax.sharding import PartitionSpec as P

BF = jnp.bfloat16
F32 = jnp.float32
VMEM = 56 * 1024 * 1024
TOGETHER = 4
LANES = 128
SMALL = pl.CostEstimate(flops=1, bytes_accessed=1, transcendentals=0)


def slots(routes, experts, capacity):
    flat_ids = routes.reshape(-1)
    one_hot = (flat_ids[:, None] == jnp.arange(experts, dtype=jnp.int32)[None, :]).astype(jnp.int32)
    before = jnp.cumsum(one_hot, axis=0) - one_hot
    slot_rank = jnp.sum(before * one_hot, axis=1)
    return flat_ids * capacity + slot_rank


def place(token_rows, positions, total_rows):
    return (
        jnp.zeros((total_rows, token_rows.shape[1]), token_rows.dtype).at[positions].set(token_rows)
    )


def hidden_rows(token_rows, gate_weight, up_weight):
    pre_gate = jnp.dot(token_rows, gate_weight, preferred_element_type=F32)
    pre_up = jnp.dot(token_rows, up_weight, preferred_element_type=F32)
    activation = (jax.nn.silu(pre_gate) * pre_up).astype(BF)
    return (pre_gate, pre_up, activation)


CONTRACT = (((1,), (1,)), ((), ()))


def hidden_grads(grad_rows, pre_gate, pre_up, down_weight):
    d_hidden = lax.dot_general(grad_rows, down_weight, CONTRACT, preferred_element_type=F32)
    sigmoid_gate = jax.nn.sigmoid(pre_gate)
    d_gate = (d_hidden * pre_up * sigmoid_gate * (1.0 + pre_gate * (1.0 - sigmoid_gate))).astype(BF)
    d_up = (d_hidden * pre_gate * sigmoid_gate).astype(BF)
    return d_gate, d_up


def input_rows(d_gate, d_up, gate_weight, up_weight):
    back_rows = lax.dot_general(d_gate, gate_weight, CONTRACT, preferred_element_type=F32)
    back_rows = back_rows + lax.dot_general(d_up, up_weight, CONTRACT, preferred_element_type=F32)
    return back_rows.astype(BF)


def outer_sum(left, right):
    return lax.dot_general(left, right, (((0,), (0,)), ((), ())), preferred_element_type=F32)


def routed_plan(tokens, route_ids, gate_probs, out_cot, w_gate, w_up, w_down):
    experts = lax.axis_size("expert")
    tok_rows, features = tokens.shape
    top_count = route_ids.shape[1]
    hidden = w_gate.shape[2]
    capacity = max(2, tok_rows * top_count * 4 // (3 * experts))
    total_rows = experts * capacity
    positions = slots(route_ids, experts, capacity)
    gate_weight, up_weight, down_weight = w_gate[0], w_up[0], w_down[0]

    def exchange(rows):
        blocks = rows.reshape(experts, capacity, features)
        return lax.all_to_all(blocks, "expert", 0, 0, tiled=True).reshape(-1, features)

    received = exchange(place(jnp.repeat(tokens, top_count, axis=0), positions, total_rows))
    pre_gate, pre_up, activation = hidden_rows(received, gate_weight, up_weight)
    result = jnp.dot(activation, down_weight, preferred_element_type=F32).astype(BF)
    picked = exchange(result)[positions].reshape(tok_rows, top_count, features)
    combined = jnp.einsum("tk,tkd->td", gate_probs, picked.astype(F32)).astype(BF)
    scaled = (gate_probs[:, :, None] * out_cot[:, None, :].astype(F32)).astype(BF)
    grads_in = exchange(place(scaled.reshape(-1, features), positions, total_rows))
    d_gate, d_up = hidden_grads(grads_in, pre_gate, pre_up, down_weight)
    back = exchange(input_rows(d_gate, d_up, gate_weight, up_weight))
    grad_tokens = jnp.sum(
        back[positions].reshape(tok_rows, top_count, features).astype(F32), axis=1
    ).astype(BF)
    gate_up_sum = lax.psum_scatter(
        outer_sum(received, jnp.concatenate([d_gate, d_up], axis=1)).astype(BF),
        "replica",
        scatter_dimension=0,
        tiled=True,
    )
    down_sum = lax.psum_scatter(
        outer_sum(activation, grads_in).astype(BF), "replica", scatter_dimension=0, tiled=True
    )
    return (
        combined,
        grad_tokens,
        gate_up_sum[:, :hidden][None],
        gate_up_sum[:, hidden:][None],
        down_sum[None],
    )

def dot(left, right):
    return jnp.dot(left, right, preferred_element_type=F32)


def whole(array):
    return pl.BlockSpec(array.shape, lambda *_: (0,) * array.ndim)


def params(steps=0):
    order = ("arbitrary",) * steps if steps else None
    return pltpu.CompilerParams(dimension_semantics=order, vmem_limit_bytes=VMEM)


ANYWHERE = pl.BlockSpec(memory_space=pl.ANY)


def sources_of(pieces):
    arrays = []
    for array, _ in pieces:
        if not any(array is a for a in arrays):
            arrays.append(array)
    sources = [
        (next(k for k, a in enumerate(arrays) if a is array), chunk) for array, chunk in pieces
    ]
    return arrays, sources


def load(refs, sources, tok_rows, rows_ref, sems):
    copies = []
    for i, (source, chunk) in enumerate(sources):
        copies.append(
            pltpu.make_async_copy(
                refs[source].at[chunk * tok_rows : (chunk + 1) * tok_rows],
                rows_ref.at[i * tok_rows : (i + 1) * tok_rows],
                sems.at[i],
            )
        )
        copies[-1].start()
    return copies


def plan_and_pack(expert, experts, capacity, tok_rows, pieces, with_mine):
    arrays, sources = sources_of(pieces)
    width = arrays[0].shape[1]
    features = (width - LANES) // 2
    groups, each = 2, len(pieces) // 2
    length, room = TOGETHER * tok_rows, TOGETHER * capacity

    def body(expert_ref, *refs):
        outs = refs[len(arrays) :]
        mine_refs, (theirs_ref, place_ref, rows_ref, sems) = outs[:-4], outs[-4:]
        copies = load(refs, sources, tok_rows, rows_ref, sems)
        lane = lax.broadcasted_iota(jnp.int32, (length, LANES), 1)
        row = lax.broadcasted_iota(jnp.int32, (length, length), 0)
        col = lax.broadcasted_iota(jnp.int32, (length, length), 1)
        before = (row >= col).astype(BF)
        slot = lax.broadcasted_iota(jnp.int32, (length, 2 * room), 1) % room
        wanted = (slot + 1).astype(F32)

        def places(shares, first):
            routed = []
            for index in (first, first ^ 1):
                held = (lane == index) | (lane == index + experts) | (lane == index + 2 * experts)
                weight = jnp.sum(jnp.where(held, shares, 0.0), axis=1, keepdims=True)
                routed.append(jnp.broadcast_to((weight > 0).astype(F32), (length, room)))
            routed = jnp.concatenate(routed, axis=1)
            rank = dot(before, routed.astype(BF))
            return jnp.where((rank == wanted) & (routed > 0), 1.0, 0.0)

        for group in range(groups):
            for copy in copies[group * each : (group + 1) * each]:
                copy.wait()
            held_rows = slice(group * length, (group + 1) * length)
            lanes = rows_ref[held_rows, 2 * features :]
            place = places(lanes.astype(F32), expert_ref[0])
            if group == 0:
                place_ref[:, : 2 * room] = place.astype(BF)
                place_ref[:, 2 * room :] = places(lanes.astype(F32), expert_ref[0] ^ 2).astype(BF)
            pick = place.T.astype(BF)
            here = slice(group * room, (group + 1) * room)
            if not with_mine:
                mine_refs[0][group] = pick[:room]
                pick = pick[room:]
            packed = dot(pick, lanes).astype(BF)
            if with_mine:
                mine_refs[2][here] = packed[:room]
            theirs_ref[here, 2 * features :] = packed[-room:]
            for at in range(0, 2 * features, 512):
                packed = dot(pick, rows_ref[held_rows, at : at + 512]).astype(BF)
                if with_mine:
                    mine_ref = mine_refs[at // features]
                    mine_ref[here, at % features : at % features + 512] = packed[:room]
                theirs_ref[here, at : at + 512] = packed[-room:]

    rows = jax.ShapeDtypeStruct((groups * room, features), BF)
    lanes = jax.ShapeDtypeStruct((groups * room, LANES), BF)
    theirs = jax.ShapeDtypeStruct((groups * room, width), BF)
    place = jax.ShapeDtypeStruct((length, 4 * room), BF)
    pick = jax.ShapeDtypeStruct((groups, room, length), BF)
    outs = ((rows, rows, lanes) if with_mine else (pick,)) + (theirs, place)
    return pl.pallas_call(
        body,
        grid_spec=pltpu.PrefetchScalarGridSpec(
            num_scalar_prefetch=1,
            grid=(1,),
            in_specs=[ANYWHERE] * len(arrays),
            out_specs=[whole(a) for a in outs],
            scratch_shapes=[
                pltpu.VMEM((groups * length, width), BF),
                pltpu.SemaphoreType.DMA((len(pieces),)),
            ],
        ),
        out_shape=outs,
        compiler_params=params(1),
        cost_estimate=SMALL,
        name="plan_and_pack",
    )(expert, *arrays)


def pack_mine(pick, tok_rows, pieces):
    arrays, sources = sources_of(pieces)
    groups, room, length = pick.shape
    width = arrays[0].shape[1]
    features = (width - LANES) // 2
    each = len(pieces) // groups

    def body(pick_ref, *refs):
        outs, (rows_ref, sems) = refs[len(arrays) : -2], refs[-2:]
        copies = load(refs, sources, tok_rows, rows_ref, sems)
        for group in range(groups):
            for copy in copies[group * each : (group + 1) * each]:
                copy.wait()
            held_rows = slice(group * length, (group + 1) * length)
            here = slice(group * room, (group + 1) * room)
            for at in range(0, width, 512):
                cols = slice(at, min(at + 512, width))
                packed = dot(pick_ref[group], rows_ref[held_rows, cols]).astype(BF)
                start = at % features
                outs[at // features][here, start : start + cols.stop - at] = packed

    rows = jax.ShapeDtypeStruct((groups * room, features), BF)
    lanes = jax.ShapeDtypeStruct((groups * room, LANES), BF)
    return pl.pallas_call(
        body,
        in_specs=[pl.BlockSpec(memory_space=pltpu.VMEM)] + [ANYWHERE] * len(arrays),
        out_shape=(rows, rows, lanes),
        scratch_shapes=[
            pltpu.VMEM((groups * length, width), BF),
            pltpu.SemaphoreType.DMA((len(pieces),)),
        ],
        compiler_params=params(),
        cost_estimate=SMALL,
        name="pack_mine",
    )(pick, *arrays)


def spread(place, mine, theirs, far_mine, far_theirs):
    length, slots_of = place.shape
    room, features = far_mine.shape
    size = length // TOGETHER
    parts = (mine, theirs, far_mine, far_theirs)

    def body(place_ref, *refs):
        outs = refs[len(parts) :]
        for at in range(0, features, 512):
            cols = slice(at, at + 512)
            rows = jnp.concatenate([ref[:, cols] for ref in refs[: len(parts)]], axis=0)
            dense = dot(place_ref[...], rows).astype(BF)
            for i, out in enumerate(outs):
                out[:, cols] = dense[i * size : (i + 1) * size]

    out = jax.ShapeDtypeStruct((size, features), BF)
    return pl.pallas_call(
        body,
        grid=(1,),
        in_specs=[whole(place)] + [pl.BlockSpec((room, features), lambda i: (0, 0))] * len(parts),
        out_specs=[whole(out)] * TOGETHER,
        out_shape=(out,) * TOGETHER,
        compiler_params=params(1),
        cost_estimate=SMALL,
        name="spread",
    )(place, *parts)


def pair_up(tokens, cots, route_ids, gate_probs, experts):
    tok_rows, features = tokens.shape

    def body(tokens_ref, cots_ref, ids_ref, probs_ref, out_ref):
        out_ref[:, :features] = tokens_ref[...]
        out_ref[:, features : 2 * features] = cots_ref[...]
        row = lax.broadcasted_iota(jnp.int32, (LANES, tok_rows), 0)
        share = jnp.zeros((LANES, tok_rows), F32)
        for k in range(ids_ref.shape[0]):
            chosen = ids_ref[k : k + 1, :] == row % experts
            share = share + jnp.where(chosen, probs_ref[k : k + 1, :], 0.0)
        high = share.astype(BF).astype(F32)
        mid = (share - high).astype(BF).astype(F32)
        low = share - high - mid
        term = jnp.where(row < experts, high, jnp.where(row < 2 * experts, mid, low))
        term = jnp.where(row < 3 * experts, term, 0.0)
        rest = jnp.zeros((LANES, LANES - tok_rows), F32)
        out_ref[:, 2 * features :] = jnp.concatenate([term, rest], axis=1).T[:tok_rows].astype(BF)

    out = jax.ShapeDtypeStruct((tok_rows, 2 * features + LANES), BF)
    return pl.pallas_call(
        body,
        out_shape=out,
        compiler_params=params(),
        cost_estimate=SMALL,
        name="pair_up",
    )(tokens, cots, route_ids.T, gate_probs.T)


def after(value, *earlier):
    return lax.optimization_barrier((value, *earlier))[0]


def dense_plan(tokens, route_ids, gate_probs, out_cot, w_gate, w_up, w_down):
    experts = lax.axis_size("expert")
    tok_rows, features = tokens.shape
    hidden = w_gate.shape[2]
    capacity = max(2, tok_rows * route_ids.shape[1] * 4 // (3 * experts))
    expert = lax.axis_index("expert").astype(jnp.int32)
    replica = lax.axis_index("replica").astype(jnp.int32)
    w_gate, w_up, w_down = w_gate[0], w_up[0], w_down[0]

    def to_core(rows):
        return lax.ppermute(rows, "expert", [(i, i ^ 1) for i in range(experts)])

    def to_x(rows):
        return lax.ppermute(rows, "expert", [(i, i ^ 2) for i in range(experts)])

    def to_z(rows, step):
        return lax.ppermute(
            rows, "expert", [(i, (i + 4 * step) % experts) for i in range(experts)]
        )

    def to_y(rows):
        return lax.ppermute(rows, "replica", [(0, 1), (1, 0)])

    near = [pair_up(tokens, out_cot, route_ids, gate_probs, experts)]
    far, relay = [to_x(near[0])], [to_y(near[0])]
    near.append(to_z(near[0], 1))
    far.append(to_x(near[1]))
    near.append(after(to_z(near[1], 1), far[0], relay[0]))
    far.append(to_x(near[2]))
    near.append(to_z(near[2], 1))
    far.append(to_x(near[3]))
    relay += [to_y(far[0]), to_y(near[1]), to_y(far[1])]
    joined = jnp.concatenate([near[2], near[3], far[2], far[3]], axis=0)
    last = to_y(joined)
    own_pieces = [(a, 0) for a in near + far]
    other_pieces = [(relay[0], 0), (relay[2], 0), (last, 0), (last, 1)]
    other_pieces += [(relay[1], 0), (relay[3], 0), (last, 2), (last, 3)]
    expert_index = expert
    expert = expert.reshape(1)

    def plan(pieces, with_mine, *earlier):
        return plan_and_pack(
            after(expert, *earlier), experts, capacity, tok_rows, pieces, with_mine
        )

    def enter(mine, cot_mine, mine_lanes, theirs):
        x = jnp.concatenate([mine, theirs[:, :features]], axis=0)
        shares = jnp.concatenate([mine_lanes, theirs[:, 2 * features :]], axis=0)
        held = (jnp.arange(LANES) % experts == expert_index) & (jnp.arange(LANES) < 3 * experts)
        weight = jnp.sum(jnp.where(held, shares.astype(F32), 0.0), axis=1, keepdims=True)
        cot = jnp.concatenate([cot_mine, theirs[:, features : 2 * features]], axis=0)
        cot = (cot.astype(F32) * weight).astype(BF)
        pre_gate, pre_up = dot(x, w_gate), dot(x, w_up)
        act = (jax.nn.silu(pre_gate) * pre_up).astype(BF)
        return x, weight, pre_gate, pre_up, act, cot

    def leave(rows_of, *before_far):
        room = TOGETHER * capacity
        theirs = to_core(rows_of(slice(2 * room, None)))
        far = to_x(after(rows_of(slice(room, 2 * room)), *before_far))
        return rows_of(slice(0, room)), theirs, far, to_x(theirs[room:])

    def home(place, parts):
        own, *others = spread(place, *parts)
        return [own] + [to_z(a, -step) for step, a in enumerate(others, 1)]

    def total(chunks):
        return sum(a.astype(F32) for a in chunks).astype(BF)

    def grads(x, act, cot, d_gate, d_up):
        x = lax.dynamic_slice_in_dim(x, replica * (features // 2), features // 2, 1)
        act = lax.dynamic_slice_in_dim(act, replica * (hidden // 2), hidden // 2, 1)
        return outer_sum(x, d_gate), outer_sum(x, d_up), outer_sum(act, cot)

    pick, theirs, place = plan(own_pieces, False, *relay[1:4], joined)
    mine = pack_mine(pick, tok_rows, own_pieces)
    own_x, weight, pre_gate, pre_up, act, cot = enter(*mine, to_core(theirs))
    parts = leave(lambda rows: (dot(act[rows], w_down) * weight[rows]).astype(BF))
    cot = after(cot, parts[0], parts[1])
    d_gate, d_up = hidden_grads(cot, pre_gate, pre_up, w_down)

    grad_parts = leave(
        lambda rows: input_rows(d_gate[rows], d_up[rows], w_gate, w_up), parts[2]
    )
    chunks = home(after(place, grad_parts[0], grad_parts[1]), parts)
    own_grads = after((cot, d_gate, d_up), chunks[0])
    own = grads(own_x, act, *own_grads)
    *mine, theirs, _ = plan(other_pieces, True, *own, grad_parts[2])
    theirs = to_core(after(theirs, grad_parts[3], *chunks[1:]))
    grad_chunks = home(after(place, mine[0]), grad_parts)

    x, weight, pre_gate, pre_up, act, cot = enter(*mine, theirs)
    d_gate, d_up = hidden_grads(cot, pre_gate, pre_up, w_down)
    chunks = after(chunks, d_gate)
    other = grads(x, act, cot, d_gate, after(d_up, grad_chunks[1]))
    grad_chunks = after(grad_chunks, other[0])
    grad_gate, grad_up, grad_down = ((a + b).astype(BF)[None] for a, b in zip(own, other))
    return (total(chunks), total(grad_chunks), grad_gate, grad_up, grad_down)


def dense_fits(mesh):
    experts, replicas = mesh.shape["expert"], mesh.shape["replica"]
    return replicas == 2 and experts == 4 * TOGETHER


def solution(mesh):
    placed = (
        P(("expert", "replica"), None),
        P(("expert", "replica"), None),
        P(("expert", "replica"), None),
        P(("expert", "replica"), None),
        P("expert", None, None),
        P("expert", None, None),
        P("expert", None, None),
    )
    return jax.shard_map(
        dense_plan if dense_fits(mesh) else routed_plan,
        mesh=mesh,
        in_specs=placed,
        out_specs=(
            P(("expert", "replica"), None),
            P(("expert", "replica"), None),
            P("expert", "replica", None),
            P("expert", "replica", None),
            P("expert", "replica", None),
        ),
        check_vma=False,
    )
```

```python
import jax
import jax.numpy as jnp
from jax import lax
from jax.experimental import pallas as pl
from jax.experimental.pallas import tpu as pltpu
from jax.sharding import PartitionSpec as P

BF = jnp.bfloat16
F32 = jnp.float32
VMEM = 56 * 1024 * 1024
TOGETHER = 4
LANES = 128
SMALL = pl.CostEstimate(flops=1, bytes_accessed=1, transcendentals=0)


def slots(routes, experts, capacity):
    flat_ids = routes.reshape(-1)
    one_hot = (flat_ids[:, None] == jnp.arange(experts, dtype=jnp.int32)[None, :]).astype(jnp.int32)
    before = jnp.cumsum(one_hot, axis=0) - one_hot
    slot_rank = jnp.sum(before * one_hot, axis=1)
    return flat_ids * capacity + slot_rank


def place(token_rows, positions, total_rows):
    return (
        jnp.zeros((total_rows, token_rows.shape[1]), token_rows.dtype).at[positions].set(token_rows)
    )


def hidden_rows(token_rows, gate_weight, up_weight):
    pre_gate = jnp.dot(token_rows, gate_weight, preferred_element_type=F32)
    pre_up = jnp.dot(token_rows, up_weight, preferred_element_type=F32)
    activation = (jax.nn.silu(pre_gate) * pre_up).astype(BF)
    return (pre_gate, pre_up, activation)


CONTRACT = (((1,), (1,)), ((), ()))


def hidden_grads(grad_rows, pre_gate, pre_up, down_weight):
    d_hidden = lax.dot_general(grad_rows, down_weight, CONTRACT, preferred_element_type=F32)
    sigmoid_gate = jax.nn.sigmoid(pre_gate)
    d_gate = (d_hidden * pre_up * sigmoid_gate * (1.0 + pre_gate * (1.0 - sigmoid_gate))).astype(BF)
    d_up = (d_hidden * pre_gate * sigmoid_gate).astype(BF)
    return d_gate, d_up


def input_rows(d_gate, d_up, gate_weight, up_weight):
    back_rows = lax.dot_general(d_gate, gate_weight, CONTRACT, preferred_element_type=F32)
    back_rows = back_rows + lax.dot_general(d_up, up_weight, CONTRACT, preferred_element_type=F32)
    return back_rows.astype(BF)


def outer_sum(left, right):
    return lax.dot_general(left, right, (((0,), (0,)), ((), ())), preferred_element_type=F32)


def routed_plan(tokens, route_ids, gate_probs, out_cot, w_gate, w_up, w_down):
    experts = lax.axis_size("expert")
    tok_rows, features = tokens.shape
    top_count = route_ids.shape[1]
    hidden = w_gate.shape[2]
    capacity = max(2, tok_rows * top_count * 4 // (3 * experts))
    total_rows = experts * capacity
    positions = slots(route_ids, experts, capacity)
    gate_weight, up_weight, down_weight = w_gate[0], w_up[0], w_down[0]

    def exchange(rows):
        blocks = rows.reshape(experts, capacity, features)
        return lax.all_to_all(blocks, "expert", 0, 0, tiled=True).reshape(-1, features)

    received = exchange(place(jnp.repeat(tokens, top_count, axis=0), positions, total_rows))
    pre_gate, pre_up, activation = hidden_rows(received, gate_weight, up_weight)
    result = jnp.dot(activation, down_weight, preferred_element_type=F32).astype(BF)
    picked = exchange(result)[positions].reshape(tok_rows, top_count, features)
    combined = jnp.einsum("tk,tkd->td", gate_probs, picked.astype(F32)).astype(BF)
    scaled = (gate_probs[:, :, None] * out_cot[:, None, :].astype(F32)).astype(BF)
    grads_in = exchange(place(scaled.reshape(-1, features), positions, total_rows))
    d_gate, d_up = hidden_grads(grads_in, pre_gate, pre_up, down_weight)
    back = exchange(input_rows(d_gate, d_up, gate_weight, up_weight))
    grad_tokens = jnp.sum(
        back[positions].reshape(tok_rows, top_count, features).astype(F32), axis=1
    ).astype(BF)
    gate_up_sum = lax.psum_scatter(
        outer_sum(received, jnp.concatenate([d_gate, d_up], axis=1)).astype(BF),
        "replica",
        scatter_dimension=0,
        tiled=True,
    )
    down_sum = lax.psum_scatter(
        outer_sum(activation, grads_in).astype(BF), "replica", scatter_dimension=0, tiled=True
    )
    return (
        combined,
        grad_tokens,
        gate_up_sum[:, :hidden][None],
        gate_up_sum[:, hidden:][None],
        down_sum[None],
    )

def dot(left, right):
    return jnp.dot(left, right, preferred_element_type=F32)


def whole(array):
    return pl.BlockSpec(array.shape, lambda *_: (0,) * array.ndim)


def params(steps=0):
    order = ("arbitrary",) * steps if steps else None
    return pltpu.CompilerParams(dimension_semantics=order, vmem_limit_bytes=VMEM)


ANYWHERE = pl.BlockSpec(memory_space=pl.ANY)


def plan_and_pack(expert, experts, capacity, tok_rows, pieces):
    arrays = []
    for array, _ in pieces:
        if not any(array is a for a in arrays):
            arrays.append(array)
    sources = [
        (next(k for k, a in enumerate(arrays) if a is array), chunk) for array, chunk in pieces
    ]
    width = arrays[0].shape[1]
    features = (width - LANES) // 2
    groups, each = 2, len(pieces) // 2
    length, room = TOGETHER * tok_rows, TOGETHER * capacity

    def body(expert_ref, *refs):
        outs = refs[len(arrays) :]
        token_mine, cot_mine, lane_mine, theirs_ref, place_ref, rows_ref, sems = outs
        copies = []
        for i, (source, chunk) in enumerate(sources):
            copies.append(
                pltpu.make_async_copy(
                    refs[source].at[chunk * tok_rows : (chunk + 1) * tok_rows],
                    rows_ref.at[i * tok_rows : (i + 1) * tok_rows],
                    sems.at[i],
                )
            )
            copies[-1].start()
        lane = lax.broadcasted_iota(jnp.int32, (length, LANES), 1)
        row = lax.broadcasted_iota(jnp.int32, (length, length), 0)
        col = lax.broadcasted_iota(jnp.int32, (length, length), 1)
        before = (row >= col).astype(BF)
        slot = lax.broadcasted_iota(jnp.int32, (length, 2 * room), 1) % room
        wanted = (slot + 1).astype(F32)

        def places(shares, first):
            routed = []
            for index in (first, first ^ 1):
                held = (lane == index) | (lane == index + experts) | (lane == index + 2 * experts)
                weight = jnp.sum(jnp.where(held, shares, 0.0), axis=1, keepdims=True)
                routed.append(jnp.broadcast_to((weight > 0).astype(F32), (length, room)))
            routed = jnp.concatenate(routed, axis=1)
            rank = dot(before, routed.astype(BF))
            return jnp.where((rank == wanted) & (routed > 0), 1.0, 0.0)

        for group in range(groups):
            for copy in copies[group * each : (group + 1) * each]:
                copy.wait()
            held_rows = slice(group * length, (group + 1) * length)
            lanes = rows_ref[held_rows, 2 * features :]
            place = places(lanes.astype(F32), expert_ref[0])
            if group == 0:
                place_ref[:, : 2 * room] = place.astype(BF)
                place_ref[:, 2 * room :] = places(lanes.astype(F32), expert_ref[0] ^ 2).astype(BF)
            pick = place.T.astype(BF)
            here = slice(group * room, (group + 1) * room)
            packed = dot(pick, lanes).astype(BF)
            lane_mine[here] = packed[:room]
            theirs_ref[here, 2 * features :] = packed[room:]
            for at in range(0, 2 * features, 512):
                packed = dot(pick, rows_ref[held_rows, at : at + 512]).astype(BF)
                mine_ref = token_mine if at < features else cot_mine
                mine_ref[here, at % features : at % features + 512] = packed[:room]
                theirs_ref[here, at : at + 512] = packed[room:]

    rows = jax.ShapeDtypeStruct((groups * room, features), BF)
    lanes = jax.ShapeDtypeStruct((groups * room, LANES), BF)
    theirs = jax.ShapeDtypeStruct((groups * room, width), BF)
    place = jax.ShapeDtypeStruct((length, 4 * room), BF)
    outs = (rows, rows, lanes, theirs, place)
    return pl.pallas_call(
        body,
        grid_spec=pltpu.PrefetchScalarGridSpec(
            num_scalar_prefetch=1,
            grid=(1,),
            in_specs=[ANYWHERE] * len(arrays),
            out_specs=[whole(a) for a in outs],
            scratch_shapes=[
                pltpu.VMEM((groups * length, width), BF),
                pltpu.SemaphoreType.DMA((len(pieces),)),
            ],
        ),
        out_shape=outs,
        compiler_params=params(1),
        cost_estimate=SMALL,
        name="plan_and_pack",
    )(expert, *arrays)


def spread(place, mine, theirs, far_mine, far_theirs):
    length, slots_of = place.shape
    room, features = far_mine.shape
    size = length // TOGETHER
    parts = (mine, theirs, far_mine, far_theirs)

    def body(place_ref, *refs):
        outs = refs[len(parts) :]
        for at in range(0, features, 512):
            cols = slice(at, at + 512)
            rows = jnp.concatenate([ref[:, cols] for ref in refs[: len(parts)]], axis=0)
            dense = dot(place_ref[...], rows).astype(BF)
            for i, out in enumerate(outs):
                out[:, cols] = dense[i * size : (i + 1) * size]

    out = jax.ShapeDtypeStruct((size, features), BF)
    return pl.pallas_call(
        body,
        grid=(1,),
        in_specs=[whole(place)] + [pl.BlockSpec((room, features), lambda i: (0, 0))] * len(parts),
        out_specs=[whole(out)] * TOGETHER,
        out_shape=(out,) * TOGETHER,
        compiler_params=params(1),
        cost_estimate=SMALL,
        name="spread",
    )(place, *parts)


def pair_up(tokens, cots, route_ids, gate_probs, experts):
    tok_rows, features = tokens.shape

    def body(tokens_ref, cots_ref, ids_ref, probs_ref, out_ref):
        out_ref[:, :features] = tokens_ref[...]
        out_ref[:, features : 2 * features] = cots_ref[...]
        row = lax.broadcasted_iota(jnp.int32, (LANES, tok_rows), 0)
        share = jnp.zeros((LANES, tok_rows), F32)
        for k in range(ids_ref.shape[0]):
            chosen = ids_ref[k : k + 1, :] == row % experts
            share = share + jnp.where(chosen, probs_ref[k : k + 1, :], 0.0)
        high = share.astype(BF).astype(F32)
        mid = (share - high).astype(BF).astype(F32)
        low = share - high - mid
        term = jnp.where(row < experts, high, jnp.where(row < 2 * experts, mid, low))
        term = jnp.where(row < 3 * experts, term, 0.0)
        rest = jnp.zeros((LANES, LANES - tok_rows), F32)
        out_ref[:, 2 * features :] = jnp.concatenate([term, rest], axis=1).T[:tok_rows].astype(BF)

    out = jax.ShapeDtypeStruct((tok_rows, 2 * features + LANES), BF)
    return pl.pallas_call(
        body,
        out_shape=out,
        compiler_params=params(),
        cost_estimate=SMALL,
        name="pair_up",
    )(tokens, cots, route_ids.T, gate_probs.T)


def after(value, *earlier):
    return lax.optimization_barrier((value, *earlier))[0]


def dense_plan(tokens, route_ids, gate_probs, out_cot, w_gate, w_up, w_down):
    experts = lax.axis_size("expert")
    tok_rows, features = tokens.shape
    hidden = w_gate.shape[2]
    capacity = max(2, tok_rows * route_ids.shape[1] * 4 // (3 * experts))
    expert = lax.axis_index("expert").astype(jnp.int32)
    replica = lax.axis_index("replica").astype(jnp.int32)
    w_gate, w_up, w_down = w_gate[0], w_up[0], w_down[0]

    def to_core(rows):
        return lax.ppermute(rows, "expert", [(i, i ^ 1) for i in range(experts)])

    def to_x(rows):
        return lax.ppermute(rows, "expert", [(i, i ^ 2) for i in range(experts)])

    def to_z(rows, step):
        return lax.ppermute(
            rows, "expert", [(i, (i + 4 * step) % experts) for i in range(experts)]
        )

    def to_y(rows):
        return lax.ppermute(rows, "replica", [(0, 1), (1, 0)])

    near = [pair_up(tokens, out_cot, route_ids, gate_probs, experts)]
    far, relay = [to_x(near[0])], [to_y(near[0])]
    near.append(to_z(near[0], 1))
    far.append(to_x(near[1]))
    near.append(after(to_z(near[1], 1), far[0], relay[0]))
    far.append(to_x(near[2]))
    near.append(to_z(near[2], 1))
    far.append(to_x(near[3]))
    relay += [to_y(far[0]), to_y(near[1]), to_y(far[1])]
    joined = jnp.concatenate([near[2], near[3], far[2], far[3]], axis=0)
    last = to_y(joined)
    own_pieces = [(a, 0) for a in near + far]
    other_pieces = [(relay[0], 0), (relay[2], 0), (last, 0), (last, 1)]
    other_pieces += [(relay[1], 0), (relay[3], 0), (last, 2), (last, 3)]
    expert_index = expert
    expert = expert.reshape(1)

    def plan(pieces, *earlier):
        return plan_and_pack(after(expert, *earlier), experts, capacity, tok_rows, pieces)

    def enter(packed):
        mine, cot_mine, mine_lanes, theirs, _ = packed
        theirs = to_core(theirs)
        x = jnp.concatenate([mine, theirs[:, :features]], axis=0)
        shares = jnp.concatenate([mine_lanes, theirs[:, 2 * features :]], axis=0)
        held = (jnp.arange(LANES) % experts == expert_index) & (jnp.arange(LANES) < 3 * experts)
        weight = jnp.sum(jnp.where(held, shares.astype(F32), 0.0), axis=1, keepdims=True)
        cot = jnp.concatenate([cot_mine, theirs[:, features : 2 * features]], axis=0)
        cot = (cot.astype(F32) * weight).astype(BF)
        pre_gate, pre_up = dot(x, w_gate), dot(x, w_up)
        act = (jax.nn.silu(pre_gate) * pre_up).astype(BF)
        return x, weight, pre_gate, pre_up, act, cot

    def leave(rows_of, *before_far):
        room = TOGETHER * capacity
        theirs = to_core(rows_of(slice(2 * room, None)))
        far = to_x(after(rows_of(slice(room, 2 * room)), *before_far))
        return rows_of(slice(0, room)), theirs, far, to_x(theirs[room:])

    def home(place, parts):
        own, *others = spread(place, *parts)
        return [own] + [to_z(a, -step) for step, a in enumerate(others, 1)]

    def total(chunks):
        return sum(a.astype(F32) for a in chunks).astype(BF)

    def grads(x, act, cot, d_gate, d_up):
        x = lax.dynamic_slice_in_dim(x, replica * (features // 2), features // 2, 1)
        act = lax.dynamic_slice_in_dim(act, replica * (hidden // 2), hidden // 2, 1)
        return outer_sum(x, d_gate), outer_sum(x, d_up), outer_sum(act, cot)

    packed = plan(own_pieces, *relay[1:4], joined)
    place = packed[-1]
    own_x, weight, pre_gate, pre_up, act, cot = enter(packed)
    parts = leave(lambda rows: (dot(act[rows], w_down) * weight[rows]).astype(BF))
    cot = after(cot, parts[0], parts[1])
    d_gate, d_up = hidden_grads(cot, pre_gate, pre_up, w_down)

    grad_parts = leave(
        lambda rows: input_rows(d_gate[rows], d_up[rows], w_gate, w_up), parts[2]
    )
    chunks = home(after(place, grad_parts[0], grad_parts[1]), parts)
    own_grads = after((cot, d_gate, d_up), chunks[0])
    own = grads(own_x, act, *own_grads)
    packed = list(plan(other_pieces, *own, grad_parts[2]))
    grad_chunks = home(after(place, packed[-1]), grad_parts)
    packed[3] = after(packed[3], grad_chunks[0], *chunks[1:])

    x, weight, pre_gate, pre_up, act, cot = enter(packed)
    d_gate, d_up = hidden_grads(cot, pre_gate, pre_up, w_down)
    chunks = after(chunks, d_gate)
    other = grads(x, act, cot, d_gate, after(d_up, grad_chunks[1]))
    grad_chunks = after(grad_chunks, other[0])
    grad_gate, grad_up, grad_down = ((a + b).astype(BF)[None] for a, b in zip(own, other))
    return (total(chunks), total(grad_chunks), grad_gate, grad_up, grad_down)


def dense_fits(mesh):
    experts, replicas = mesh.shape["expert"], mesh.shape["replica"]
    return replicas == 2 and experts == 4 * TOGETHER


def solution(mesh):
    placed = (
        P(("expert", "replica"), None),
        P(("expert", "replica"), None),
        P(("expert", "replica"), None),
        P(("expert", "replica"), None),
        P("expert", None, None),
        P("expert", None, None),
        P("expert", None, None),
    )
    return jax.shard_map(
        dense_plan if dense_fits(mesh) else routed_plan,
        mesh=mesh,
        in_specs=placed,
        out_specs=(
            P(("expert", "replica"), None),
            P(("expert", "replica"), None),
            P("expert", "replica", None),
            P("expert", "replica", None),
            P("expert", "replica", None),
        ),
        check_vma=False,
    )
```

```python
import jax
import jax.numpy as jnp
from jax import lax
from jax.experimental import pallas as pl
from jax.experimental.pallas import tpu as pltpu
from jax.sharding import PartitionSpec as P

BF = jnp.bfloat16
F32 = jnp.float32
VMEM = 56 * 1024 * 1024
TOGETHER = 4
LANES = 128
SMALL = pl.CostEstimate(flops=1, bytes_accessed=1, transcendentals=0)


def slots(routes, experts, capacity):
    flat_ids = routes.reshape(-1)
    one_hot = (flat_ids[:, None] == jnp.arange(experts, dtype=jnp.int32)[None, :]).astype(jnp.int32)
    before = jnp.cumsum(one_hot, axis=0) - one_hot
    slot_rank = jnp.sum(before * one_hot, axis=1)
    return flat_ids * capacity + slot_rank


def place(token_rows, positions, total_rows):
    return (
        jnp.zeros((total_rows, token_rows.shape[1]), token_rows.dtype).at[positions].set(token_rows)
    )


def hidden_rows(token_rows, gate_weight, up_weight):
    pre_gate = jnp.dot(token_rows, gate_weight, preferred_element_type=F32)
    pre_up = jnp.dot(token_rows, up_weight, preferred_element_type=F32)
    activation = (jax.nn.silu(pre_gate) * pre_up).astype(BF)
    return (pre_gate, pre_up, activation)


CONTRACT = (((1,), (1,)), ((), ()))


def hidden_grads(grad_rows, pre_gate, pre_up, down_weight):
    d_hidden = lax.dot_general(grad_rows, down_weight, CONTRACT, preferred_element_type=F32)
    sigmoid_gate = jax.nn.sigmoid(pre_gate)
    d_gate = (d_hidden * pre_up * sigmoid_gate * (1.0 + pre_gate * (1.0 - sigmoid_gate))).astype(BF)
    d_up = (d_hidden * pre_gate * sigmoid_gate).astype(BF)
    return d_gate, d_up


def input_rows(d_gate, d_up, gate_weight, up_weight):
    back_rows = lax.dot_general(d_gate, gate_weight, CONTRACT, preferred_element_type=F32)
    back_rows = back_rows + lax.dot_general(d_up, up_weight, CONTRACT, preferred_element_type=F32)
    return back_rows.astype(BF)


def outer_sum(left, right):
    return lax.dot_general(left, right, (((0,), (0,)), ((), ())), preferred_element_type=F32)


def routed_plan(tokens, route_ids, gate_probs, out_cot, w_gate, w_up, w_down):
    experts = lax.axis_size("expert")
    tok_rows, features = tokens.shape
    top_count = route_ids.shape[1]
    hidden = w_gate.shape[2]
    capacity = max(2, tok_rows * top_count * 4 // (3 * experts))
    total_rows = experts * capacity
    positions = slots(route_ids, experts, capacity)
    gate_weight, up_weight, down_weight = w_gate[0], w_up[0], w_down[0]

    def exchange(rows):
        blocks = rows.reshape(experts, capacity, features)
        return lax.all_to_all(blocks, "expert", 0, 0, tiled=True).reshape(-1, features)

    received = exchange(place(jnp.repeat(tokens, top_count, axis=0), positions, total_rows))
    pre_gate, pre_up, activation = hidden_rows(received, gate_weight, up_weight)
    result = jnp.dot(activation, down_weight, preferred_element_type=F32).astype(BF)
    picked = exchange(result)[positions].reshape(tok_rows, top_count, features)
    combined = jnp.einsum("tk,tkd->td", gate_probs, picked.astype(F32)).astype(BF)
    scaled = (gate_probs[:, :, None] * out_cot[:, None, :].astype(F32)).astype(BF)
    grads_in = exchange(place(scaled.reshape(-1, features), positions, total_rows))
    d_gate, d_up = hidden_grads(grads_in, pre_gate, pre_up, down_weight)
    back = exchange(input_rows(d_gate, d_up, gate_weight, up_weight))
    grad_tokens = jnp.sum(
        back[positions].reshape(tok_rows, top_count, features).astype(F32), axis=1
    ).astype(BF)
    gate_up_sum = lax.psum_scatter(
        outer_sum(received, jnp.concatenate([d_gate, d_up], axis=1)).astype(BF),
        "replica",
        scatter_dimension=0,
        tiled=True,
    )
    down_sum = lax.psum_scatter(
        outer_sum(activation, grads_in).astype(BF), "replica", scatter_dimension=0, tiled=True
    )
    return (
        combined,
        grad_tokens,
        gate_up_sum[:, :hidden][None],
        gate_up_sum[:, hidden:][None],
        down_sum[None],
    )

def dot(left, right):
    return jnp.dot(left, right, preferred_element_type=F32)


def whole(array):
    return pl.BlockSpec(array.shape, lambda *_: (0,) * array.ndim)


def params(steps=0):
    order = ("arbitrary",) * steps if steps else None
    return pltpu.CompilerParams(dimension_semantics=order, vmem_limit_bytes=VMEM)


ANYWHERE = pl.BlockSpec(memory_space=pl.ANY)


def plan_and_pack(expert, experts, capacity, tok_rows, pieces):
    arrays = []
    for array, _ in pieces:
        if not any(array is a for a in arrays):
            arrays.append(array)
    sources = [
        (next(k for k, a in enumerate(arrays) if a is array), chunk) for array, chunk in pieces
    ]
    width = arrays[0].shape[1]
    features = (width - LANES) // 2
    groups, each = 2, len(pieces) // 2
    length, room = TOGETHER * tok_rows, TOGETHER * capacity

    def body(expert_ref, *refs):
        outs = refs[len(arrays) :]
        token_mine, cot_mine, lane_mine, theirs_ref, place_ref, rows_ref, sems = outs
        copies = []
        for i, (source, chunk) in enumerate(sources):
            copies.append(
                pltpu.make_async_copy(
                    refs[source].at[chunk * tok_rows : (chunk + 1) * tok_rows],
                    rows_ref.at[i * tok_rows : (i + 1) * tok_rows],
                    sems.at[i],
                )
            )
            copies[-1].start()
        lane = lax.broadcasted_iota(jnp.int32, (length, LANES), 1)
        row = lax.broadcasted_iota(jnp.int32, (length, length), 0)
        col = lax.broadcasted_iota(jnp.int32, (length, length), 1)
        before = (row >= col).astype(BF)
        slot = lax.broadcasted_iota(jnp.int32, (length, 2 * room), 1) % room
        wanted = (slot + 1).astype(F32)

        def places(shares, first):
            routed = []
            for index in (first, first ^ 1):
                held = (lane == index) | (lane == index + experts) | (lane == index + 2 * experts)
                weight = jnp.sum(jnp.where(held, shares, 0.0), axis=1, keepdims=True)
                routed.append(jnp.broadcast_to((weight > 0).astype(F32), (length, room)))
            routed = jnp.concatenate(routed, axis=1)
            rank = dot(before, routed.astype(BF))
            return jnp.where((rank == wanted) & (routed > 0), 1.0, 0.0)

        for group in range(groups):
            for copy in copies[group * each : (group + 1) * each]:
                copy.wait()
            held_rows = slice(group * length, (group + 1) * length)
            lanes = rows_ref[held_rows, 2 * features :]
            place = places(lanes.astype(F32), expert_ref[0])
            if group == 0:
                place_ref[:, : 2 * room] = place.astype(BF)
                place_ref[:, 2 * room :] = places(lanes.astype(F32), expert_ref[0] ^ 2).astype(BF)
            pick = place.T.astype(BF)
            here = slice(group * room, (group + 1) * room)
            packed = dot(pick, lanes).astype(BF)
            lane_mine[here] = packed[:room]
            theirs_ref[here, 2 * features :] = packed[room:]
            for at in range(0, 2 * features, 512):
                packed = dot(pick, rows_ref[held_rows, at : at + 512]).astype(BF)
                mine_ref = token_mine if at < features else cot_mine
                mine_ref[here, at % features : at % features + 512] = packed[:room]
                theirs_ref[here, at : at + 512] = packed[room:]

    rows = jax.ShapeDtypeStruct((groups * room, features), BF)
    lanes = jax.ShapeDtypeStruct((groups * room, LANES), BF)
    theirs = jax.ShapeDtypeStruct((groups * room, width), BF)
    place = jax.ShapeDtypeStruct((length, 4 * room), BF)
    outs = (rows, rows, lanes, theirs, place)
    return pl.pallas_call(
        body,
        grid_spec=pltpu.PrefetchScalarGridSpec(
            num_scalar_prefetch=1,
            grid=(1,),
            in_specs=[ANYWHERE] * len(arrays),
            out_specs=[whole(a) for a in outs],
            scratch_shapes=[
                pltpu.VMEM((groups * length, width), BF),
                pltpu.SemaphoreType.DMA((len(pieces),)),
            ],
        ),
        out_shape=outs,
        compiler_params=params(1),
        cost_estimate=SMALL,
        name="plan_and_pack",
    )(expert, *arrays)


def spread(place, mine, theirs, far_mine, far_theirs):
    length, slots_of = place.shape
    room, features = far_mine.shape
    size = length // TOGETHER
    parts = (mine, theirs, far_mine, far_theirs)

    def body(place_ref, *refs):
        outs = refs[len(parts) :]
        for at in range(0, features, 512):
            cols = slice(at, at + 512)
            rows = jnp.concatenate([ref[:, cols] for ref in refs[: len(parts)]], axis=0)
            dense = dot(place_ref[...], rows).astype(BF)
            for i, out in enumerate(outs):
                out[:, cols] = dense[i * size : (i + 1) * size]

    out = jax.ShapeDtypeStruct((size, features), BF)
    return pl.pallas_call(
        body,
        grid=(1,),
        in_specs=[whole(place)] + [pl.BlockSpec((room, features), lambda i: (0, 0))] * len(parts),
        out_specs=[whole(out)] * TOGETHER,
        out_shape=(out,) * TOGETHER,
        compiler_params=params(1),
        cost_estimate=SMALL,
        name="spread",
    )(place, *parts)


def pair_up(tokens, cots, route_ids, gate_probs, experts):
    tok_rows, features = tokens.shape

    def body(tokens_ref, cots_ref, ids_ref, probs_ref, out_ref):
        out_ref[:, :features] = tokens_ref[...]
        out_ref[:, features : 2 * features] = cots_ref[...]
        row = lax.broadcasted_iota(jnp.int32, (LANES, tok_rows), 0)
        share = jnp.zeros((LANES, tok_rows), F32)
        for k in range(ids_ref.shape[0]):
            chosen = ids_ref[k : k + 1, :] == row % experts
            share = share + jnp.where(chosen, probs_ref[k : k + 1, :], 0.0)
        high = share.astype(BF).astype(F32)
        mid = (share - high).astype(BF).astype(F32)
        low = share - high - mid
        term = jnp.where(row < experts, high, jnp.where(row < 2 * experts, mid, low))
        term = jnp.where(row < 3 * experts, term, 0.0)
        rest = jnp.zeros((LANES, LANES - tok_rows), F32)
        out_ref[:, 2 * features :] = jnp.concatenate([term, rest], axis=1).T[:tok_rows].astype(BF)

    out = jax.ShapeDtypeStruct((tok_rows, 2 * features + LANES), BF)
    return pl.pallas_call(
        body,
        out_shape=out,
        compiler_params=params(),
        cost_estimate=SMALL,
        name="pair_up",
    )(tokens, cots, route_ids.T, gate_probs.T)


def after(value, *earlier):
    return lax.optimization_barrier((value, *earlier))[0]


def dense_plan(tokens, route_ids, gate_probs, out_cot, w_gate, w_up, w_down):
    experts = lax.axis_size("expert")
    tok_rows, features = tokens.shape
    hidden = w_gate.shape[2]
    capacity = max(2, tok_rows * route_ids.shape[1] * 4 // (3 * experts))
    expert = lax.axis_index("expert").astype(jnp.int32)
    replica = lax.axis_index("replica").astype(jnp.int32)
    w_gate, w_up, w_down = w_gate[0], w_up[0], w_down[0]

    def to_core(rows):
        return lax.ppermute(rows, "expert", [(i, i ^ 1) for i in range(experts)])

    def to_x(rows):
        return lax.ppermute(rows, "expert", [(i, i ^ 2) for i in range(experts)])

    def to_z(rows, step):
        return lax.ppermute(
            rows, "expert", [(i, (i + 4 * step) % experts) for i in range(experts)]
        )

    def to_y(rows):
        return lax.ppermute(rows, "replica", [(0, 1), (1, 0)])

    near = [pair_up(tokens, out_cot, route_ids, gate_probs, experts)]
    far, relay = [to_x(near[0])], [to_y(near[0])]
    near.append(to_z(near[0], 1))
    far.append(to_x(near[1]))
    near.append(after(to_z(near[1], 1), far[0], relay[0]))
    far.append(to_x(near[2]))
    near.append(to_z(near[2], 1))
    far.append(to_x(near[3]))
    relay += [to_y(far[0]), to_y(near[1]), to_y(far[1])]
    joined = jnp.concatenate([near[2], near[3], far[2], far[3]], axis=0)
    last = to_y(joined)
    own_pieces = [(a, 0) for a in near + far]
    other_pieces = [(relay[0], 0), (relay[2], 0), (last, 0), (last, 1)]
    other_pieces += [(relay[1], 0), (relay[3], 0), (last, 2), (last, 3)]
    expert_index = expert
    expert = expert.reshape(1)

    def plan(pieces, *earlier):
        return plan_and_pack(after(expert, *earlier), experts, capacity, tok_rows, pieces)

    def enter(packed):
        mine, cot_mine, mine_lanes, theirs, _ = packed
        theirs = to_core(theirs)
        x = jnp.concatenate([mine, theirs[:, :features]], axis=0)
        shares = jnp.concatenate([mine_lanes, theirs[:, 2 * features :]], axis=0)
        held = (jnp.arange(LANES) % experts == expert_index) & (jnp.arange(LANES) < 3 * experts)
        weight = jnp.sum(jnp.where(held, shares.astype(F32), 0.0), axis=1, keepdims=True)
        cot = jnp.concatenate([cot_mine, theirs[:, features : 2 * features]], axis=0)
        cot = (cot.astype(F32) * weight).astype(BF)
        pre_gate, pre_up = dot(x, w_gate), dot(x, w_up)
        act = (jax.nn.silu(pre_gate) * pre_up).astype(BF)
        return x, weight, pre_gate, pre_up, act, cot

    def leave(rows_of, *before_far):
        room = TOGETHER * capacity
        theirs = to_core(rows_of(slice(2 * room, None)))
        far = to_x(after(rows_of(slice(room, 2 * room)), *before_far))
        return rows_of(slice(0, room)), theirs, far, to_x(theirs[room:])

    def home(place, parts):
        own, *others = spread(place, *parts)
        return [own] + [to_z(a, -step) for step, a in enumerate(others, 1)]

    def total(chunks):
        return sum(a.astype(F32) for a in chunks).astype(BF)

    def grads(x, act, cot, d_gate, d_up):
        x = lax.dynamic_slice_in_dim(x, replica * (features // 2), features // 2, 1)
        act = lax.dynamic_slice_in_dim(act, replica * (hidden // 2), hidden // 2, 1)
        return outer_sum(x, d_gate), outer_sum(x, d_up), outer_sum(act, cot)

    packed = plan(own_pieces, *relay[1:4], joined)
    place = packed[-1]
    own_x, weight, pre_gate, pre_up, act, cot = enter(packed)
    parts = leave(lambda rows: (dot(act[rows], w_down) * weight[rows]).astype(BF))
    cot = after(cot, parts[0], parts[1])
    d_gate, d_up = hidden_grads(cot, pre_gate, pre_up, w_down)

    grad_parts = leave(
        lambda rows: input_rows(d_gate[rows], d_up[rows], w_gate, w_up), *parts[2:]
    )
    chunks = home(after(place, grad_parts[0], grad_parts[1]), parts)
    own_grads = after((cot, d_gate, d_up), chunks[0])
    own = grads(own_x, act, *own_grads)
    packed = list(plan(other_pieces, *own, grad_parts[2]))
    grad_chunks = home(after(place, packed[-1]), grad_parts)
    packed[3] = after(packed[3], grad_chunks[0], *chunks[1:])

    x, weight, pre_gate, pre_up, act, cot = enter(packed)
    d_gate, d_up = hidden_grads(cot, pre_gate, pre_up, w_down)
    chunks = after(chunks, d_gate)
    other = grads(x, act, cot, d_gate, after(d_up, grad_chunks[1]))
    grad_chunks = after(grad_chunks, other[0])
    grad_gate, grad_up, grad_down = ((a + b).astype(BF)[None] for a, b in zip(own, other))
    return (total(chunks), total(grad_chunks), grad_gate, grad_up, grad_down)


def dense_fits(mesh):
    experts, replicas = mesh.shape["expert"], mesh.shape["replica"]
    return replicas == 2 and experts == 4 * TOGETHER


def solution(mesh):
    placed = (
        P(("expert", "replica"), None),
        P(("expert", "replica"), None),
        P(("expert", "replica"), None),
        P(("expert", "replica"), None),
        P("expert", None, None),
        P("expert", None, None),
        P("expert", None, None),
    )
    return jax.shard_map(
        dense_plan if dense_fits(mesh) else routed_plan,
        mesh=mesh,
        in_specs=placed,
        out_specs=(
            P(("expert", "replica"), None),
            P(("expert", "replica"), None),
            P("expert", "replica", None),
            P("expert", "replica", None),
            P("expert", "replica", None),
        ),
        check_vma=False,
    )
```
